32 devices in a mesh: grp: 4 (over z), seq: 8 (over y, x, core).
Axes of the slice: x: 2, y: 2, z: 4, core: 2. Of those that a mesh axis runs over, the one named last changes fastest.
Arguments:
- long_x: bfloat16 [4, 1024, 768], P('grp', 'seq'), may hold values from -6 to 6
- short_x: bfloat16 [128, 256, 768], P(('grp', 'seq')), may hold values from -6 to 6
- long_dy: bfloat16 [4, 1024, 768], P('grp', 'seq'), may hold values from -6 to 6
- short_dy: bfloat16 [128, 256, 768], P(('grp', 'seq')), may hold values from -6 to 6
- short_live: int32 [32], P(('grp', 'seq')), may hold values from 0 to 4, as said below
- query_weight: bfloat16 [768, 768], replicated, may hold values from -0.21875 to 0.21875
- key_weight: bfloat16 [768, 768], replicated, may hold values from -0.21875 to 0.21875
- value_weight: bfloat16 [768, 768], replicated, may hold values from -0.21875 to 0.21875
- out_weight: bfloat16 [768, 768], replicated, may hold values from -0.4375 to 0.4375
- up_weight: bfloat16 [768, 3072], replicated, may hold values from -0.21875 to 0.21875
- down_weight: bfloat16 [3072, 768], replicated, may hold values from -0.109375 to 0.109375
- length_proj: bfloat16 [256, 1024], replicated, may hold values from -0.25 to 0.25
- gain_one: float32 [768], replicated, may hold values from 0.5 to 1.5
- shift_one: float32 [768], replicated, may hold values from -1.5 to 1.5
- gain_two: float32 [768], replicated, may hold values from 0.5 to 1.5
- shift_two: float32 [768], replicated, may hold values from -1.5 to 1.5
Outputs:
- long_out: bfloat16 [4, 1024, 768], P('grp', 'seq')
- short_out: bfloat16 [128, 256, 768], P(('grp', 'seq'))
- long_grad: bfloat16 [4, 1024, 768], P('grp', 'seq')
- short_grad: bfloat16 [128, 256, 768], P(('grp', 'seq'))
- query_grad: float32 [768, 768], P(('grp', 'seq'))
- key_grad: float32 [768, 768], P(('grp', 'seq'))
- value_grad: float32 [768, 768], P(('grp', 'seq'))
- out_grad: float32 [768, 768], P(('grp', 'seq'))
- up_grad: float32 [768, 3072], P(('grp', 'seq'))
- down_grad: float32 [3072, 768], P(('grp', 'seq'))
- proj_grad: float32 [256, 1024], P('grp', 'seq')
- gain_one_grad: float32 [768], P(('grp', 'seq'))
- shift_one_grad: float32 [768], P(('grp', 'seq'))
- gain_two_grad: float32 [768], P(('grp', 'seq'))
- shift_two_grad: float32 [768], P(('grp', 'seq'))
The draws below stay inside these ranges and needn't reach their ends.
Inputs may be any that keep to these rules, and one draw needn't show every extreme that they name: `short_live`: some device has all 4 short items live and some device has none.
All inputs are finite; a program needn't handle non-finite values.
Results may differ from the reference program's by a relative error of at most 0.033.
Values may be sent and summed in bfloat16 or wider, within the bound.
A program may use at most 256 MiB of HBM per device.

```python
import jax
import jax.numpy as jnp
from jax import lax

HD = 64
FF = 3072
KP = 256
SHORT = 256
SLOTS = 4
D = 768
LONG = 1024
ITEMS = 4
SHORTS = 128
N_SEQ = 8
DEVICES = 32


def draw_short_live(key, part):
    key = jax.random.fold_in(key, 11)
    count_key, pick_key = jax.random.split(key)
    counts = jax.random.randint(count_key, (DEVICES,), 0, SLOTS + 1)
    chosen = jax.random.permutation(pick_key, DEVICES)
    counts = counts.at[chosen[0]].set(SLOTS)
    counts = counts.at[chosen[1]].set(0)
    return counts.astype(jnp.int32)


def raised(array, stream_key, source, target, blocks, factor):
    def block_of(axis_at):
        return (jnp.arange(array.shape[axis_at]) // (array.shape[axis_at] // blocks)).reshape((-1,) + (1,) * (array.ndim - 1 - axis_at))

    near = jax.random.permutation(stream_key, blocks)[block_of(target)]
    second = (block_of(target) + blocks // 2) % blocks
    return jnp.where((block_of(source) == near) | (block_of(source) == second), factor * array, array)


def block_levels(rng, shape, shards, least, high):
    def one(dim, parts):
        draws = jax.random.uniform(jax.random.fold_in(jax.random.fold_in(rng, 6), dim), (parts,), jnp.float32, least / len(shards), high / len(shards))
        return jnp.repeat(jnp.exp(draws), shape[dim] // parts).reshape((-1,) + (1,) * (len(shape) - dim - 1))

    level = one(*shards[0])
    for cut in shards[1:]:
        level = level * one(*cut)
    return level


def normal_values(stream_key, dims, scale, most, shards=(), held_as=jnp.bfloat16):
    factor_of = block_levels(stream_key, dims, shards, -0.22, 0.18) if shards else 1.0
    drawn = jax.random.normal(stream_key, dims, jnp.float32) * scale * factor_of
    return jnp.minimum(jnp.maximum(drawn, -most), most).astype(held_as)


def gaussian_with(key, extent, width, reach, cuts, heavy, held_as=jnp.bfloat16):
    drawn = width * jax.random.normal(key, extent, jnp.float32)
    if cuts:
        drawn = drawn * block_levels(key, extent, cuts, -0.22, 0.18)
    return jnp.clip(raised(drawn, jax.random.fold_in(key, 3), *heavy), -reach, reach).astype(held_as)


def setup_inputs(seed: int = 0) -> dict:
    key_list = jax.random.split(jax.random.key(seed), 17)
    return {
        "long_x": normal_values(key_list[0], (ITEMS, LONG, D), 1.0, 6.0, ((0, 4), (1, 8))),
        "short_x": normal_values(key_list[1], (SHORTS, SHORT, D), 1.0, 6.0, ((0, 32),)),
        "long_dy": gaussian_with(key_list[2], (ITEMS, LONG, D), 1.0, 6.0, ((0, 4), (1, 8)), (1, 2, 8, 2.0)),
        "short_dy": gaussian_with(key_list[3], (SHORTS, SHORT, D), 1.0, 6.0, ((0, 32),), (0, 2, 32, 2.75)),
        "short_live": draw_short_live(jax.random.fold_in(key_list[16], 71), 0),
        "query_weight": normal_values(key_list[5], (D, D), D ** -0.5, 0.21875),
        "key_weight": normal_values(key_list[6], (D, D), D ** -0.5, 0.21875),
        "value_weight": normal_values(key_list[7], (D, D), D ** -0.5, 0.21875),
        "out_weight": normal_values(key_list[8], (D, D), (D // 4) ** -0.5, 0.4375),
        "up_weight": normal_values(key_list[9], (D, FF), D ** -0.5, 0.21875),
        "down_weight": normal_values(key_list[10], (FF, D), FF ** -0.5, 0.109375),
        "length_proj": normal_values(key_list[11], (KP, LONG), (2 * SHORT) ** -0.5, 0.25),
        "gain_one": jnp.clip(1.0 + 0.1 * jax.random.normal(key_list[12], (D,), jnp.float32), 0.5, 1.5),
        "shift_one": normal_values(key_list[13], (D,), 0.3, 1.5, (), jnp.float32),
        "gain_two": jnp.clip(1.0 + 0.1 * jax.random.normal(key_list[14], (D,), jnp.float32), 0.5, 1.5),
        "shift_two": normal_values(key_list[15], (D,), 0.3, 1.5, (), jnp.float32),
    }


@jax.custom_vjp
def low(v):
    return lax.optimization_barrier(v.astype(jnp.bfloat16)).astype(jnp.float32)

@jax.custom_vjp
def low_back(v):
    return v

def low_keep(v):
    return (low(v), None)

def low_pass(kept, grad):
    return (grad,)

def back_keep(v):
    return (v, None)

def back_low(kept, grad):
    return (low(grad),)
low.defvjp(low_keep, low_pass)
low_back.defvjp(back_keep, back_low)
highest = lax.Precision.HIGHEST
norm_eps = 1e-05

def rounded(value):
    return low(low_back(value))

def norm_rows(resid, gain_vec, shift_vec):
    row_mean = lax.optimization_barrier(jnp.mean(resid, axis=-1, keepdims=True))
    centred = resid - row_mean
    variance = lax.optimization_barrier(jnp.mean(centred * centred, axis=-1, keepdims=True))
    return centred * lax.rsqrt(variance + norm_eps) * gain_vec + shift_vec

def attend_block(sequences, proj_cols, params, shard_count):
    query_w, key_w, value_w, out_w, up_w, down_w, gain_first, shift_first, gain_second, shift_second = params
    seq_count, length, model_width = sequences.shape
    head_count = model_width // HD
    shard_len = length // shard_count
    queries = rounded(0.125 * jnp.einsum('nld,de->nle', sequences, query_w, precision=highest))
    key_vecs = rounded(jnp.einsum('nld,de->nle', sequences, key_w, precision=highest))
    value_vecs = rounded(jnp.einsum('nld,de->nle', sequences, value_w, precision=highest))
    proj_shards = proj_cols.reshape(KP, shard_count, shard_len)
    key_shards = key_vecs.reshape(seq_count, shard_count, shard_len, model_width)
    value_shards = value_vecs.reshape(seq_count, shard_count, shard_len, model_width)
    key_part = low(jnp.einsum('ksl,nsld->nskd', proj_shards, key_shards, precision=highest))
    value_part = low(jnp.einsum('ksl,nsld->nskd', proj_shards, value_shards, precision=highest))
    key_sum = rounded(lax.optimization_barrier(jnp.sum(key_part, axis=1)))
    value_sum = rounded(lax.optimization_barrier(jnp.sum(value_part, axis=1)))
    copy_shape = (seq_count, shard_count, KP, model_width)
    key_copies = low_back(jnp.broadcast_to(key_sum[:, None], copy_shape))
    value_copies = low_back(jnp.broadcast_to(value_sum[:, None], copy_shape))
    query_heads = queries.reshape(seq_count, shard_count, shard_len, head_count, HD)
    key_heads = key_copies.reshape(seq_count, shard_count, KP, head_count, HD)
    value_heads = value_copies.reshape(seq_count, shard_count, KP, head_count, HD)
    scores = low_back(jnp.einsum('nslhe,nskhe->nshlk', query_heads, key_heads, precision=highest))
    attn_probs = low(jax.nn.softmax(scores, axis=-1))
    mixed_heads = rounded(jnp.einsum('nshlk,nskhe->nslhe', attn_probs, value_heads, precision=highest).reshape(seq_count, length, model_width))
    attn_out = low_back(jnp.einsum('nld,de->nle', mixed_heads, out_w, precision=highest))
    hidden = norm_rows(sequences + attn_out, gain_first, shift_first)
    upward = low_back(jnp.einsum('nld,df->nlf', low(hidden), up_w, precision=highest))
    activated = low(jax.nn.gelu(upward, approximate=True))
    branch = low_back(jnp.einsum('nlf,fd->nld', activated, down_w, precision=highest))
    return norm_rows(hidden + branch, gain_second, shift_second)

def reference(long_x, short_x, long_dy, short_dy, short_live, query_weight, key_weight, value_weight, out_weight, up_weight, down_weight, length_proj, gain_one, shift_one, gain_two, shift_two):
    live_mask = (jnp.arange(SLOTS)[None, :] < short_live[:, None]).astype(jnp.float32)
    live_groups = live_mask.reshape(ITEMS, N_SEQ * SLOTS, 1, 1)
    model_width = long_x.shape[-1]
    short_groups = short_x.astype(jnp.float32).reshape(ITEMS, N_SEQ * SLOTS, SHORT, model_width)
    params = tuple((weight.astype(jnp.float32) for weight in (query_weight, key_weight, value_weight, out_weight, up_weight, down_weight, length_proj, gain_one, shift_one, gain_two, shift_two)))

    def forward(weights, long_in, short_in):
        proj_all = weights[6]
        others = weights[:6] + weights[7:]

        def long_item(sequence):
            return attend_block(sequence[None], proj_all, others, N_SEQ)[0]

        def short_group(pieces):
            return attend_block(pieces[0], proj_all[:, :SHORT], others, 1) * pieces[1]
        long_result = lax.map(jax.checkpoint(long_item), long_in)
        short_result = lax.map(jax.checkpoint(short_group), (short_in, live_groups))
        return (long_result, short_result)
    outputs, pullback = jax.vjp(forward, params, long_x.astype(jnp.float32), short_groups)
    grads, long_back, short_back = pullback((long_dy.astype(jnp.float32), short_dy.astype(jnp.float32).reshape(short_groups.shape)))
    return (outputs[0].astype(jnp.bfloat16), outputs[1].reshape(short_x.shape).astype(jnp.bfloat16), long_back.astype(jnp.bfloat16), short_back.reshape(short_x.shape).astype(jnp.bfloat16), grads[0], grads[1], grads[2], grads[3], grads[4], grads[5], grads[6], grads[7], grads[8], grads[9], grads[10])
```

```python
import functools

import jax
import jax.numpy as jnp
from jax import lax
from jax.experimental import pallas as pl
from jax.experimental.pallas import tpu as pltpu
from jax.sharding import PartitionSpec as P

HD = 64
KP = 256


norm_eps = 1e-05


def shortened(shard):
    return jax.tree.map(lambda a: a.astype(jnp.bfloat16) if a.dtype == jnp.float32 else a, shard)


def norm_rows(resid, gain_vec, shift_vec):
    row_mean = jnp.mean(resid, axis=-1, keepdims=True)
    centred = resid - row_mean
    variance = jnp.mean(centred * centred, axis=-1, keepdims=True)
    return centred * lax.rsqrt(variance + norm_eps) * gain_vec + shift_vec


def smooth_gate(upward):
    return jax.nn.gelu(upward, approximate=True)


def same_sums(partials):
    return partials


def layer_pass(sequences, cotangent, live_rows, proj_cols, fold_summaries, fold_grads, params):
    (
        query_w,
        key_w,
        value_w,
        out_w,
        up_w,
        down_w,
        gain_first,
        shift_first,
        gain_second,
        shift_second,
    ) = params
    seq_count, length, model_width = sequences.shape
    head_count = model_width // HD
    wide = jnp.float32
    narrow = jnp.bfloat16
    queries = (
        0.125 * jnp.einsum("nld,de->nle", sequences, query_w, preferred_element_type=wide)
    ).astype(narrow)
    key_vecs = jnp.einsum("nld,de->nle", sequences, key_w, preferred_element_type=wide).astype(
        narrow
    )
    value_vecs = jnp.einsum("nld,de->nle", sequences, value_w, preferred_element_type=wide).astype(
        narrow
    )
    key_part = jnp.einsum("kl,nld->nkd", proj_cols, key_vecs, preferred_element_type=wide)
    value_part = jnp.einsum("kl,nld->nkd", proj_cols, value_vecs, preferred_element_type=wide)
    key_sum, value_sum = fold_summaries((key_part, value_part))
    key_heads = key_sum.astype(narrow).reshape(seq_count, KP, head_count, HD)
    value_heads = value_sum.astype(narrow).reshape(seq_count, KP, head_count, HD)
    query_heads = queries.reshape(seq_count, length, head_count, HD)
    scores = jnp.einsum("nlhe,nkhe->nhlk", query_heads, key_heads, preferred_element_type=wide)
    attn_probs = jax.nn.softmax(scores, axis=-1)
    probs_low = attn_probs.astype(narrow)
    mixed_heads = (
        jnp.einsum("nhlk,nkhe->nlhe", probs_low, value_heads, preferred_element_type=wide)
        .reshape(seq_count, length, model_width)
        .astype(narrow)
    )
    attn_out = jnp.einsum("nld,de->nle", mixed_heads, out_w, preferred_element_type=wide)
    hidden, first_back = jax.vjp(
        norm_rows, sequences.astype(wide) + attn_out, gain_first, shift_first
    )
    hidden_low = hidden.astype(narrow)
    upward = jnp.einsum("nld,df->nlf", hidden_low, up_w, preferred_element_type=wide)
    activated, gate_back = jax.vjp(smooth_gate, upward)
    activated_low = activated.astype(narrow)
    branch = jnp.einsum("nlf,fd->nld", activated_low, down_w, preferred_element_type=wide)
    normed, second_back = jax.vjp(norm_rows, hidden + branch, gain_second, shift_second)
    result = normed * live_rows[:, None, None]
    grad_top = cotangent.astype(wide) * live_rows[:, None, None]
    grad_resid_two, grad_gain_two, grad_shift_two = second_back(grad_top)
    grad_branch = grad_resid_two.astype(narrow)
    grad_down = jnp.einsum("nlf,nld->fd", activated_low, grad_branch, preferred_element_type=wide)
    grad_activated = jnp.einsum("nld,fd->nlf", grad_branch, down_w, preferred_element_type=wide)
    (grad_upward,) = gate_back(grad_activated)
    grad_upward_low = grad_upward.astype(narrow)
    grad_up = jnp.einsum("nld,nlf->df", hidden_low, grad_upward_low, preferred_element_type=wide)
    grad_hidden = grad_resid_two + jnp.einsum(
        "nlf,df->nld", grad_upward_low, up_w, preferred_element_type=wide
    )
    grad_resid_one, grad_gain_one, grad_shift_one = first_back(grad_hidden)
    grad_attn = grad_resid_one.astype(narrow)
    grad_out = jnp.einsum("nld,nle->de", mixed_heads, grad_attn, preferred_element_type=wide)
    grad_mixed = (
        jnp.einsum("nle,de->nld", grad_attn, out_w, preferred_element_type=wide)
        .astype(narrow)
        .reshape(seq_count, length, head_count, HD)
    )
    grad_probs = jnp.einsum("nlhe,nkhe->nhlk", grad_mixed, value_heads, preferred_element_type=wide)
    value_grad_part = jnp.einsum(
        "nhlk,nlhe->nkhe", probs_low, grad_mixed, preferred_element_type=wide
    ).reshape(seq_count, KP, model_width)
    grad_scores = attn_probs * (
        grad_probs - jnp.sum(grad_probs * attn_probs, axis=-1, keepdims=True)
    )
    scores_low = grad_scores.astype(narrow)
    grad_queries = (
        jnp.einsum("nhlk,nkhe->nlhe", scores_low, key_heads, preferred_element_type=wide).astype(
            narrow
        )
        * 0.125
    ).reshape(seq_count, length, model_width)
    key_grad_part = jnp.einsum(
        "nhlk,nlhe->nkhe", scores_low, query_heads, preferred_element_type=wide
    ).reshape(seq_count, KP, model_width)
    key_grad_sum, value_grad_sum = fold_grads((key_grad_part, value_grad_part))
    key_grad_low = key_grad_sum.astype(narrow)
    value_grad_low = value_grad_sum.astype(narrow)
    grad_keys = jnp.einsum(
        "kl,nkd->nld", proj_cols, key_grad_low, preferred_element_type=wide
    ).astype(narrow)
    grad_values = jnp.einsum(
        "kl,nkd->nld", proj_cols, value_grad_low, preferred_element_type=wide
    ).astype(narrow)
    grad_cols = jnp.einsum(
        "nkd,nld->kl", key_grad_low, key_vecs, preferred_element_type=wide
    ) + jnp.einsum("nkd,nld->kl", value_grad_low, value_vecs, preferred_element_type=wide)
    grad_query = jnp.einsum("nld,nle->de", sequences, grad_queries, preferred_element_type=wide)
    grad_key = jnp.einsum("nld,nle->de", sequences, grad_keys, preferred_element_type=wide)
    grad_value = jnp.einsum("nld,nle->de", sequences, grad_values, preferred_element_type=wide)
    grad_sequences = grad_resid_one + jnp.einsum(
        "nle,de->nld", grad_queries, query_w, preferred_element_type=wide
    )
    grad_sequences = grad_sequences + jnp.einsum(
        "nle,de->nld", grad_keys, key_w, preferred_element_type=wide
    )
    grad_sequences = grad_sequences + jnp.einsum(
        "nle,de->nld", grad_values, value_w, preferred_element_type=wide
    )
    weight_grads = (
        grad_query,
        grad_key,
        grad_value,
        grad_out,
        grad_up,
        grad_down,
        grad_gain_one,
        grad_shift_one,
        grad_gain_two,
        grad_shift_two,
    )
    return (result, grad_sequences, weight_grads, grad_cols)


def shards(
    long_x,
    short_x,
    long_dy,
    short_dy,
    short_live,
    query_weight,
    key_weight,
    value_weight,
    out_weight,
    up_weight,
    down_weight,
    length_proj,
    gain_one,
    shift_one,
    gain_two,
    shift_two,
):
    params = (
        query_weight,
        key_weight,
        value_weight,
        out_weight,
        up_weight,
        down_weight,
        gain_one,
        shift_one,
        gain_two,
        shift_two,
    )
    shard_len = long_x.shape[1]
    slot_count = short_x.shape[0]
    short_len = short_x.shape[1]
    shard_start = lax.axis_index("seq") * shard_len
    long_cols = lax.dynamic_slice_in_dim(length_proj, shard_start, shard_len, 1)

    def sum_summaries(partials):
        return jax.tree.map(
            lambda part: part.astype(jnp.float32), lax.psum(shortened(partials), "seq")
        )

    def sum_summary_grads(partials):
        return jax.tree.map(
            lambda part: part.astype(jnp.float32), lax.psum(shortened(partials), "seq")
        )

    long_live = jnp.ones((long_x.shape[0],), jnp.float32)
    long_result, long_back, long_weights, long_proj = layer_pass(
        long_x, long_dy, long_live, long_cols, sum_summaries, sum_summary_grads, params
    )
    short_mask = (jnp.arange(slot_count) < short_live[0]).astype(jnp.float32)
    short_result, short_back, short_weights, short_proj = layer_pass(
        short_x, short_dy, short_mask, length_proj[:, :short_len], same_sums, same_sums, params
    )
    summed = jax.tree.map(jnp.add, long_weights, short_weights)
    (
        grad_query,
        grad_key,
        grad_value,
        grad_out,
        grad_up,
        grad_down,
        grad_gain_one,
        grad_shift_one,
        grad_gain_two,
        grad_shift_two,
    ) = summed
    proj_total = jnp.zeros(length_proj.shape, jnp.float32)
    proj_total = lax.dynamic_update_slice_in_dim(proj_total, long_proj, shard_start, 1)
    proj_total = proj_total.at[:, :short_len].add(short_proj)
    proj_rows = lax.psum_scatter(
        proj_total.astype(jnp.bfloat16), "grp", scatter_dimension=0, tiled=True
    )
    proj_part = lax.psum_scatter(proj_rows, "seq", scatter_dimension=1, tiled=True).astype(
        jnp.float32
    )
    reduced = (
        lax.psum_scatter(grad_query, ("grp", "seq"), scatter_dimension=0, tiled=True),
        lax.psum_scatter(grad_key, ("grp", "seq"), scatter_dimension=0, tiled=True),
        lax.psum_scatter(grad_value, ("grp", "seq"), scatter_dimension=0, tiled=True),
        lax.psum_scatter(grad_out, ("grp", "seq"), scatter_dimension=0, tiled=True),
        lax.psum_scatter(grad_up, ("grp", "seq"), scatter_dimension=0, tiled=True),
        lax.psum_scatter(grad_down, ("grp", "seq"), scatter_dimension=0, tiled=True),
        lax.psum_scatter(grad_gain_one, ("grp", "seq"), scatter_dimension=0, tiled=True),
        lax.psum_scatter(grad_shift_one, ("grp", "seq"), scatter_dimension=0, tiled=True),
        lax.psum_scatter(grad_gain_two, ("grp", "seq"), scatter_dimension=0, tiled=True),
        lax.psum_scatter(grad_shift_two, ("grp", "seq"), scatter_dimension=0, tiled=True),
    )
    reduced = tuple(reduced)
    return (
        (
            long_result.astype(jnp.bfloat16),
            short_result.astype(jnp.bfloat16),
            long_back.astype(jnp.bfloat16),
            short_back.astype(jnp.bfloat16),
        )
        + reduced[:6]
        + (proj_part,)
        + reduced[6:]
    )


MESH_ID = pl.DeviceIdType.MESH
BF = jnp.bfloat16
F32 = jnp.float32
VMEM_BYTES = 63 * 2**20
GELU_A = 0.7978845608028654
GELU_B = 0.044715 * GELU_A
SEQ = 8


def mm(a, b, ca=1, cb=0):
    return lax.dot_general(a, b, (((ca,), (cb,)), ((), ())), preferred_element_type=F32)


def span(start, size):
    return pl.ds(pl.multiple_of(start, size), size)


def here():
    return lax.axis_index("grp"), lax.axis_index("seq")


def greet(peers):
    barrier = pltpu.get_barrier_semaphore()
    for peer in peers:
        pl.semaphore_signal(barrier, inc=1, device_id=peer, device_id_type=MESH_ID)
    pl.semaphore_wait(barrier, len(peers))


def seq_peers():
    g, s = here()
    return [(g, lax.rem(s + k, SEQ)) for k in range(1, SEQ)]


def grp_peers(groups):
    g, s = here()
    return [(lax.rem(g + k, groups), s) for k in range(1, groups)]


class Exchange:
    def __init__(self, part, got, full, send1, recv1, send2, recv2):
        self.part, self.got, self.full = part, got, full
        self.sems = (send1, recv1, send2, recv2)

    def first(self):
        g, s = here()
        send1, recv1, _, _ = self.sems
        out = []
        for k in range(1, SEQ):
            to = lax.rem(s + k, SEQ)
            out.append(
                pltpu.make_async_remote_copy(
                    src_ref=self.part.at[to],
                    dst_ref=self.got.at[k - 1],
                    send_sem=send1.at[k - 1],
                    recv_sem=recv1.at[k - 1],
                    device_id=(g, to),
                    device_id_type=MESH_ID,
                )
            )
        return out

    def second(self):
        g, s = here()
        _, _, send2, recv2 = self.sems
        out = []
        for k in range(1, SEQ):
            to = lax.rem(s + k, SEQ)
            out.append(
                pltpu.make_async_remote_copy(
                    src_ref=self.full.at[s],
                    dst_ref=self.full.at[s],
                    send_sem=send2.at[k - 1],
                    recv_sem=recv2.at[k - 1],
                    device_id=(g, to),
                    device_id_type=MESH_ID,
                )
            )
        return out

    def start(self):
        for copy in self.first():
            copy.start()

    def middle(self):
        _, s = here()
        for copy in self.first():
            copy.wait_recv()
        total = self.part[s].astype(F32)
        for k in range(SEQ - 1):
            total += self.got[k].astype(F32)
        self.full[s] = total.astype(BF)
        for copy in self.second():
            copy.start()

    def finish(self):
        for copy in self.second():
            copy.wait_recv()

    def close(self):
        for copy in self.first() + self.second():
            copy.wait_send()


def exchange_scratch(rows, width):
    return [
        pltpu.VMEM((SEQ, rows, width), BF),
        pltpu.VMEM((SEQ - 1, rows, width), BF),
        pltpu.VMEM((SEQ, rows, width), BF),
    ] + [pltpu.SemaphoreType.DMA((SEQ - 1,)) for _ in range(4)]


def halves(block):
    low_lane = lax.broadcasted_iota(jnp.int32, block.shape, 1) < HD
    zero = jnp.zeros_like(block)
    return jnp.concatenate([jnp.where(low_lane, block, zero), jnp.where(low_lane, zero, block)], 0)


def unhalve(block):
    n = block.shape[0] // 2
    low_lane = lax.broadcasted_iota(jnp.int32, (n, block.shape[1]), 1) < HD
    return jnp.where(low_lane, block[:n], block[n:])


def attend(rows, q, ks, vs, probs, mixed, width):
    for pair in range(width // (2 * HD)):
        lanes = slice(pair * 2 * HD, (pair + 1) * 2 * HD)
        scores = mm(q[rows, lanes], halves(ks[:, lanes]), 1, 1)
        parts = []
        for h in range(2):
            sc = scores[:, h * KP : (h + 1) * KP]
            e = jnp.exp(sc - jnp.max(sc, -1, keepdims=True))
            parts.append((e * (1.0 / jnp.sum(e, -1, keepdims=True))).astype(BF))
        p = jnp.concatenate(parts, 1)
        probs[pair, rows, :] = p
        mixed[rows, lanes] = mm(p, halves(vs[:, lanes])).astype(BF)


def forward_kernel(
    slots,
    long_x,
    short_x,
    wq,
    wk,
    wv,
    proj,
    q_out,
    k_out,
    v_out,
    probs_out,
    sums_out,
    mixed_out,
    x,
    wqv,
    wkv,
    wvv,
    pcols,
    pshort,
    q,
    k,
    v,
    probs,
    sums,
    mixed,
    part,
    got,
    full,
    s1,
    r1,
    s2,
    r2,
    sem_in,
    sem_out,
):
    g, s = here()
    short_len = short_x.shape[1]
    width = x.shape[1]
    shorts = slots * short_len
    tokens = x.shape[0]
    shard = tokens - shorts
    long_rows = slice(shorts, tokens)
    copy = pltpu.make_async_copy
    in_long = copy(long_x.at[0], x.at[pl.ds(shorts, shard)], sem_in.at[0])
    in_cols = copy(proj.at[:, span(s * shard, shard)], pcols, sem_in.at[1])
    in_wk = copy(wk, wkv, sem_in.at[2])
    in_wv = copy(wv, wvv, sem_in.at[3])
    in_short = [
        copy(short_x.at[i], x.at[pl.ds(i * short_len, short_len)], sem_in.at[6 + i])
        for i in range(slots)
    ]
    in_wq = copy(wq, wqv, sem_in.at[4])
    in_pshort = copy(proj.at[:, pl.ds(0, short_len)], pshort, sem_in.at[5])
    for c in [in_long, in_cols, in_wk, in_wv] + in_short + [in_wq, in_pshort]:
        c.start()
    greet(seq_peers())
    exchange = Exchange(part, got, full, s1, r1, s2, r2)
    in_long.wait()
    in_wk.wait()
    k[long_rows, :] = mm(x[long_rows, :], wkv[...]).astype(BF)
    in_wv.wait()
    v[long_rows, :] = mm(x[long_rows, :], wvv[...]).astype(BF)
    in_cols.wait()
    blocks = KP // SEQ
    part[:, :, 0:width] = mm(pcols[...], k[long_rows, :]).astype(BF).reshape(SEQ, blocks, width)
    part[:, :, width:] = mm(pcols[...], v[long_rows, :]).astype(BF).reshape(SEQ, blocks, width)
    exchange.start()
    for c in in_short:
        c.wait()
    k[0:shorts, :] = mm(x[0:shorts, :], wkv[...]).astype(BF)
    v[0:shorts, :] = mm(x[0:shorts, :], wvv[...]).astype(BF)
    in_wq.wait()
    q[...] = (0.125 * mm(x[...], wqv[...])).astype(BF)
    in_pshort.wait()
    for i in range(slots):
        rows = slice(i * short_len, (i + 1) * short_len)
        sums[2 * i] = mm(pshort[...], k[rows, :]).astype(BF)
        sums[2 * i + 1] = mm(pshort[...], v[rows, :]).astype(BF)
    exchange.middle()

    @pl.loop(0, slots)
    def _(i):
        attend(span(i * short_len, short_len), q, sums.at[2 * i], sums.at[2 * i + 1], probs, mixed, width)

    exchange.finish()
    sums[2 * slots] = full[:, :, 0:width].reshape(KP, width)
    sums[2 * slots + 1] = full[:, :, width:].reshape(KP, width)
    attend(pl.ds(shorts, shard), q, sums.at[2 * slots], sums.at[2 * slots + 1], probs, mixed, width)
    outs = [
        copy(a, b, sem_out.at[n])
        for n, (a, b) in enumerate(
            [(q, q_out), (k, k_out), (v, v_out), (probs, probs_out), (sums, sums_out), (mixed, mixed_out)]
        )
    ]
    for c in outs:
        c.start()
    for c in outs:
        c.wait()
    exchange.close()


def forward_call(long_x, short_x, wq, wk, wv, proj):
    slots, short_len, width = short_x.shape
    shard = long_x.shape[1]
    tokens = slots * short_len + shard
    pairs = width // (2 * HD)
    blocks = KP // SEQ
    sds = jax.ShapeDtypeStruct
    anyspace = pl.BlockSpec(memory_space=pl.ANY)
    row = (tokens, width)
    shapes = [row, row, row, (pairs, tokens, 2 * KP), (2 * slots + 2, KP, width), row]
    return pl.pallas_call(
        functools.partial(forward_kernel, slots),
        name="attention_forward",
        out_shape=[sds(a, BF) for a in shapes],
        in_specs=[anyspace] * 6,
        out_specs=[anyspace] * 6,
        scratch_shapes=[
            pltpu.VMEM(row, BF),
            pltpu.VMEM((width, width), BF),
            pltpu.VMEM((width, width), BF),
            pltpu.VMEM((width, width), BF),
            pltpu.VMEM((KP, shard), BF),
            pltpu.VMEM((KP, short_len), BF),
        ]
        + [pltpu.VMEM(a, BF) for a in shapes]
        + exchange_scratch(blocks, 2 * width)
        + [pltpu.SemaphoreType.DMA((6 + slots,)), pltpu.SemaphoreType.DMA((6,))],
        compiler_params=pltpu.CompilerParams(
            collective_id=0, has_side_effects=True, vmem_limit_bytes=VMEM_BYTES
        ),
    )(long_x, short_x, wq, wk, wv, proj)


def norm_stats(v):
    mean = jnp.mean(v, -1, keepdims=True)
    centred = v - mean
    root = lax.rsqrt(jnp.mean(centred * centred, -1, keepdims=True) + norm_eps)
    return centred * root, root


def norm_back(grad, gain, xhat, root):
    gg = grad * gain
    return (gg - jnp.mean(gg, -1, keepdims=True) - xhat * jnp.mean(gg * xhat, -1, keepdims=True)) * root


def fold_rows(v):
    return jnp.sum(v.reshape(v.shape[0] // 8, 8, v.shape[1]), 0)


def gelu_pair(u):
    u2 = u * u
    s = 0.5 + 0.5 * jnp.tanh(u * (GELU_A + GELU_B * u2))
    a = u * s
    return a, s + a * (1.0 - s) * (2.0 * GELU_A + 6.0 * GELU_B * u2)


def places(groups):
    out = []
    for d in range(groups * SEQ):
        z, y, x, c = d // SEQ, (d // 4) % 2, (d // 2) % 2, d % 2
        out.append((((c * 2 + x) * 2 + y) * groups + z, ((c * 2 + y) * 2 + x) * groups + z))
    return out


def middle_kernel(
    slots,
    groups,
    long_x,
    short_x,
    mixed_in,
    wo_in,
    up_in,
    down_in,
    long_dy,
    short_dy,
    live,
    gain1,
    shift1,
    gain2,
    shift2,
    long_out,
    short_out,
    resid_out,
    gmix_out,
    gdown_out,
    gup_out,
    gout_out,
    vec_out,
    x,
    mixed,
    wo,
    up,
    down,
    dy,
    act,
    slope,
    xhat,
    root1,
    hid,
    low,
    resid,
    pack,
    tmp,
    sem_in,
    sem_out,
):
    short_len = short_x.shape[1]
    tokens, width = x.shape
    shorts = slots * short_len
    shard = tokens - shorts
    wide = up.shape[1]
    copy = pltpu.make_async_copy
    low_spans = [pl.ds(i * short_len, short_len) for i in range(slots)]

    def rows_in(long_a, short_a, b, base):
        return [copy(long_a.at[0], b.at[pl.ds(shorts, shard)], sem_in.at[base])] + [
            copy(short_a.at[i], b.at[low_spans[i]], sem_in.at[base + 1 + i]) for i in range(slots)
        ]

    first = [copy(mixed_in, mixed, sem_in.at[0]), copy(wo_in, wo, sem_in.at[1])]
    first += rows_in(long_x, short_x, x, 4)
    in_up = copy(up_in, up, sem_in.at[2])
    in_down = copy(down_in, down, sem_in.at[3])
    in_dy = rows_in(long_dy, short_dy, dy, 5 + slots)
    for c in first + [in_up, in_down] + in_dy:
        c.start()
    for c in first:
        c.wait()
    block = 384

    @pl.loop(0, tokens // block)
    def _(i):
        r = span(i * block, block)
        xh, rs = norm_stats(mm(mixed[r, :], wo[...]) + x[r, :].astype(F32))
        xhat[r, :] = xh
        root1[r, :] = jnp.broadcast_to(rs, (block, 128))
        hid[r, :] = (xh * gain1[...] + shift1[...]).astype(BF)

    in_up.wait()
    in_down.wait()
    chunk = 768

    @pl.loop(0, wide // chunk)
    def _(j):
        c = span(j * chunk, chunk)
        a, slope_j = gelu_pair(mm(hid[...], up[:, c]))
        a = a.astype(BF)
        act[:, c] = a
        slope[:, c] = slope_j.astype(BF)
        d = mm(a, down[c, :])

        @pl.when(j == 0)
        def _():
            resid[...] = d

        @pl.when(j > 0)
        def _():
            resid[...] += d

    vec_out[...] = jnp.zeros_like(vec_out)
    for c in in_dy:
        c.wait()
    rb = 128

    @pl.loop(0, tokens // rb)
    def _(i):
        r = span(i * rb, rb)
        alive = jnp.where(lax.div(i * rb, short_len) < live[0], 1.0, 0.0).astype(F32)
        alive = jnp.where(i * rb >= shorts, 1.0, alive)
        xh, rs = norm_stats(xhat[r, :] * gain1[...] + shift1[...] + resid[r, :])
        top = alive * dy[r, :].astype(F32)
        vec_out[16:24, :] += fold_rows(top * xh)
        vec_out[24:32, :] += fold_rows(top)
        dy[r, :] = (alive * (xh * gain2[...] + shift2[...])).astype(BF)
        dx = norm_back(top, gain2[...], xh, rs)
        resid[r, :] = dx
        low[r, :] = dx.astype(BF)

    outs = [copy(dy.at[pl.ds(shorts, shard)], long_out.at[0], sem_out.at[0])]
    outs += [copy(dy.at[low_spans[i]], short_out.at[i], sem_out.at[1 + i]) for i in range(slots)]
    for c in outs:
        c.start()
    base = 1 + slots
    place = places(groups)
    rows = wide // (groups * SEQ)
    half = rows // 2

    @pl.loop(0, groups)
    def _(j):
        c = span(j * SEQ * rows, SEQ * rows)
        d = mm(act[:, c], low[...], 0, 0)
        for s in range(SEQ):
            pack[0, place[s][0] + j] = d[s * rows : s * rows + half].astype(BF)
            pack[1, place[s][1] + j] = d[s * rows + half : (s + 1) * rows].astype(BF)

    out_down = copy(pack, gdown_out, sem_out.at[base])
    out_down.start()

    @pl.loop(0, wide // chunk)
    def _(j):
        c = span(j * chunk, chunk)
        gu = (mm(low[...], down[c, :], 1, 1) * slope[:, c].astype(F32)).astype(BF)
        slope[:, c] = gu
        resid[...] += mm(gu, up[:, c], 1, 1)

    out_down.wait()
    few = width // (groups * SEQ)
    for jp in range(2):

        @pl.loop(0, 2)
        def _(k):
            c = span((jp * 2 + k) * width, width)
            tmp[k] = mm(hid[...], slope[:, c], 0, 0)

        for d in range(groups * SEQ):
            pack[jp, place[d][jp]] = jnp.concatenate(
                [tmp[k, few * d : few * (d + 1), :] for k in range(2)], 0
            ).astype(BF)
    out_up = copy(pack, gup_out, sem_out.at[base + 1])
    out_up.start()

    @pl.loop(0, tokens // rb)
    def _(i):
        r = span(i * rb, rb)
        gh = resid[r, :]
        xh = xhat[r, :]
        vec_out[0:8, :] += fold_rows(gh * xh)
        vec_out[8:16, :] += fold_rows(gh)
        dx = norm_back(gh, gain1[...], xh, root1[r, 0:1])
        resid[r, :] = dx
        low[r, :] = dx.astype(BF)

    out_resid = copy(resid, resid_out, sem_out.at[base + 2])
    out_resid.start()
    tmp[0] = mm(mixed[...], low[...], 0, 0)
    out_gout = copy(tmp.at[0], gout_out, sem_out.at[base + 3])
    out_gout.start()
    hid[...] = mm(low[...], wo[...], 1, 1).astype(BF)
    out_gmix = copy(hid, gmix_out, sem_out.at[base + 4])
    out_gmix.start()
    for c in outs + [out_up, out_resid, out_gout, out_gmix]:
        c.wait()


def middle_call(groups, long_x, short_x, mixed, wo, up, down, long_dy, short_dy, live, vectors):
    slots, short_len, width = short_x.shape
    tokens = slots * short_len + long_x.shape[1]
    wide = up.shape[1]
    devices = groups * SEQ
    sds = jax.ShapeDtypeStruct
    anyspace = pl.BlockSpec(memory_space=pl.ANY)
    vmem = pl.BlockSpec(memory_space=pltpu.VMEM)
    row = (tokens, width)
    packed = (2, devices, wide // devices // 2, width)
    return pl.pallas_call(
        functools.partial(middle_kernel, slots, groups),
        name="feed_forward",
        out_shape=[
            sds(long_x.shape, BF),
            sds(short_x.shape, BF),
            sds(row, F32),
            sds(row, BF),
            sds(packed, BF),
            sds(packed, BF),
            sds((width, width), F32),
            sds((32, width), F32),
        ],
        in_specs=[anyspace] * 8 + [pl.BlockSpec(memory_space=pltpu.SMEM)] + [vmem] * 4,
        out_specs=[anyspace] * 7 + [vmem],
        scratch_shapes=[
            pltpu.VMEM(row, BF),
            pltpu.VMEM(row, BF),
            pltpu.VMEM((width, width), BF),
            pltpu.VMEM((width, wide), BF),
            pltpu.VMEM((wide, width), BF),
            pltpu.VMEM(row, BF),
            pltpu.VMEM((tokens, wide), BF),
            pltpu.VMEM((tokens, wide), BF),
            pltpu.VMEM(row, F32),
            pltpu.VMEM((tokens, 128), F32),
            pltpu.VMEM(row, BF),
            pltpu.VMEM(row, BF),
            pltpu.VMEM(row, F32),
            pltpu.VMEM(packed, BF),
            pltpu.VMEM((2, width, width), F32),
            pltpu.SemaphoreType.DMA((6 + 2 * slots,)),
            pltpu.SemaphoreType.DMA((6 + slots,)),
        ],
        compiler_params=pltpu.CompilerParams(vmem_limit_bytes=VMEM_BYTES),
    )(long_x, short_x, mixed, wo, up, down, long_dy, short_dy, live, *vectors)


class Scatter:
    def __init__(self, src, local, bits, bufs):
        self.src, self.local, self.bits = src, local, bits
        (self.recv, self.last, self.send_sem, self.recv_sem, self.send_z, self.recv_z) = bufs[:6]
        self.own, self.own_sem = bufs[6:] if local else (None, None)

    def kept(self, n):
        _, s = here()
        src = self.src if n == 0 else self.recv[n - 1]
        size = src.shape[0] // 2
        return src, lax.rem(lax.div(s, self.bits[n]), 2) * size, size

    def hop(self, n):
        g, s = here()
        bit = self.bits[n]
        mine = lax.rem(lax.div(s, bit), 2)
        src, _, size = self.kept(n)
        return pltpu.make_async_remote_copy(
            src_ref=src.at[pl.ds((1 - mine) * size, size)],
            dst_ref=self.recv[n],
            send_sem=self.send_sem.at[n],
            recv_sem=self.recv_sem.at[n],
            device_id=(g, s + bit - 2 * bit * mine),
            device_id_type=MESH_ID,
        )

    def keep(self):
        src, start, size = self.kept(0)
        return pltpu.make_async_copy(src.at[pl.ds(start, size)], self.own, self.own_sem.at[0])

    def along(self):
        g, s = here()
        groups = self.recv[2].shape[0]
        out = []
        for k in range(1, groups):
            to = lax.rem(g + k, groups)
            out.append(
                pltpu.make_async_remote_copy(
                    src_ref=self.recv[2].at[to],
                    dst_ref=self.last.at[k - 1],
                    send_sem=self.send_z.at[k - 1],
                    recv_sem=self.recv_z.at[k - 1],
                    device_id=(to, s),
                    device_id_type=MESH_ID,
                )
            )
        return out

    def start(self):
        self.hop(0).start()
        if self.local:
            self.keep().start()

    def step(self, n):
        src, start, size = self.kept(n)
        self.hop(n).wait_recv()
        if n == 0 and self.local:
            self.keep().wait()
            src, start = self.own, 0
        dst = self.recv[n]

        @pl.loop(0, size)
        def _(i):
            dst[i] = (dst[i].astype(F32) + src[start + i].astype(F32)).astype(BF)

        if n < 2:
            self.hop(n + 1).start()
        else:
            for c in self.along():
                c.start()

    def total(self):
        for c in self.along():
            c.wait_recv()
        g, _ = here()
        total = self.recv[2][g].astype(F32)
        for k in range(self.last.shape[0]):
            total += self.last[k].astype(F32)
        return total

    def close(self):
        for n in range(3):
            self.hop(n).wait_send()
        for c in self.along():
            c.wait_send()


def scatter_scratch(groups, rows, width, local):
    n = groups * SEQ
    out = [pltpu.VMEM((n // 2**k, rows, width), BF) for k in (1, 2, 3)]
    out += [pltpu.VMEM((groups - 1, rows, width), BF)]
    out += [pltpu.SemaphoreType.DMA((3,)), pltpu.SemaphoreType.DMA((3,))]
    out += [pltpu.SemaphoreType.DMA((groups - 1,)), pltpu.SemaphoreType.DMA((groups - 1,))]
    if local:
        out += [pltpu.VMEM((n // 2, rows, width), BF), pltpu.SemaphoreType.DMA((1,))]
    return out


def scatter_bufs(refs):
    return (tuple(refs[:3]),) + tuple(refs[3:])


class Vectors:
    def __init__(self, mine, recv, last, send_sem, recv_sem, send_z, recv_z):
        self.mine, self.recv, self.last = mine, recv, last
        self.sems = (send_sem, recv_sem, send_z, recv_z)

    def hop(self, n):
        g, s = here()
        bit = 1 << n
        other = s + bit - 2 * bit * lax.rem(lax.div(s, bit), 2)
        return pltpu.make_async_remote_copy(
            src_ref=self.mine.at[n],
            dst_ref=self.recv.at[n],
            send_sem=self.sems[0].at[n],
            recv_sem=self.sems[1].at[n],
            device_id=(g, other),
            device_id_type=MESH_ID,
        )

    def along(self):
        g, s = here()
        groups = self.last.shape[0] + 1
        return [
            pltpu.make_async_remote_copy(
                src_ref=self.mine.at[3],
                dst_ref=self.last.at[k - 1],
                send_sem=self.sems[2].at[k - 1],
                recv_sem=self.sems[3].at[k - 1],
                device_id=(lax.rem(g + k, groups), s),
                device_id_type=MESH_ID,
            )
            for k in range(1, groups)
        ]

    def start(self):
        self.hop(0).start()

    def step(self, n):
        self.hop(n).wait_recv()
        self.mine[n + 1] = self.mine[n] + self.recv[n]
        if n < 2:
            self.hop(n + 1).start()
        else:
            for c in self.along():
                c.start()

    def total(self):
        for c in self.along():
            c.wait_recv()
        return self.mine[3] + sum(self.last[k] for k in range(self.last.shape[0]))

    def close(self):
        for c in [self.hop(n) for n in range(3)] + self.along():
            c.wait_send()


class ProjGrad:
    def __init__(self, part, got, short, got_short, *sems):
        self.part, self.got, self.short, self.got_short, self.sems = part, got, short, got_short, sems

    def along(self):
        g, s = here()
        groups = self.part.shape[0]
        out = []
        for k in range(1, groups):
            to = lax.rem(g + k, groups)
            out.append(
                pltpu.make_async_remote_copy(
                    src_ref=self.part.at[to],
                    dst_ref=self.got.at[k - 1],
                    send_sem=self.sems[0].at[k - 1],
                    recv_sem=self.sems[1].at[k - 1],
                    device_id=(to, s),
                    device_id_type=MESH_ID,
                )
            )
        return out

    def across(self, b):
        g, s = here()
        slot = lax.rem(s - b + 2 * SEQ - 1, SEQ)
        return pltpu.make_async_remote_copy(
            src_ref=self.short.at[b],
            dst_ref=self.got_short.at[slot],
            send_sem=self.sems[2].at[b],
            recv_sem=self.sems[3].at[slot],
            device_id=(g, jnp.int32(b)),
            device_id_type=MESH_ID,
        )

    def arrived(self, slot):
        g, s = here()
        return pltpu.make_async_remote_copy(
            src_ref=self.short.at[0],
            dst_ref=self.got_short.at[slot],
            send_sem=self.sems[2].at[0],
            recv_sem=self.sems[3].at[slot],
            device_id=(g, s),
            device_id_type=MESH_ID,
        )

    def start(self):
        for c in self.along():
            c.start()

    def middle(self, out, shard):
        g, s = here()
        for c in self.along():
            c.wait_recv()
        total = self.part[g].astype(F32)
        for k in range(self.got.shape[0]):
            total += self.got[k].astype(F32)
        out[...] = total[:, 0:shard]
        for b in range(self.short.shape[0]):
            self.short[b] = total[:, (b + 1) * shard : (b + 2) * shard].astype(BF)

            @pl.when(s != b)
            def _(b=b):
                self.across(b).start()

    def finish(self, out):
        _, s = here()
        count = self.short.shape[0]

        @pl.when(s < count)
        def _():
            total = out[...] + self.short[lax.rem(s, count)].astype(F32)
            for slot in range(SEQ - 1):
                self.arrived(slot).wait_recv()
                total += self.got_short[slot].astype(F32)
            out[...] = total

    def close(self):
        _, s = here()
        for c in self.along():
            c.wait_send()
        for b in range(self.short.shape[0]):

            @pl.when(s != b)
            def _(b=b):
                self.across(b).wait_send()


def attend_back(rows, q, gmix, probs, ks, vs, put, width):
    for pair in range(width // (2 * HD)):
        lanes = slice(pair * 2 * HD, (pair + 1) * 2 * HD)
        gm = gmix[rows, lanes]
        qp = q[rows, lanes]
        p = probs[pair, rows, :]
        gp = mm(gm, halves(vs[:, lanes]), 1, 1)
        value_grad = unhalve(mm(p, gm, 0, 0)).astype(BF)
        parts = []
        for h in range(2):
            ph = p[:, h * KP : (h + 1) * KP].astype(F32)
            t = ph * gp[:, h * KP : (h + 1) * KP]
            parts.append((t - ph * jnp.sum(t, -1, keepdims=True)).astype(BF))
        gs = jnp.concatenate(parts, 1)
        q[rows, lanes] = (mm(gs, halves(ks[:, lanes])).astype(BF).astype(F32) * 0.125).astype(BF)
        key_grad = unhalve(mm(gs, qp, 0, 0)).astype(BF)
        put(lanes, key_grad, value_grad)


def backward_kernel(slots, groups, *refs):
    refs = list(refs)

    def take(n):
        out = refs[:n]
        del refs[:n]
        return out

    (long_x, short_x, q_in, k_in, v_in, probs_in, sums_in, gmix_in, resid_in, gdown, gup, gout) = take(12)
    (wq_in, wk_in, wv_in, proj, vec_in) = take(5)
    (long_grad, short_grad, grad_q, grad_k, grad_v, grad_o, grad_up, grad_down, grad_proj, vec_out) = take(10)
    (x, q, k, v, probs, sums, gmix, resid, wq, wk, wv, pcols, pshort) = take(13)
    (tmp, pack, ksum, vsum, pacc) = take(5)
    sem_in, sem_out = take(2)
    exchange = Exchange(*take(7))
    vectors = Vectors(*take(7))
    projected = ProjGrad(*take(8))
    xy, yx = (1, 2, 4), (1, 4, 2)
    down0 = Scatter(gdown.at[0], True, xy, scatter_bufs(take(10)))
    down1 = Scatter(gdown.at[1], True, yx, scatter_bufs(take(10)))
    up0 = Scatter(gup.at[0], True, xy, scatter_bufs(take(10)))
    up1 = Scatter(gup.at[1], True, yx, scatter_bufs(take(10)))
    qk = Scatter(pack.at[0], False, xy, scatter_bufs(take(8)))
    vo = Scatter(pack.at[1], False, yx, scatter_bufs(take(8)))
    assert not refs

    g, s = here()
    short_len = short_x.shape[1]
    tokens, width = x.shape
    shorts = slots * short_len
    shard = tokens - shorts
    copy = pltpu.make_async_copy
    long_rows = pl.ds(shorts, shard)
    greet(seq_peers() + grp_peers(groups))
    for piece in (down0, down1, up0, up1):
        piece.start()
    ins = {}
    for name, a, b in [
        ("gmix", gmix_in, gmix),
        ("q", q_in, q),
        ("probs", probs_in, probs),
        ("sums", sums_in, sums),
        ("k", k_in, k),
        ("v", v_in, v),
        ("pshort", proj.at[:, pl.ds(0, short_len)], pshort),
        ("pcols", proj.at[:, span(s * shard, shard)], pcols),
        ("x", long_x.at[0], x.at[long_rows]),
        ("wq", wq_in, wq),
        ("wk", wk_in, wk),
        ("wv", wv_in, wv),
        ("resid", resid_in, resid),
    ]:
        ins[name] = copy(a, b, sem_in.at[len(ins)])
    for i in range(slots):
        ins[i] = copy(short_x.at[i], x.at[pl.ds(i * short_len, short_len)], sem_in.at[len(ins)])
    for c in ins.values():
        c.start()
    vec = jnp.sum(vec_in[...].reshape(4, 8, width), 1)
    vectors.mine[0] = jnp.concatenate([vec, jnp.zeros_like(vec)], 0)
    vectors.start()
    for name in ("gmix", "q", "probs", "sums"):
        ins[name].wait()
    blocks = KP // SEQ

    def put_long(lanes, key_grad, value_grad):
        other = slice(lanes.start + width, lanes.stop + width)
        exchange.part[:, :, lanes] = key_grad.reshape(SEQ, blocks, 2 * HD)
        exchange.part[:, :, other] = value_grad.reshape(SEQ, blocks, 2 * HD)

    attend_back(long_rows, q, gmix, probs, sums.at[2 * slots], sums.at[2 * slots + 1], put_long, width)
    exchange.start()
    vectors.step(0)
    down0.step(0)
    down1.step(0)
    for name in ("k", "v", "pshort", "pcols"):
        ins[name].wait()
    pacc[...] = jnp.zeros_like(pacc)

    def put_short(lanes, key_grad, value_grad):
        ksum[:, lanes] = key_grad
        vsum[:, lanes] = value_grad

    @pl.loop(0, slots)
    def _(i):
        rows = span(i * short_len, short_len)
        attend_back(rows, q, gmix, probs, sums.at[2 * i], sums.at[2 * i + 1], put_short, width)
        pacc[...] += mm(ksum[...], k[rows, :], 1, 1) + mm(vsum[...], v[rows, :], 1, 1)
        k[rows, :] = mm(pshort[...], ksum[...], 0, 0).astype(BF)
        v[rows, :] = mm(pshort[...], vsum[...], 0, 0).astype(BF)

        @pl.when(i == 0)
        def _():
            exchange.middle()
            up0.step(0)
            up1.step(0)
            vectors.step(1)

        @pl.when(i == 1)
        def _():
            down0.step(1)
            down1.step(1)
            vectors.step(2)

        @pl.when(i == 2)
        def _():
            up0.step(1)
            up1.step(1)

    exchange.finish()
    ksum[...] = exchange.full[:, :, 0:width].reshape(KP, width)
    vsum[...] = exchange.full[:, :, width:].reshape(KP, width)
    long_cols = mm(ksum[...], k[long_rows, :], 1, 1) + mm(vsum[...], v[long_rows, :], 1, 1)
    k[long_rows, :] = mm(pcols[...], ksum[...], 0, 0).astype(BF)
    v[long_rows, :] = mm(pcols[...], vsum[...], 0, 0).astype(BF)
    prow = KP // groups
    projected.part[:, :, 0:shard] = long_cols.astype(BF).reshape(groups, prow, shard)
    projected.part[:, :, shard:] = pacc[...].astype(BF).reshape(groups, prow, short_len)
    projected.start()
    down0.step(2)
    down1.step(2)
    for name in ["x"] + list(range(slots)):
        ins[name].wait()
    place = places(groups)
    few = width // (groups * SEQ)

    def packed(n):
        for d in range(groups * SEQ):
            pack[n, place[d][n]] = jnp.concatenate(
                [tmp[m, few * d : few * (d + 1), :] for m in range(2)], 0
            ).astype(BF)

    tmp[0] = mm(x[...], q[...], 0, 0)
    tmp[1] = mm(x[...], k[...], 0, 0)
    packed(0)
    qk.start()
    up0.step(2)
    up1.step(2)
    in_gout = copy(gout, tmp.at[1], sem_out.at[0])
    in_gout.start()
    tmp[0] = mm(x[...], v[...], 0, 0)
    in_gout.wait()
    packed(1)
    vo.start()
    projected.middle(grad_proj, shard)
    for name in ("wq", "wk", "wv", "resid"):
        ins[name].wait()
    block = 384
    for i in range(tokens // block):
        r = pl.ds(i * block, block)
        gmix[r, :] = (
            resid[r, :] + mm(q[r, :], wq[...], 1, 1) + mm(k[r, :], wk[...], 1, 1) + mm(v[r, :], wv[...], 1, 1)
        ).astype(BF)
        if i < 3:
            qk.step(i)
            vo.step(i)
    outs = [copy(gmix.at[long_rows], long_grad.at[0], sem_out.at[1])]
    outs += [
        copy(gmix.at[pl.ds(i * short_len, short_len)], short_grad.at[i], sem_out.at[2 + i]) for i in range(slots)
    ]
    for c in outs:
        c.start()
    half = grad_down.shape[0] // 2
    grad_down[0:half, :] = down0.total()
    grad_down[half:, :] = down1.total()
    for n, piece in enumerate((up0, up1)):
        t = piece.total()
        grad_up[:, 2 * n * width : (2 * n + 1) * width] = t[0:few]
        grad_up[:, (2 * n + 1) * width : (2 * n + 2) * width] = t[few:]
    vec_out[...] = vectors.total()
    projected.finish(grad_proj)
    t = qk.total()
    grad_q[...] = t[0:few]
    grad_k[...] = t[few:]
    t = vo.total()
    grad_v[...] = t[0:few]
    grad_o[...] = t[few:]
    for c in outs:
        c.wait()
    for piece in (down0, down1, up0, up1, qk, vo, vectors, projected, exchange):
        piece.close()


def backward_call(groups, long_x, short_x, saved, gmix, resid, gdown, gup, gout, wq, wk, wv, proj, vec):
    slots, short_len, width = short_x.shape
    shard = long_x.shape[1]
    tokens = slots * short_len + shard
    devices = groups * SEQ
    pairs = width // (2 * HD)
    few = width // devices
    sds = jax.ShapeDtypeStruct
    anyspace = pl.BlockSpec(memory_space=pl.ANY)
    vmem = pl.BlockSpec(memory_space=pltpu.VMEM)
    dma = pltpu.SemaphoreType.DMA
    row = (tokens, width)
    square = (width, width)
    prow = KP // groups
    piece = gdown.shape[2]
    few_shapes = [(few, width)] * 4 + [(few, 4 * width), (4 * few, width), (prow, shard), (8, width)]
    scratch = [pltpu.VMEM(row, BF)] * 4
    scratch += [pltpu.VMEM((pairs, tokens, 2 * KP), BF), pltpu.VMEM((2 * slots + 2, KP, width), BF)]
    scratch += [pltpu.VMEM(row, BF), pltpu.VMEM(row, F32)] + [pltpu.VMEM(square, BF)] * 3
    scratch += [pltpu.VMEM((KP, shard), BF), pltpu.VMEM((KP, short_len), BF)]
    scratch += [pltpu.VMEM((2,) + square, F32), pltpu.VMEM((2, devices, piece, width), BF)]
    scratch += [pltpu.VMEM((KP, width), BF)] * 2 + [pltpu.VMEM((KP, short_len), F32)]
    scratch += [dma((13 + slots,)), dma((2 + slots,))]
    scratch += exchange_scratch(KP // SEQ, 2 * width)
    scratch += [pltpu.VMEM((4, 8, width), F32), pltpu.VMEM((3, 8, width), F32), pltpu.VMEM((groups - 1, 8, width), F32)]
    scratch += [dma((3,)), dma((3,)), dma((groups - 1,)), dma((groups - 1,))]
    heads = short_len // shard
    scratch += [pltpu.VMEM((groups, prow, shard + short_len), BF), pltpu.VMEM((groups - 1, prow, shard + short_len), BF)]
    scratch += [pltpu.VMEM((heads, prow, shard), BF), pltpu.VMEM((SEQ - 1, prow, shard), BF)]
    scratch += [dma((groups - 1,)), dma((groups - 1,)), dma((heads,)), dma((SEQ - 1,))]
    for local in (True, True, True, True, False, False):
        scratch += scatter_scratch(groups, piece, width, local)
    return pl.pallas_call(
        functools.partial(backward_kernel, slots, groups),
        name="attention_backward",
        out_shape=[sds(long_x.shape, BF), sds(short_x.shape, BF)] + [sds(a, F32) for a in few_shapes],
        in_specs=[anyspace] * 16 + [vmem],
        out_specs=[anyspace] * 2 + [vmem] * 8,
        scratch_shapes=scratch,
        compiler_params=pltpu.CompilerParams(
            collective_id=1, has_side_effects=True, vmem_limit_bytes=VMEM_BYTES
        ),
    )(long_x, short_x, *saved, gmix, resid, gdown, gup, gout, wq, wk, wv, proj, vec)


def fast_shards(groups, *args):
    (long_x, short_x, long_dy, short_dy, live, wq, wk, wv, wo, up, down, proj, g1, b1, g2, b2) = args
    q, k, v, probs, sums, mixed = forward_call(long_x, short_x, wq, wk, wv, proj)
    vectors = [a.reshape(1, -1) for a in (g1, b1, g2, b2)]
    long_out, short_out, resid, gmix, gdown, gup, gout, vec = middle_call(
        groups, long_x, short_x, mixed, wo, up, down, long_dy, short_dy, live, vectors
    )
    outs = backward_call(
        groups, long_x, short_x, (q, k, v, probs, sums), gmix, resid, gdown, gup, gout, wq, wk, wv, proj, vec
    )
    few = g1.shape[0] // (groups * SEQ)
    start = (lax.axis_index("grp") * SEQ + lax.axis_index("seq")) * few
    mine = lax.dynamic_slice_in_dim(outs[9], start, few, 1)
    return (long_out, short_out) + tuple(outs[:9]) + tuple(mine[i] for i in range(4))


def fits(mesh, args):
    long_x, width, wide = args[0], args[0].shape[2], args[9].shape[1]
    devices = mesh.shape["grp"] * mesh.shape["seq"]
    whole = width % (devices * 8) == 0 and wide == 4 * width
    return mesh.shape["seq"] == SEQ and whole and long_x.shape[0] == 1


def solution(mesh):
    placed = (
        P("grp", "seq", None),
        P(("grp", "seq"), None, None),
        P("grp", "seq", None),
        P(("grp", "seq"), None, None),
        P(("grp", "seq")),
        P(),
        P(),
        P(),
        P(),
        P(),
        P(),
        P(),
        P(),
        P(),
        P(),
        P(),
    )
    groups = mesh.shape["grp"]

    def body(*args):
        if fits(mesh, args):
            return fast_shards(groups, *args)
        return shards(*args)

    return jax.shard_map(
        body,
        mesh=mesh,
        in_specs=placed,
        out_specs=(
            P("grp", "seq", None),
            P(("grp", "seq"), None, None),
            P("grp", "seq", None),
            P(("grp", "seq"), None, None),
            P(("grp", "seq"), None),
            P(("grp", "seq"), None),
            P(("grp", "seq"), None),
            P(("grp", "seq"), None),
            P(("grp", "seq"), None),
            P(("grp", "seq"), None),
            P("grp", "seq"),
            P(("grp", "seq")),
            P(("grp", "seq")),
            P(("grp", "seq")),
            P(("grp", "seq")),
        ),
        check_vma=False,
    )
```

```python
import functools

import jax
import jax.numpy as jnp
from jax import lax
from jax.experimental import pallas as pl
from jax.experimental.pallas import tpu as pltpu
from jax.sharding import PartitionSpec as P

HD = 64
KP = 256


norm_eps = 1e-05


def shortened(shard):
    return jax.tree.map(lambda a: a.astype(jnp.bfloat16) if a.dtype == jnp.float32 else a, shard)


def norm_rows(resid, gain_vec, shift_vec):
    row_mean = jnp.mean(resid, axis=-1, keepdims=True)
    centred = resid - row_mean
    variance = jnp.mean(centred * centred, axis=-1, keepdims=True)
    return centred * lax.rsqrt(variance + norm_eps) * gain_vec + shift_vec


def smooth_gate(upward):
    return jax.nn.gelu(upward, approximate=True)


def same_sums(partials):
    return partials


def layer_pass(sequences, cotangent, live_rows, proj_cols, fold_summaries, fold_grads, params):
    (
        query_w,
        key_w,
        value_w,
        out_w,
        up_w,
        down_w,
        gain_first,
        shift_first,
        gain_second,
        shift_second,
    ) = params
    seq_count, length, model_width = sequences.shape
    head_count = model_width // HD
    wide = jnp.float32
    narrow = jnp.bfloat16
    queries = (
        0.125 * jnp.einsum("nld,de->nle", sequences, query_w, preferred_element_type=wide)
    ).astype(narrow)
    key_vecs = jnp.einsum("nld,de->nle", sequences, key_w, preferred_element_type=wide).astype(
        narrow
    )
    value_vecs = jnp.einsum("nld,de->nle", sequences, value_w, preferred_element_type=wide).astype(
        narrow
    )
    key_part = jnp.einsum("kl,nld->nkd", proj_cols, key_vecs, preferred_element_type=wide)
    value_part = jnp.einsum("kl,nld->nkd", proj_cols, value_vecs, preferred_element_type=wide)
    key_sum, value_sum = fold_summaries((key_part, value_part))
    key_heads = key_sum.astype(narrow).reshape(seq_count, KP, head_count, HD)
    value_heads = value_sum.astype(narrow).reshape(seq_count, KP, head_count, HD)
    query_heads = queries.reshape(seq_count, length, head_count, HD)
    scores = jnp.einsum("nlhe,nkhe->nhlk", query_heads, key_heads, preferred_element_type=wide)
    attn_probs = jax.nn.softmax(scores, axis=-1)
    probs_low = attn_probs.astype(narrow)
    mixed_heads = (
        jnp.einsum("nhlk,nkhe->nlhe", probs_low, value_heads, preferred_element_type=wide)
        .reshape(seq_count, length, model_width)
        .astype(narrow)
    )
    attn_out = jnp.einsum("nld,de->nle", mixed_heads, out_w, preferred_element_type=wide)
    hidden, first_back = jax.vjp(
        norm_rows, sequences.astype(wide) + attn_out, gain_first, shift_first
    )
    hidden_low = hidden.astype(narrow)
    upward = jnp.einsum("nld,df->nlf", hidden_low, up_w, preferred_element_type=wide)
    activated, gate_back = jax.vjp(smooth_gate, upward)
    activated_low = activated.astype(narrow)
    branch = jnp.einsum("nlf,fd->nld", activated_low, down_w, preferred_element_type=wide)
    normed, second_back = jax.vjp(norm_rows, hidden + branch, gain_second, shift_second)
    result = normed * live_rows[:, None, None]
    grad_top = cotangent.astype(wide) * live_rows[:, None, None]
    grad_resid_two, grad_gain_two, grad_shift_two = second_back(grad_top)
    grad_branch = grad_resid_two.astype(narrow)
    grad_down = jnp.einsum("nlf,nld->fd", activated_low, grad_branch, preferred_element_type=wide)
    grad_activated = jnp.einsum("nld,fd->nlf", grad_branch, down_w, preferred_element_type=wide)
    (grad_upward,) = gate_back(grad_activated)
    grad_upward_low = grad_upward.astype(narrow)
    grad_up = jnp.einsum("nld,nlf->df", hidden_low, grad_upward_low, preferred_element_type=wide)
    grad_hidden = grad_resid_two + jnp.einsum(
        "nlf,df->nld", grad_upward_low, up_w, preferred_element_type=wide
    )
    grad_resid_one, grad_gain_one, grad_shift_one = first_back(grad_hidden)
    grad_attn = grad_resid_one.astype(narrow)
    grad_out = jnp.einsum("nld,nle->de", mixed_heads, grad_attn, preferred_element_type=wide)
    grad_mixed = (
        jnp.einsum("nle,de->nld", grad_attn, out_w, preferred_element_type=wide)
        .astype(narrow)
        .reshape(seq_count, length, head_count, HD)
    )
    grad_probs = jnp.einsum("nlhe,nkhe->nhlk", grad_mixed, value_heads, preferred_element_type=wide)
    value_grad_part = jnp.einsum(
        "nhlk,nlhe->nkhe", probs_low, grad_mixed, preferred_element_type=wide
    ).reshape(seq_count, KP, model_width)
    grad_scores = attn_probs * (
        grad_probs - jnp.sum(grad_probs * attn_probs, axis=-1, keepdims=True)
    )
    scores_low = grad_scores.astype(narrow)
    grad_queries = (
        jnp.einsum("nhlk,nkhe->nlhe", scores_low, key_heads, preferred_element_type=wide).astype(
            narrow
        )
        * 0.125
    ).reshape(seq_count, length, model_width)
    key_grad_part = jnp.einsum(
        "nhlk,nlhe->nkhe", scores_low, query_heads, preferred_element_type=wide
    ).reshape(seq_count, KP, model_width)
    key_grad_sum, value_grad_sum = fold_grads((key_grad_part, value_grad_part))
    key_grad_low = key_grad_sum.astype(narrow)
    value_grad_low = value_grad_sum.astype(narrow)
    grad_keys = jnp.einsum(
        "kl,nkd->nld", proj_cols, key_grad_low, preferred_element_type=wide
    ).astype(narrow)
    grad_values = jnp.einsum(
        "kl,nkd->nld", proj_cols, value_grad_low, preferred_element_type=wide
    ).astype(narrow)
    grad_cols = jnp.einsum(
        "nkd,nld->kl", key_grad_low, key_vecs, preferred_element_type=wide
    ) + jnp.einsum("nkd,nld->kl", value_grad_low, value_vecs, preferred_element_type=wide)
    grad_query = jnp.einsum("nld,nle->de", sequences, grad_queries, preferred_element_type=wide)
    grad_key = jnp.einsum("nld,nle->de", sequences, grad_keys, preferred_element_type=wide)
    grad_value = jnp.einsum("nld,nle->de", sequences, grad_values, preferred_element_type=wide)
    grad_sequences = grad_resid_one + jnp.einsum(
        "nle,de->nld", grad_queries, query_w, preferred_element_type=wide
    )
    grad_sequences = grad_sequences + jnp.einsum(
        "nle,de->nld", grad_keys, key_w, preferred_element_type=wide
    )
    grad_sequences = grad_sequences + jnp.einsum(
        "nle,de->nld", grad_values, value_w, preferred_element_type=wide
    )
    weight_grads = (
        grad_query,
        grad_key,
        grad_value,
        grad_out,
        grad_up,
        grad_down,
        grad_gain_one,
        grad_shift_one,
        grad_gain_two,
        grad_shift_two,
    )
    return (result, grad_sequences, weight_grads, grad_cols)


def shards(
    long_x,
    short_x,
    long_dy,
    short_dy,
    short_live,
    query_weight,
    key_weight,
    value_weight,
    out_weight,
    up_weight,
    down_weight,
    length_proj,
    gain_one,
    shift_one,
    gain_two,
    shift_two,
):
    params = (
        query_weight,
        key_weight,
        value_weight,
        out_weight,
        up_weight,
        down_weight,
        gain_one,
        shift_one,
        gain_two,
        shift_two,
    )
    shard_len = long_x.shape[1]
    slot_count = short_x.shape[0]
    short_len = short_x.shape[1]
    shard_start = lax.axis_index("seq") * shard_len
    long_cols = lax.dynamic_slice_in_dim(length_proj, shard_start, shard_len, 1)

    def sum_summaries(partials):
        return jax.tree.map(
            lambda part: part.astype(jnp.float32), lax.psum(shortened(partials), "seq")
        )

    def sum_summary_grads(partials):
        return jax.tree.map(
            lambda part: part.astype(jnp.float32), lax.psum(shortened(partials), "seq")
        )

    long_live = jnp.ones((long_x.shape[0],), jnp.float32)
    long_result, long_back, long_weights, long_proj = layer_pass(
        long_x, long_dy, long_live, long_cols, sum_summaries, sum_summary_grads, params
    )
    short_mask = (jnp.arange(slot_count) < short_live[0]).astype(jnp.float32)
    short_result, short_back, short_weights, short_proj = layer_pass(
        short_x, short_dy, short_mask, length_proj[:, :short_len], same_sums, same_sums, params
    )
    summed = jax.tree.map(jnp.add, long_weights, short_weights)
    (
        grad_query,
        grad_key,
        grad_value,
        grad_out,
        grad_up,
        grad_down,
        grad_gain_one,
        grad_shift_one,
        grad_gain_two,
        grad_shift_two,
    ) = summed
    proj_total = jnp.zeros(length_proj.shape, jnp.float32)
    proj_total = lax.dynamic_update_slice_in_dim(proj_total, long_proj, shard_start, 1)
    proj_total = proj_total.at[:, :short_len].add(short_proj)
    proj_rows = lax.psum_scatter(
        proj_total.astype(jnp.bfloat16), "grp", scatter_dimension=0, tiled=True
    )
    proj_part = lax.psum_scatter(proj_rows, "seq", scatter_dimension=1, tiled=True).astype(
        jnp.float32
    )
    reduced = (
        lax.psum_scatter(grad_query, ("grp", "seq"), scatter_dimension=0, tiled=True),
        lax.psum_scatter(grad_key, ("grp", "seq"), scatter_dimension=0, tiled=True),
        lax.psum_scatter(grad_value, ("grp", "seq"), scatter_dimension=0, tiled=True),
        lax.psum_scatter(grad_out, ("grp", "seq"), scatter_dimension=0, tiled=True),
        lax.psum_scatter(grad_up, ("grp", "seq"), scatter_dimension=0, tiled=True),
        lax.psum_scatter(grad_down, ("grp", "seq"), scatter_dimension=0, tiled=True),
        lax.psum_scatter(grad_gain_one, ("grp", "seq"), scatter_dimension=0, tiled=True),
        lax.psum_scatter(grad_shift_one, ("grp", "seq"), scatter_dimension=0, tiled=True),
        lax.psum_scatter(grad_gain_two, ("grp", "seq"), scatter_dimension=0, tiled=True),
        lax.psum_scatter(grad_shift_two, ("grp", "seq"), scatter_dimension=0, tiled=True),
    )
    reduced = tuple(reduced)
    return (
        (
            long_result.astype(jnp.bfloat16),
            short_result.astype(jnp.bfloat16),
            long_back.astype(jnp.bfloat16),
            short_back.astype(jnp.bfloat16),
        )
        + reduced[:6]
        + (proj_part,)
        + reduced[6:]
    )


MESH_ID = pl.DeviceIdType.MESH
BF = jnp.bfloat16
F32 = jnp.float32
VMEM_BYTES = 65400 * 1024
GELU_A = 0.7978845608028654
GELU_B = 0.044715 * GELU_A
SEQ = 8


def mm(a, b, ca=1, cb=0):
    return lax.dot_general(a, b, (((ca,), (cb,)), ((), ())), preferred_element_type=F32)


def span(start, size, step=None):
    return pl.ds(pl.multiple_of(start, step or size), size)


def here():
    return lax.axis_index("grp"), lax.axis_index("seq")


def greet(peers):
    barrier = pltpu.get_barrier_semaphore()
    for peer in peers:
        pl.semaphore_signal(barrier, inc=1, device_id=peer, device_id_type=MESH_ID)
    pl.semaphore_wait(barrier, len(peers))


def seq_peers():
    g, s = here()
    return [(g, lax.rem(s + k, SEQ)) for k in range(1, SEQ)]


def grp_peers(groups):
    g, s = here()
    return [(lax.rem(g + k, groups), s) for k in range(1, groups)]


class Exchange:
    def __init__(self, part, got_core, got, full, send_sem, recv_sem):
        self.part, self.got_core, self.got, self.full = part, got_core, got, full
        self.send_sem, self.recv_sem = send_sem, recv_sem

    def place(self):
        _, s = here()
        core, chip = lax.rem(s, 2), lax.div(s, 2)
        x, y = 1 - 2 * lax.rem(chip, 2), 2 - 4 * lax.div(chip, 2)
        return core, chip, (chip + x, chip + y, chip + x + y)

    def send(self, n, src, dst, to):
        g, _ = here()
        return pltpu.make_async_remote_copy(
            src_ref=src,
            dst_ref=dst,
            send_sem=self.send_sem.at[n],
            recv_sem=self.recv_sem.at[n],
            device_id=(g, to),
            device_id_type=MESH_ID,
        )

    def halve(self):
        core, chip, _ = self.place()
        return self.send(0, self.part.at[pl.ds(4 * (1 - core), 4)], self.got_core, 2 * chip + 1 - core)

    def across(self):
        core, _, chips = self.place()
        return [
            self.send(1 + k, self.part.at[4 * core + to], self.got.at[k], 2 * to + core) for k, to in enumerate(chips)
        ]

    def spread(self):
        core, chip, chips = self.place()
        own = self.full.at[4 * core + chip]
        return [self.send(4 + k, own, own, 2 * to + core) for k, to in enumerate(chips)]

    def join(self):
        core, chip, _ = self.place()
        own = self.full.at[pl.ds(4 * core, 4)]
        return self.send(7, own, own, 2 * chip + 1 - core)

    def start(self):
        self.halve().start()

    def first(self):
        core, _, _ = self.place()
        self.halve().wait_recv()
        for n in range(4):
            self.part[4 * core + n] = (self.part[4 * core + n].astype(F32) + self.got_core[n].astype(F32)).astype(BF)
        for c in self.across():
            c.start()

    def second(self):
        core, chip, _ = self.place()
        for c in self.across():
            c.wait_recv()
        total = self.part[4 * core + chip].astype(F32)
        for k in range(3):
            total += self.got[k].astype(F32)
        self.full[4 * core + chip] = total.astype(BF)
        for c in self.spread():
            c.start()

    def third(self):
        for c in self.spread():
            c.wait_recv()
        self.join().start()

    def finish(self):
        self.join().wait_recv()

    def close(self):
        for c in [self.halve()] + self.across() + self.spread() + [self.join()]:
            c.wait_send()


def exchange_scratch(rows, width):
    shapes = [(SEQ, rows, width), (4, rows, width), (3, rows, width), (SEQ, rows, width)]
    return [pltpu.VMEM(a, BF) for a in shapes] + [pltpu.SemaphoreType.DMA((8,)) for _ in range(4)]


def halves(block):
    low_lane = lax.broadcasted_iota(jnp.int32, block.shape, 1) < HD
    zero = jnp.zeros_like(block)
    return jnp.concatenate([jnp.where(low_lane, block, zero), jnp.where(low_lane, zero, block)], 0)


def unhalve(block):
    n = block.shape[0] // 2
    low_lane = lax.broadcasted_iota(jnp.int32, (n, block.shape[1]), 1) < HD
    return jnp.where(low_lane, block[:n], block[n:])


def norm_stats(v):
    mean = jnp.mean(v, -1, keepdims=True)
    centred = v - mean
    root = lax.rsqrt(jnp.mean(centred * centred, -1, keepdims=True) + norm_eps)
    return centred * root, root


def norm_back(grad, gain, xhat, root):
    gg = grad * gain
    return (gg - jnp.mean(gg, -1, keepdims=True) - xhat * jnp.mean(gg * xhat, -1, keepdims=True)) * root


def fold_rows(v):
    return jnp.sum(v.reshape(v.shape[0] // 8, 8, v.shape[1]), 0)


def gelu_pair(u):
    u2 = u * u
    s = 0.5 + 0.5 * jnp.tanh(u * (GELU_A + GELU_B * u2))
    a = u * s
    return a, s + a * (1.0 - s) * (2.0 * GELU_A + 6.0 * GELU_B * u2)


def places(groups):
    out = []
    for d in range(groups * SEQ):
        z, y, x, c = d // SEQ, (d // 4) % 2, (d // 2) % 2, d % 2
        out.append((((x * 2 + y) * groups + z, c), ((y * 2 + x) * groups + z, c)))
    return out


class Scatter:
    def __init__(self, src, base, bits, recv0, recv1, recv2, last, send_sem, recv_sem, send_z, recv_z):
        self.src, self.base, self.bits = src, base, bits
        self.recv, self.last = (recv0, recv1, recv2), last
        self.rows, self.lanes = last.shape[1:]
        self.send_sem, self.recv_sem, self.send_z, self.recv_z = send_sem, recv_sem, send_z, recv_z

    def mine(self, n):
        _, s = here()
        return lax.rem(lax.div(s, self.bits[n]), 2)

    def half(self, n, which):
        size = self.recv[n].shape[0]
        if n == 0:
            return self.src, self.base, which * self.lanes
        return self.recv[n - 1], which * size, 0

    def hop(self, n):
        g, s = here()
        mine, bit = self.mine(n), self.bits[n]
        src, row, lane = self.half(n, 1 - mine)
        size = self.recv[n].shape[0]
        return pltpu.make_async_remote_copy(
            src_ref=src.at[span(row, size, self.rows), span(lane, self.lanes, 128)],
            dst_ref=self.recv[n],
            send_sem=self.send_sem.at[n],
            recv_sem=self.recv_sem.at[n],
            device_id=(g, s + bit - 2 * bit * mine),
            device_id_type=MESH_ID,
        )

    def along(self):
        g, s = here()
        groups = self.last.shape[0] + 1
        out = []
        for k in range(1, groups):
            to = lax.rem(g + k, groups)
            out.append(
                pltpu.make_async_remote_copy(
                    src_ref=self.recv[2].at[span(to * self.rows, self.rows)],
                    dst_ref=self.last.at[k - 1],
                    send_sem=self.send_z.at[k - 1],
                    recv_sem=self.recv_z.at[k - 1],
                    device_id=(to, s),
                    device_id_type=MESH_ID,
                )
            )
        return out

    def start(self):
        self.hop(0).start()

    def step(self, n):
        src, row, lane = self.half(n, self.mine(n))
        self.hop(n).wait_recv()
        dst = self.recv[n]
        block = 2 * self.rows

        @pl.loop(0, dst.shape[0] // block)
        def _(i):
            to, at = span(i * block, block), span(row + i * block, block, self.rows)
            dst[to, :] = (dst[to, :].astype(F32) + src[at, span(lane, self.lanes, 128)].astype(F32)).astype(BF)

        if n < 2:
            self.hop(n + 1).start()
        else:
            for c in self.along():
                c.start()

    def total(self, out, row, column):
        for c in self.along():
            c.wait_recv()
        g, _ = here()
        total = self.recv[2][span(g * self.rows, self.rows), :].astype(F32)
        for k in range(self.last.shape[0]):
            total += self.last[k].astype(F32)
        few = self.rows // 2
        out[row : row + few, column : column + self.lanes] = total[:few]
        out[row : row + few, column + self.lanes : column + 2 * self.lanes] = total[few:]

    def close(self):
        for n in range(3):
            self.hop(n).wait_send()
        for c in self.along():
            c.wait_send()


class Vectors:
    def __init__(self, mine, recv, last, send_sem, recv_sem, send_z, recv_z):
        self.mine, self.recv, self.last = mine, recv, last
        self.sems = (send_sem, recv_sem, send_z, recv_z)

    def hop(self, n):
        g, s = here()
        bit = 1 << n
        other = s + bit - 2 * bit * lax.rem(lax.div(s, bit), 2)
        return pltpu.make_async_remote_copy(
            src_ref=self.mine.at[n],
            dst_ref=self.recv.at[n],
            send_sem=self.sems[0].at[n],
            recv_sem=self.sems[1].at[n],
            device_id=(g, other),
            device_id_type=MESH_ID,
        )

    def along(self):
        g, s = here()
        groups = self.last.shape[0] + 1
        return [
            pltpu.make_async_remote_copy(
                src_ref=self.mine.at[3],
                dst_ref=self.last.at[k - 1],
                send_sem=self.sems[2].at[k - 1],
                recv_sem=self.sems[3].at[k - 1],
                device_id=(lax.rem(g + k, groups), s),
                device_id_type=MESH_ID,
            )
            for k in range(1, groups)
        ]

    def start(self):
        self.hop(0).start()

    def step(self, n):
        self.hop(n).wait_recv()
        self.mine[n + 1] = self.mine[n] + self.recv[n]
        if n < 2:
            self.hop(n + 1).start()
        else:
            for c in self.along():
                c.start()

    def total(self):
        for c in self.along():
            c.wait_recv()
        return self.mine[3] + sum(self.last[k] for k in range(self.last.shape[0]))

    def close(self):
        for c in [self.hop(n) for n in range(3)] + self.along():
            c.wait_send()


class ProjGrad:
    def __init__(self, part, got, short, got_short, *sems):
        self.part, self.got, self.short, self.got_short, self.sems = part, got, short, got_short, sems

    def along(self):
        g, s = here()
        groups = self.part.shape[0]
        out = []
        for k in range(1, groups):
            to = lax.rem(g + k, groups)
            out.append(
                pltpu.make_async_remote_copy(
                    src_ref=self.part.at[to],
                    dst_ref=self.got.at[k - 1],
                    send_sem=self.sems[0].at[k - 1],
                    recv_sem=self.sems[1].at[k - 1],
                    device_id=(to, s),
                    device_id_type=MESH_ID,
                )
            )
        return out

    def across(self, b):
        g, s = here()
        slot = lax.rem(s - b + 2 * SEQ - 1, SEQ)
        return pltpu.make_async_remote_copy(
            src_ref=self.short.at[b],
            dst_ref=self.got_short.at[slot],
            send_sem=self.sems[2].at[b],
            recv_sem=self.sems[3].at[slot],
            device_id=(g, jnp.int32(b)),
            device_id_type=MESH_ID,
        )

    def arrived(self, slot):
        g, s = here()
        return pltpu.make_async_remote_copy(
            src_ref=self.short.at[0],
            dst_ref=self.got_short.at[slot],
            send_sem=self.sems[2].at[0],
            recv_sem=self.sems[3].at[slot],
            device_id=(g, s),
            device_id_type=MESH_ID,
        )

    def start(self):
        for c in self.along():
            c.start()

    def middle(self, out, shard):
        g, s = here()
        for c in self.along():
            c.wait_recv()
        total = self.part[g].astype(F32)
        for k in range(self.got.shape[0]):
            total += self.got[k].astype(F32)
        out[...] = total[:, 0:shard]
        for b in range(self.short.shape[0]):
            self.short[b] = total[:, (b + 1) * shard : (b + 2) * shard].astype(BF)

            @pl.when(s != b)
            def _(b=b):
                self.across(b).start()

    def finish(self, out):
        _, s = here()
        count = self.short.shape[0]

        @pl.when(s < count)
        def _():
            total = out[...] + self.short[lax.rem(s, count)].astype(F32)
            for slot in range(SEQ - 1):
                self.arrived(slot).wait_recv()
                total += self.got_short[slot].astype(F32)
            out[...] = total

    def close(self):
        _, s = here()
        for c in self.along():
            c.wait_send()
        for b in range(self.short.shape[0]):

            @pl.when(s != b)
            def _(b=b):
                self.across(b).wait_send()


def layer_kernel(slots, groups, shard, *refs):
    refs = list(refs)

    def take(n):
        out = refs[:n]
        del refs[:n]
        return out

    (long_x, short_x, long_dy, short_dy, live) = take(5)
    (wq_in, wk_in, wv_in, wo_in, up_in, down_in, proj) = take(7)
    (gain1, shift1, gain2, shift2) = (a[...].reshape(1, -1) for a in take(4))
    (long_out, short_out, long_grad, short_grad) = take(4)
    (grad_q, grad_k, grad_v, grad_o, grad_up, grad_down, grad_proj, vec_out) = take(8)
    (q_hbm, k_hbm, v_hbm, mixed_hbm, probs_hbm, sums_hbm) = take(6)
    (arena, resid, root, vec, pcols, pshort, pacc) = take(7)
    (sem_in, sem_out, sem_back) = take(3)
    exch_bufs = take(4)
    forward_exchange = Exchange(*exch_bufs, *take(2))
    backward_exchange = Exchange(*exch_bufs, *take(2))
    vectors = Vectors(*take(7))
    projected = ProjGrad(*take(8))

    g, s = here()
    short_len = short_x.shape[1]
    width = resid.shape[1]
    wide = 4 * width
    shorts = slots * short_len
    tokens = shorts + shard
    devices = groups * SEQ
    few = width // devices
    lanes = width // 2
    act, slope, up, down = 0, 4 * tokens, 8 * tokens, 8 * tokens + wide
    xs = 8 * tokens + 2 * wide
    ms, hs = xs + tokens, xs + 2 * tokens
    xhs = hs + tokens
    wo = xhs + tokens
    pack = wo + width
    pack_up = act
    q1, k1, v1, probs1, sums1 = act, act + tokens, act + 2 * tokens, act + 3 * tokens, pack
    v2 = pack_up + 4 * width
    q2 = v2 + tokens
    sums2 = q2 + tokens
    ksum = sums2 + (2 * slots + 2) * KP
    vsum = ksum + KP
    ms2 = vsum + KP
    k2 = ms2 + tokens
    probs2 = k2 + tokens
    weights = hs

    orders = ((1, 2, 4), (1, 4, 2))

    def unit(base, order):
        return Scatter(arena, base, orders[order], *take(8))

    downs = [unit(pack + n * width, n % 2) for n in range(4)]
    ups = [unit(pack_up + n * width, n % 2) for n in range(4)]
    unit_o, unit_q, unit_v, unit_k = (unit(pack + n * width, n % 2) for n in range(4))
    assert not refs

    copy = pltpu.make_async_copy
    at = lambda base, size: arena.at[pl.ds(base, size)]
    counts = {"in": 0, "out": 0, "back": 0}

    def move(kind, a, b):
        sem = {"in": sem_in, "out": sem_out, "back": sem_back}[kind]
        counts[kind] += 1
        return copy(a, b, sem.at[counts[kind] - 1])

    def rows_of(long_a, short_a, base, kind, back=False):
        pairs = [(long_a.at[0], at(base + shorts, shard))]
        pairs += [(short_a.at[i], at(base + i * short_len, short_len)) for i in range(slots)]
        return [move(kind, b, a) if back else move(kind, a, b) for a, b in pairs]

    in_x = rows_of(long_x, short_x, xs, "in")
    in_cols = move("in", proj.at[:, span(s * shard, shard)], pcols)
    in_wk = move("in", wk_in, at(weights + width, width))
    in_wv = move("in", wv_in, at(weights + 2 * width, width))
    in_wq = move("in", wq_in, at(weights, width))
    in_pshort = move("in", proj.at[:, pl.ds(0, short_len)], pshort)
    in_wo = move("in", wo_in, at(wo, width))
    in_up = [move("in", up_in.at[:, pl.ds(j * width, width)], at(up + j * width, width)) for j in range(4)]
    in_down = move("in", down_in, at(down, wide))
    for c in [in_x[0], in_wk, in_wv, in_cols] + in_x[1:] + [in_wq, in_pshort, in_wo] + in_up + [in_down]:
        c.start()
    greet(seq_peers() + grp_peers(groups))

    part, full = forward_exchange.part, forward_exchange.full
    blocks = KP // SEQ
    in_x[0].wait()
    in_wk.wait()
    arena[pl.ds(k1 + shorts, shard), :] = mm(arena[pl.ds(xs + shorts, shard), :], arena[pl.ds(weights + width, width), :]).astype(BF)
    in_wv.wait()
    arena[pl.ds(v1 + shorts, shard), :] = mm(arena[pl.ds(xs + shorts, shard), :], arena[pl.ds(weights + 2 * width, width), :]).astype(BF)
    in_cols.wait()
    part[:, :, 0:width] = mm(pcols[...], arena[pl.ds(k1 + shorts, shard), :]).astype(BF).reshape(SEQ, blocks, width)
    part[:, :, width:] = mm(pcols[...], arena[pl.ds(v1 + shorts, shard), :]).astype(BF).reshape(SEQ, blocks, width)
    forward_exchange.start()
    for c in in_x[1:]:
        c.wait()
    arena[pl.ds(k1, shorts), :] = mm(arena[pl.ds(xs, shorts), :], arena[pl.ds(weights + width, width), :]).astype(BF)
    arena[pl.ds(v1, shorts), :] = mm(arena[pl.ds(xs, shorts), :], arena[pl.ds(weights + 2 * width, width), :]).astype(BF)
    out_k = move("out", at(k1, tokens), k_hbm)
    out_v = move("out", at(v1, tokens), v_hbm)
    out_k.start()
    out_v.start()
    forward_exchange.first()
    in_wq.wait()
    arena[pl.ds(q1, tokens), :] = (0.125 * mm(arena[pl.ds(xs, tokens), :], arena[pl.ds(weights, width), :])).astype(BF)
    out_q = move("out", at(q1, tokens), q_hbm)
    out_q.start()
    in_pshort.wait()
    for i in range(slots):
        arena[pl.ds(sums1 + 2 * i * KP, KP), :] = mm(pshort[...], arena[pl.ds(k1 + i * short_len, short_len), :]).astype(BF)
        arena[pl.ds(sums1 + (2 * i + 1) * KP, KP), :] = mm(pshort[...], arena[pl.ds(v1 + i * short_len, short_len), :]).astype(BF)
    forward_exchange.second()

    heads = width // HD
    item_rows = heads * short_len // width * KP

    def head(h, size):
        beside = width // size
        return h // beside * KP, slice(h % beside * size, (h % beside + 1) * size)

    def staged(before, between, after):
        now, last = before(0), None
        for pair in range(heads // 2):
            ahead = before(pair + 1) if pair + 1 < heads // 2 else None
            middle = between(pair, *now)
            if last is not None:
                after(pair - 1, last)
            now, last = ahead, middle
        after(heads // 2 - 1, last)

    def lanes_of(pair):
        return slice(pair * 2 * HD, (pair + 1) * 2 * HD)

    def attend(row, size, sums, probs):
        def scores(pair):
            q = arena[span(q1 + row, size, 128), lanes_of(pair)]
            return (mm(halves(arena[span(sums, KP), lanes_of(pair)]), q, 1, 1),)

        def softmax(pair, sc):
            parts = []
            for h in range(2):
                part = sc[h * KP : (h + 1) * KP]
                e = jnp.exp(part - jnp.max(part, 0, keepdims=True))
                parts.append((e * (1.0 / jnp.sum(e, 0, keepdims=True))).astype(BF))
                first, cols = head(2 * pair + h, size)
                arena[span(probs + first, KP, 128), cols] = parts[h]
            return jnp.concatenate(parts, 0)

        def mix(pair, p):
            out = mm(halves(arena[span(sums + KP, KP), lanes_of(pair)]), p, 0, 0)
            arena[span(ms + row, size, 128), lanes_of(pair)] = out.T.astype(BF)

        staged(scores, softmax, mix)

    @pl.loop(0, slots)
    def _(i):
        attend(i * short_len, short_len, sums1 + 2 * i * KP, probs1 + i * item_rows)

    long_probs = probs1 + slots * item_rows
    out_probs = [move("out", at(probs1, slots * item_rows), probs_hbm.at[pl.ds(0, slots * item_rows)])]
    out_probs[0].start()
    forward_exchange.third()
    forward_exchange.finish()
    long_sums = sums1 + 2 * slots * KP
    arena[pl.ds(long_sums, KP), :] = full[:, :, 0:width].reshape(KP, width)
    arena[pl.ds(long_sums + KP, KP), :] = full[:, :, width:].reshape(KP, width)
    attend(shorts, shard, long_sums, long_probs)
    long_size = heads * shard // width * KP
    out_probs += [move("out", at(long_probs, long_size), probs_hbm.at[pl.ds(slots * item_rows, long_size)])]
    out_sums = move("out", at(sums1, (2 * slots + 2) * KP), sums_hbm)
    out_mixed = move("out", at(ms, tokens), mixed_hbm)
    for c in out_probs[1:] + [out_sums, out_mixed]:
        c.start()

    in_wo.wait()
    block = tokens // 3

    @pl.loop(0, 3)
    def _(i):
        r = span(i * block, block)
        x = arena[span(xs + i * block, block, 128), :].astype(F32)
        xh, rs = norm_stats(mm(arena[span(ms + i * block, block, 128), :], arena[pl.ds(wo, width), :]) + x)
        arena[span(xhs + i * block, block, 128), :] = xh.astype(BF)
        root[r, :] = jnp.broadcast_to(rs, (block, 128))
        hidden = xh * gain1 + shift1
        resid[r, :] = hidden
        arena[span(hs + i * block, block, 128), :] = hidden.astype(BF)

    in_dy = rows_of(long_dy, short_dy, xs, "in")
    for c in in_dy:
        c.start()
    for c in [out_k, out_v, out_q, out_mixed] + out_probs:
        c.wait()
    for c in in_up + [in_down]:
        c.wait()

    part_rows = tokens // 2

    @pl.loop(0, 8)
    def _(i):
        j, r = lax.div(i, 2), lax.rem(i, 2) * part_rows
        hidden = arena[span(hs + r, part_rows, 64), :]
        a, slope_j = gelu_pair(mm(hidden, arena[span(up + j * width, width, 128), :]))
        a = a.astype(BF)
        arena[span(act + j * tokens + r, part_rows, 64), :] = a
        arena[span(slope + j * tokens + r, part_rows, 64), :] = slope_j.astype(BF)
        resid[span(r, part_rows), :] += mm(a, arena[span(down + j * width, width, 128), :])

    vec[...] = jnp.zeros_like(vec)
    for c in in_dy:
        c.wait()
    rb = 128

    @pl.loop(0, tokens // rb)
    def _(i):
        r = span(i * rb, rb)
        rx = span(xs + i * rb, rb, 128)
        alive = jnp.where(lax.div(i * rb, short_len) < live[0], 1.0, 0.0).astype(F32)
        alive = jnp.where(i * rb >= shorts, 1.0, alive)
        xh, rs = norm_stats(resid[r, :])
        top = alive * arena[rx, :].astype(F32)
        vec[16:24, :] += fold_rows(top * xh)
        vec[24:32, :] += fold_rows(top)
        arena[rx, :] = (alive * (xh * gain2 + shift2)).astype(BF)
        dx = norm_back(top, gain2, xh, rs)
        resid[r, :] = dx
        arena[span(ms + i * rb, rb, 128), :] = dx.astype(BF)

    outs = rows_of(long_out, short_out, xs, "out", back=True)
    for c in outs:
        c.start()
    out_sums.wait()
    place = places(groups)

    def packed(base, order, value, step, first):
        for d in range(value.shape[0] // step):
            row, core = place[d][order]
            rows = slice(d * step + first, d * step + first + few)
            arena[span(base + row * 2 * few, 2 * few), core * lanes : (core + 1) * lanes] = jnp.concatenate(
                [value[rows, :lanes], value[rows, lanes:]], 0
            ).astype(BF)

    @pl.loop(0, groups)
    def _(j):
        value = mm(arena[span(act + j * tokens, tokens, 128), :], arena[pl.ds(ms, tokens), :], 0, 0)
        for n in range(4):
            packed(pack + n * width + j * 2 * few, n % 2, value, 4 * few, n * few)

    for piece in downs:
        piece.start()
    low = arena.at[pl.ds(ms, tokens)]

    @pl.loop(0, 8)
    def _(i):
        j, r = lax.div(i, 2), lax.rem(i, 2) * part_rows
        rj = span(slope + j * tokens + r, part_rows, 64)
        gb = low[span(r, part_rows), :]
        gu = mm(gb, arena[span(down + j * width, width, 128), :], 1, 1) * arena[rj, :].astype(F32)
        gu = gu.astype(BF)
        arena[rj, :] = gu
        resid[span(r, part_rows), :] += mm(gu, arena[span(up + j * width, width, 128), :], 1, 1)

        @pl.when(i == 2)
        def _():
            for piece in downs:
                piece.step(0)

        @pl.when(i == 6)
        def _():
            for piece in downs[:2]:
                piece.step(1)

    back = {}

    def load(name, a, b):
        back[name] = move("back", a, b)
        back[name].start()

    load("probs", probs_hbm, at(probs2, 4 * tokens))
    load("k", k_hbm, at(k2, tokens))
    load("v", v_hbm, at(v2, tokens))

    for piece in downs[2:]:
        piece.step(1)

    @pl.loop(0, 2)
    def _(m):
        for n in range(2):
            j = 2 * m + n
            gu = arena[span(slope + j * tokens, tokens, 128), :]
            packed(pack_up + j * width, n, mm(arena[pl.ds(hs, tokens), :], gu, 0, 0), few, 0)

        @pl.when(m == 0)
        def _():
            for piece in ups[:2]:
                piece.start()
            for piece in downs[:2]:
                piece.step(2)

        @pl.when(m == 1)
        def _():
            for piece in ups[2:]:
                piece.start()
            for piece in ups[:2]:
                piece.step(0)

    load("q", q_hbm, at(q2, tokens))
    load("mixed", mixed_hbm, at(ms2, tokens))
    load("sums", sums_hbm, at(sums2, (2 * slots + 2) * KP))

    @pl.loop(0, tokens // rb)
    def _(i):
        r = span(i * rb, rb)
        gh = resid[r, :]
        xh = arena[span(xhs + i * rb, rb, 128), :].astype(F32)
        vec[0:8, :] += fold_rows(gh * xh)
        vec[8:16, :] += fold_rows(gh)
        dx = norm_back(gh, gain1, xh, root[r, 0:1])
        resid[r, :] = dx
        low[r, :] = dx.astype(BF)

    load("wq", wq_in, at(weights, width))
    load("wk", wk_in, at(weights + width, width))
    load("wv", wv_in, at(weights + 2 * width, width))
    four = jnp.sum(vec[...].reshape(4, 8, width), 1)
    vectors.mine[0] = jnp.concatenate([four, jnp.zeros_like(four)], 0)
    vectors.start()
    for c in outs:
        c.wait()
    arena[pl.ds(xs, tokens), :] = mm(low[...], arena[pl.ds(wo, width), :], 1, 1).astype(BF)
    for piece in ups[2:]:
        piece.step(0)
    for piece in downs[2:]:
        piece.step(2)
    for piece in downs:
        piece.hop(0).wait_send()
    back["mixed"].wait()
    packed(pack, 0, mm(arena[pl.ds(ms2, tokens), :], low[...], 0, 0), few, 0)
    unit_o.start()
    for n, c in enumerate(rows_of(long_x, short_x, ms2, "back")):
        back["x", n] = c
        c.start()

    def attend_back(row, size, sums, probs, put_key, put_value):
        def front(pair):
            gm = arena[span(xs + row, size, 128), lanes_of(pair)]
            p = []
            for h in range(2):
                first, cols = head(2 * pair + h, size)
                p.append(arena[span(probs + first, KP, 128), cols])
            gp = mm(halves(arena[span(sums + KP, KP), lanes_of(pair)]), gm, 1, 1)
            put_value(lanes_of(pair), unhalve(mm(jnp.concatenate(p, 0), gm)).astype(BF))
            return gp, p

        def middle(pair, gp, p):
            parts = []
            for h in range(2):
                ph = p[h].astype(F32)
                t = ph * gp[h * KP : (h + 1) * KP]
                parts.append((t - ph * jnp.sum(t, 0, keepdims=True)).astype(BF))
            return jnp.concatenate(parts, 0)

        def rear(pair, gs):
            rows = span(q2 + row, size, 128)
            put_key(lanes_of(pair), unhalve(mm(gs, arena[rows, lanes_of(pair)])).astype(BF))
            gq = mm(halves(arena[span(sums, KP), lanes_of(pair)]), gs, 0, 0).T.astype(BF).astype(F32)
            arena[rows, lanes_of(pair)] = (gq * 0.125).astype(BF)

        staged(front, middle, rear)

    def put_long(first):
        def put(lanes, value):
            part[:, :, lanes.start + first : lanes.stop + first] = value.reshape(SEQ, blocks, 2 * HD)

        return put

    def put_short(base):
        def put(lanes, value):
            arena[pl.ds(base, KP), lanes] = value

        return put

    for name in ("q", "sums", "probs"):
        back[name].wait()
    forward_exchange.close()
    attend_back(shorts, shard, sums2 + 2 * slots * KP, probs2 + slots * item_rows, put_long(0), put_long(width))
    backward_exchange.start()
    unit_o.step(0)
    vectors.step(0)
    back["k"].wait()
    back["v"].wait()
    pacc[...] = jnp.zeros_like(pacc)

    def columns(cols, row, size):
        rk, rv = span(k2 + row, size, 128), span(v2 + row, size, 128)
        gk, gv = arena[pl.ds(ksum, KP), :], arena[pl.ds(vsum, KP), :]
        grad = mm(gk, arena[rk, :], 1, 1) + mm(gv, arena[rv, :], 1, 1)
        arena[rk, :] = mm(cols[...], gk, 0, 0).astype(BF)
        arena[rv, :] = mm(cols[...], gv, 0, 0).astype(BF)
        return grad

    @pl.loop(0, slots)
    def _(i):
        attend_back(i * short_len, short_len, sums2 + 2 * i * KP, probs2 + i * item_rows, put_short(ksum), put_short(vsum))
        pacc[...] += columns(pshort, i * short_len, short_len)

        @pl.when(i == 0)
        def _():
            backward_exchange.first()
            vectors.step(1)
            for piece in ups[:2]:
                piece.step(1)

        @pl.when(i == 1)
        def _():
            vectors.step(2)
            for piece in ups[2:]:
                piece.step(1)

        @pl.when(i == 2)
        def _():
            backward_exchange.second()
            unit_o.step(1)
            for piece in ups[:2]:
                piece.step(2)

        @pl.when(i == slots - 1)
        def _():
            backward_exchange.third()
            for piece in ups[2:]:
                piece.step(2)

    for n in range(1 + slots):
        back["x", n].wait()
    x2 = arena.at[pl.ds(ms2, tokens)]
    gq, gk, gv = (arena.at[pl.ds(a, tokens)] for a in (q2, k2, v2))

    packed(pack + width, 1, mm(x2[...], gq[...], 0, 0), few, 0)
    unit_q.start()
    backward_exchange.finish()
    arena[pl.ds(ksum, KP), :] = full[:, :, 0:width].reshape(KP, width)
    arena[pl.ds(vsum, KP), :] = full[:, :, width:].reshape(KP, width)
    long_cols = columns(pcols, shorts, shard)
    prow = KP // groups
    projected.part[:, :, 0:shard] = long_cols.astype(BF).reshape(groups, prow, shard)
    projected.part[:, :, shard:] = pacc[...].astype(BF).reshape(groups, prow, short_len)
    projected.start()
    packed(pack + 2 * width, 0, mm(x2[...], gv[...], 0, 0), few, 0)
    unit_v.start()
    unit_q.step(0)
    packed(pack + 3 * width, 1, mm(x2[...], gk[...], 0, 0), few, 0)
    unit_k.start()
    unit_v.step(0)
    for name in ("wq", "wk", "wv"):
        back[name].wait()
    for i in range(3):
        r = pl.ds(i * block, block)
        dx = resid[r, :]
        for n, grad in enumerate((gq, gk, gv)):
            dx += mm(grad[r, :], arena[pl.ds(weights + n * width, width), :], 1, 1)
        arena[pl.ds(xs + i * block, block), :] = dx.astype(BF)
        if i == 0:
            unit_k.step(0)
        if i == 1:
            unit_o.step(2)
    outs = rows_of(long_grad, short_grad, xs, "out", back=True)
    for c in outs:
        c.start()
    unit_q.step(1)
    for n, piece in enumerate(downs):
        piece.total(grad_down, n * few, 0)
    unit_v.step(1)
    unit_k.step(1)
    for n, piece in enumerate(ups):
        piece.total(grad_up, 0, n * width)
    projected.middle(grad_proj, shard)
    vec_out[...] = vectors.total()
    unit_q.step(2)
    unit_o.total(grad_o, 0, 0)
    unit_v.step(2)
    unit_k.step(2)
    projected.finish(grad_proj)
    unit_q.total(grad_q, 0, 0)
    unit_v.total(grad_v, 0, 0)
    unit_k.total(grad_k, 0, 0)
    for c in outs:
        c.wait()
    for piece in downs:
        for n in range(1, 3):
            piece.hop(n).wait_send()
        for c in piece.along():
            c.wait_send()
    for piece in ups + [unit_o, unit_q, unit_v, unit_k, vectors, projected, backward_exchange]:
        piece.close()


def fast_shards(groups, *args):
    (long_x, short_x, long_dy, short_dy, live, wq, wk, wv, wo, up, down, proj, g1, b1, g2, b2) = args
    slots, short_len, width = short_x.shape
    shard = long_x.shape[1]
    tokens = slots * short_len + shard
    wide = up.shape[1]
    devices = groups * SEQ
    few = width // devices
    sds = jax.ShapeDtypeStruct
    anyspace = pl.BlockSpec(memory_space=pl.ANY)
    vmem = pl.BlockSpec(memory_space=pltpu.VMEM)
    dma = pltpu.SemaphoreType.DMA
    prow = KP // groups
    out_shapes = [sds(a.shape, BF) for a in (long_x, short_x, long_x, short_x)]
    grads = [(few, width)] * 4 + [(few, wide), (4 * few, width), (prow, shard), (8, width)]
    out_shapes += [sds(a, F32) for a in grads]
    row = (tokens, width)
    out_shapes += [sds(a, BF) for a in [row] * 4 + [(4 * tokens, width), ((2 * slots + 2) * KP, width)]]
    arena = 12 * tokens + 2 * wide + width + 4 * width
    heads = short_len // shard
    scratch = [
        pltpu.VMEM((arena, width), BF),
        pltpu.VMEM(row, F32),
        pltpu.VMEM((tokens, 128), F32),
        pltpu.VMEM((32, width), F32),
        pltpu.VMEM((KP, shard), BF),
        pltpu.VMEM((KP, short_len), BF),
        pltpu.VMEM((KP, short_len), F32),
        dma((12 + 2 * (1 + slots),)),
        dma((13 + 2 * (1 + slots),)),
        dma((12 + 1 + slots,)),
    ]
    scratch += exchange_scratch(KP // SEQ, 2 * width)
    along = [dma((groups - 1,)), dma((groups - 1,))]
    scratch += [pltpu.VMEM((n, 8, width), F32) for n in (4, 3, groups - 1)] + [dma((3,)), dma((3,))] + along
    scratch += [pltpu.VMEM((n, prow, shard + short_len), BF) for n in (groups, groups - 1)]
    scratch += [pltpu.VMEM((n, prow, shard), BF) for n in (heads, SEQ - 1)]
    scratch += along + [dma((heads,)), dma((SEQ - 1,))]
    lanes = width // 2
    unit = [pltpu.VMEM((width // n, lanes), BF) for n in (1, 2, 4)]
    unit += [pltpu.VMEM((groups - 1, 2 * few, lanes), BF), dma((3,)), dma((3,))] + along
    scratch += unit * 12
    outs = pl.pallas_call(
        functools.partial(layer_kernel, slots, groups, shard),
        name="encoder_layer",
        out_shape=out_shapes,
        in_specs=[anyspace] * 4 + [pl.BlockSpec(memory_space=pltpu.SMEM)] + [anyspace] * 7 + [vmem] * 4,
        out_specs=[anyspace] * 4 + [vmem] * 8 + [anyspace] * 6,
        scratch_shapes=scratch,
        compiler_params=pltpu.CompilerParams(
            collective_id=0, has_side_effects=True, vmem_limit_bytes=VMEM_BYTES
        ),
    )(long_x, short_x, long_dy, short_dy, live, wq, wk, wv, wo, up, down, proj, g1, b1, g2, b2)
    return emit_call(outs[:12], few)


def emit_kernel(*refs):
    *ins, vec = refs[:12]
    outs, vectors, stages = refs[12:23], refs[23:27], refs[27:38]
    sem_in, sem_out = refs[38:]
    reads = [pltpu.make_async_copy(a, b, sem_in.at[n]) for n, (a, b) in enumerate(zip(ins, stages))]
    writes = [pltpu.make_async_copy(a, b, sem_out.at[n]) for n, (a, b) in enumerate(zip(stages, outs))]
    for c in reads:
        c.start()
    g, s = here()
    width = vec.shape[1]
    few = vectors[0].shape[0]
    mine = pltpu.roll(vec[...], width - (g * SEQ + s) * few, 1)
    for n in range(4):
        vectors[n][...] = mine[n, 0:few]
    for a, b in zip(reads, writes):
        a.wait()
        b.start()
    for c in writes:
        c.wait()


def emit_call(arrays, few):
    anyspace = pl.BlockSpec(memory_space=pl.ANY)
    vmem = pl.BlockSpec(memory_space=pltpu.VMEM)
    return pl.pallas_call(
        emit_kernel,
        name="emit",
        out_shape=[jax.ShapeDtypeStruct(a.shape, a.dtype) for a in arrays[:11]] + [jax.ShapeDtypeStruct((few,), F32)] * 4,
        in_specs=[anyspace] * 11 + [vmem],
        out_specs=[anyspace] * 11 + [vmem] * 4,
        scratch_shapes=[pltpu.VMEM(a.shape, a.dtype) for a in arrays[:11]] + [pltpu.SemaphoreType.DMA((11,))] * 2,
        compiler_params=pltpu.CompilerParams(vmem_limit_bytes=VMEM_BYTES),
    )(*arrays)


def fits(mesh, args):
    long_x, width, wide = args[0], args[0].shape[2], args[9].shape[1]
    devices = mesh.shape["grp"] * mesh.shape["seq"]
    whole = width % (devices * 8) == 0 and wide == 4 * width
    return mesh.shape["seq"] == SEQ and whole and long_x.shape[0] == 1


def solution(mesh):
    placed = (
        P("grp", "seq", None),
        P(("grp", "seq"), None, None),
        P("grp", "seq", None),
        P(("grp", "seq"), None, None),
        P(("grp", "seq")),
        P(),
        P(),
        P(),
        P(),
        P(),
        P(),
        P(),
        P(),
        P(),
        P(),
        P(),
    )
    groups = mesh.shape["grp"]

    def body(*args):
        if fits(mesh, args):
            return fast_shards(groups, *args)
        return shards(*args)

    return jax.shard_map(
        body,
        mesh=mesh,
        in_specs=placed,
        out_specs=(
            P("grp", "seq", None),
            P(("grp", "seq"), None, None),
            P("grp", "seq", None),
            P(("grp", "seq"), None, None),
            P(("grp", "seq"), None),
            P(("grp", "seq"), None),
            P(("grp", "seq"), None),
            P(("grp", "seq"), None),
            P(("grp", "seq"), None),
            P(("grp", "seq"), None),
            P("grp", "seq"),
            P(("grp", "seq")),
            P(("grp", "seq")),
            P(("grp", "seq")),
            P(("grp", "seq")),
        ),
        check_vma=False,
    )
```

```python
import functools

import jax
import jax.numpy as jnp
from jax import lax
from jax.experimental import pallas as pl
from jax.experimental.pallas import tpu as pltpu
from jax.sharding import PartitionSpec as P

HD = 64
KP = 256


norm_eps = 1e-05


def shortened(shard):
    return jax.tree.map(lambda a: a.astype(jnp.bfloat16) if a.dtype == jnp.float32 else a, shard)


def norm_rows(resid, gain_vec, shift_vec):
    row_mean = jnp.mean(resid, axis=-1, keepdims=True)
    centred = resid - row_mean
    variance = jnp.mean(centred * centred, axis=-1, keepdims=True)
    return centred * lax.rsqrt(variance + norm_eps) * gain_vec + shift_vec


def smooth_gate(upward):
    return jax.nn.gelu(upward, approximate=True)


def same_sums(partials):
    return partials


def layer_pass(sequences, cotangent, live_rows, proj_cols, fold_summaries, fold_grads, params):
    (
        query_w,
        key_w,
        value_w,
        out_w,
        up_w,
        down_w,
        gain_first,
        shift_first,
        gain_second,
        shift_second,
    ) = params
    seq_count, length, model_width = sequences.shape
    head_count = model_width // HD
    wide = jnp.float32
    narrow = jnp.bfloat16
    queries = (
        0.125 * jnp.einsum("nld,de->nle", sequences, query_w, preferred_element_type=wide)
    ).astype(narrow)
    key_vecs = jnp.einsum("nld,de->nle", sequences, key_w, preferred_element_type=wide).astype(
        narrow
    )
    value_vecs = jnp.einsum("nld,de->nle", sequences, value_w, preferred_element_type=wide).astype(
        narrow
    )
    key_part = jnp.einsum("kl,nld->nkd", proj_cols, key_vecs, preferred_element_type=wide)
    value_part = jnp.einsum("kl,nld->nkd", proj_cols, value_vecs, preferred_element_type=wide)
    key_sum, value_sum = fold_summaries((key_part, value_part))
    key_heads = key_sum.astype(narrow).reshape(seq_count, KP, head_count, HD)
    value_heads = value_sum.astype(narrow).reshape(seq_count, KP, head_count, HD)
    query_heads = queries.reshape(seq_count, length, head_count, HD)
    scores = jnp.einsum("nlhe,nkhe->nhlk", query_heads, key_heads, preferred_element_type=wide)
    attn_probs = jax.nn.softmax(scores, axis=-1)
    probs_low = attn_probs.astype(narrow)
    mixed_heads = (
        jnp.einsum("nhlk,nkhe->nlhe", probs_low, value_heads, preferred_element_type=wide)
        .reshape(seq_count, length, model_width)
        .astype(narrow)
    )
    attn_out = jnp.einsum("nld,de->nle", mixed_heads, out_w, preferred_element_type=wide)
    hidden, first_back = jax.vjp(
        norm_rows, sequences.astype(wide) + attn_out, gain_first, shift_first
    )
    hidden_low = hidden.astype(narrow)
    upward = jnp.einsum("nld,df->nlf", hidden_low, up_w, preferred_element_type=wide)
    activated, gate_back = jax.vjp(smooth_gate, upward)
    activated_low = activated.astype(narrow)
    branch = jnp.einsum("nlf,fd->nld", activated_low, down_w, preferred_element_type=wide)
    normed, second_back = jax.vjp(norm_rows, hidden + branch, gain_second, shift_second)
    result = normed * live_rows[:, None, None]
    grad_top = cotangent.astype(wide) * live_rows[:, None, None]
    grad_resid_two, grad_gain_two, grad_shift_two = second_back(grad_top)
    grad_branch = grad_resid_two.astype(narrow)
    grad_down = jnp.einsum("nlf,nld->fd", activated_low, grad_branch, preferred_element_type=wide)
    grad_activated = jnp.einsum("nld,fd->nlf", grad_branch, down_w, preferred_element_type=wide)
    (grad_upward,) = gate_back(grad_activated)
    grad_upward_low = grad_upward.astype(narrow)
    grad_up = jnp.einsum("nld,nlf->df", hidden_low, grad_upward_low, preferred_element_type=wide)
    grad_hidden = grad_resid_two + jnp.einsum(
        "nlf,df->nld", grad_upward_low, up_w, preferred_element_type=wide
    )
    grad_resid_one, grad_gain_one, grad_shift_one = first_back(grad_hidden)
    grad_attn = grad_resid_one.astype(narrow)
    grad_out = jnp.einsum("nld,nle->de", mixed_heads, grad_attn, preferred_element_type=wide)
    grad_mixed = (
        jnp.einsum("nle,de->nld", grad_attn, out_w, preferred_element_type=wide)
        .astype(narrow)
        .reshape(seq_count, length, head_count, HD)
    )
    grad_probs = jnp.einsum("nlhe,nkhe->nhlk", grad_mixed, value_heads, preferred_element_type=wide)
    value_grad_part = jnp.einsum(
        "nhlk,nlhe->nkhe", probs_low, grad_mixed, preferred_element_type=wide
    ).reshape(seq_count, KP, model_width)
    grad_scores = attn_probs * (
        grad_probs - jnp.sum(grad_probs * attn_probs, axis=-1, keepdims=True)
    )
    scores_low = grad_scores.astype(narrow)
    grad_queries = (
        jnp.einsum("nhlk,nkhe->nlhe", scores_low, key_heads, preferred_element_type=wide).astype(
            narrow
        )
        * 0.125
    ).reshape(seq_count, length, model_width)
    key_grad_part = jnp.einsum(
        "nhlk,nlhe->nkhe", scores_low, query_heads, preferred_element_type=wide
    ).reshape(seq_count, KP, model_width)
    key_grad_sum, value_grad_sum = fold_grads((key_grad_part, value_grad_part))
    key_grad_low = key_grad_sum.astype(narrow)
    value_grad_low = value_grad_sum.astype(narrow)
    grad_keys = jnp.einsum(
        "kl,nkd->nld", proj_cols, key_grad_low, preferred_element_type=wide
    ).astype(narrow)
    grad_values = jnp.einsum(
        "kl,nkd->nld", proj_cols, value_grad_low, preferred_element_type=wide
    ).astype(narrow)
    grad_cols = jnp.einsum(
        "nkd,nld->kl", key_grad_low, key_vecs, preferred_element_type=wide
    ) + jnp.einsum("nkd,nld->kl", value_grad_low, value_vecs, preferred_element_type=wide)
    grad_query = jnp.einsum("nld,nle->de", sequences, grad_queries, preferred_element_type=wide)
    grad_key = jnp.einsum("nld,nle->de", sequences, grad_keys, preferred_element_type=wide)
    grad_value = jnp.einsum("nld,nle->de", sequences, grad_values, preferred_element_type=wide)
    grad_sequences = grad_resid_one + jnp.einsum(
        "nle,de->nld", grad_queries, query_w, preferred_element_type=wide
    )
    grad_sequences = grad_sequences + jnp.einsum(
        "nle,de->nld", grad_keys, key_w, preferred_element_type=wide
    )
    grad_sequences = grad_sequences + jnp.einsum(
        "nle,de->nld", grad_values, value_w, preferred_element_type=wide
    )
    weight_grads = (
        grad_query,
        grad_key,
        grad_value,
        grad_out,
        grad_up,
        grad_down,
        grad_gain_one,
        grad_shift_one,
        grad_gain_two,
        grad_shift_two,
    )
    return (result, grad_sequences, weight_grads, grad_cols)


def shards(
    long_x,
    short_x,
    long_dy,
    short_dy,
    short_live,
    query_weight,
    key_weight,
    value_weight,
    out_weight,
    up_weight,
    down_weight,
    length_proj,
    gain_one,
    shift_one,
    gain_two,
    shift_two,
):
    params = (
        query_weight,
        key_weight,
        value_weight,
        out_weight,
        up_weight,
        down_weight,
        gain_one,
        shift_one,
        gain_two,
        shift_two,
    )
    shard_len = long_x.shape[1]
    slot_count = short_x.shape[0]
    short_len = short_x.shape[1]
    shard_start = lax.axis_index("seq") * shard_len
    long_cols = lax.dynamic_slice_in_dim(length_proj, shard_start, shard_len, 1)

    def sum_summaries(partials):
        return jax.tree.map(
            lambda part: part.astype(jnp.float32), lax.psum(shortened(partials), "seq")
        )

    def sum_summary_grads(partials):
        return jax.tree.map(
            lambda part: part.astype(jnp.float32), lax.psum(shortened(partials), "seq")
        )

    long_live = jnp.ones((long_x.shape[0],), jnp.float32)
    long_result, long_back, long_weights, long_proj = layer_pass(
        long_x, long_dy, long_live, long_cols, sum_summaries, sum_summary_grads, params
    )
    short_mask = (jnp.arange(slot_count) < short_live[0]).astype(jnp.float32)
    short_result, short_back, short_weights, short_proj = layer_pass(
        short_x, short_dy, short_mask, length_proj[:, :short_len], same_sums, same_sums, params
    )
    summed = jax.tree.map(jnp.add, long_weights, short_weights)
    (
        grad_query,
        grad_key,
        grad_value,
        grad_out,
        grad_up,
        grad_down,
        grad_gain_one,
        grad_shift_one,
        grad_gain_two,
        grad_shift_two,
    ) = summed
    proj_total = jnp.zeros(length_proj.shape, jnp.float32)
    proj_total = lax.dynamic_update_slice_in_dim(proj_total, long_proj, shard_start, 1)
    proj_total = proj_total.at[:, :short_len].add(short_proj)
    proj_rows = lax.psum_scatter(
        proj_total.astype(jnp.bfloat16), "grp", scatter_dimension=0, tiled=True
    )
    proj_part = lax.psum_scatter(proj_rows, "seq", scatter_dimension=1, tiled=True).astype(
        jnp.float32
    )
    reduced = (
        lax.psum_scatter(grad_query, ("grp", "seq"), scatter_dimension=0, tiled=True),
        lax.psum_scatter(grad_key, ("grp", "seq"), scatter_dimension=0, tiled=True),
        lax.psum_scatter(grad_value, ("grp", "seq"), scatter_dimension=0, tiled=True),
        lax.psum_scatter(grad_out, ("grp", "seq"), scatter_dimension=0, tiled=True),
        lax.psum_scatter(grad_up, ("grp", "seq"), scatter_dimension=0, tiled=True),
        lax.psum_scatter(grad_down, ("grp", "seq"), scatter_dimension=0, tiled=True),
        lax.psum_scatter(grad_gain_one, ("grp", "seq"), scatter_dimension=0, tiled=True),
        lax.psum_scatter(grad_shift_one, ("grp", "seq"), scatter_dimension=0, tiled=True),
        lax.psum_scatter(grad_gain_two, ("grp", "seq"), scatter_dimension=0, tiled=True),
        lax.psum_scatter(grad_shift_two, ("grp", "seq"), scatter_dimension=0, tiled=True),
    )
    reduced = tuple(reduced)
    return (
        (
            long_result.astype(jnp.bfloat16),
            short_result.astype(jnp.bfloat16),
            long_back.astype(jnp.bfloat16),
            short_back.astype(jnp.bfloat16),
        )
        + reduced[:6]
        + (proj_part,)
        + reduced[6:]
    )


MESH_ID = pl.DeviceIdType.MESH
BF = jnp.bfloat16
F32 = jnp.float32
VMEM_BYTES = 65400 * 1024
GELU_A = 0.7978845608028654
GELU_B = 0.044715 * GELU_A
SEQ = 8


def mm(a, b, ca=1, cb=0):
    return lax.dot_general(a, b, (((ca,), (cb,)), ((), ())), preferred_element_type=F32)


def span(start, size, step=None):
    return pl.ds(pl.multiple_of(start, step or size), size)


def here():
    return lax.axis_index("grp"), lax.axis_index("seq")


def greet(peers):
    barrier = pltpu.get_barrier_semaphore()
    for peer in peers:
        pl.semaphore_signal(barrier, inc=1, device_id=peer, device_id_type=MESH_ID)
    pl.semaphore_wait(barrier, len(peers))


def seq_peers():
    g, s = here()
    return [(g, lax.rem(s + k, SEQ)) for k in range(1, SEQ)]


def grp_peers(groups):
    g, s = here()
    return [(lax.rem(g + k, groups), s) for k in range(1, groups)]


class Exchange:
    def __init__(self, part, got_core, got, full, send_sem, recv_sem):
        self.part, self.got_core, self.got, self.full = part, got_core, got, full
        self.send_sem, self.recv_sem = send_sem, recv_sem

    def place(self):
        _, s = here()
        core, chip = lax.rem(s, 2), lax.div(s, 2)
        x, y = 1 - 2 * lax.rem(chip, 2), 2 - 4 * lax.div(chip, 2)
        return core, chip, (chip + x, chip + y, chip + x + y)

    def send(self, n, src, dst, to):
        g, _ = here()
        return pltpu.make_async_remote_copy(
            src_ref=src,
            dst_ref=dst,
            send_sem=self.send_sem.at[n],
            recv_sem=self.recv_sem.at[n],
            device_id=(g, to),
            device_id_type=MESH_ID,
        )

    def halve(self):
        core, chip, _ = self.place()
        return self.send(0, self.part.at[pl.ds(4 * (1 - core), 4)], self.got_core, 2 * chip + 1 - core)

    def across(self):
        core, _, chips = self.place()
        return [
            self.send(1 + k, self.part.at[4 * core + to], self.got.at[k], 2 * to + core) for k, to in enumerate(chips)
        ]

    def spread(self):
        core, chip, chips = self.place()
        own = self.full.at[4 * core + chip]
        return [self.send(4 + k, own, own, 2 * to + core) for k, to in enumerate(chips)]

    def join(self):
        core, chip, _ = self.place()
        own = self.full.at[pl.ds(4 * core, 4)]
        return self.send(7, own, own, 2 * chip + 1 - core)

    def start(self):
        self.halve().start()

    def first(self):
        core, _, _ = self.place()
        self.halve().wait_recv()
        for n in range(4):
            self.part[4 * core + n] = (self.part[4 * core + n].astype(F32) + self.got_core[n].astype(F32)).astype(BF)
        for c in self.across():
            c.start()

    def second(self):
        core, chip, _ = self.place()
        for c in self.across():
            c.wait_recv()
        total = self.part[4 * core + chip].astype(F32)
        for k in range(3):
            total += self.got[k].astype(F32)
        self.full[4 * core + chip] = total.astype(BF)
        for c in self.spread():
            c.start()

    def third(self):
        for c in self.spread():
            c.wait_recv()
        self.join().start()

    def finish(self):
        self.join().wait_recv()

    def close(self):
        for c in [self.halve()] + self.across() + self.spread() + [self.join()]:
            c.wait_send()


def exchange_scratch(rows, width):
    shapes = [(SEQ, rows, width), (4, rows, width), (3, rows, width), (SEQ, rows, width)]
    return [pltpu.VMEM(a, BF) for a in shapes] + [pltpu.SemaphoreType.DMA((8,)) for _ in range(4)]


def halves(block):
    low_lane = lax.broadcasted_iota(jnp.int32, block.shape, 1) < HD
    zero = jnp.zeros_like(block)
    return jnp.concatenate([jnp.where(low_lane, block, zero), jnp.where(low_lane, zero, block)], 0)


def unhalve(block):
    n = block.shape[0] // 2
    low_lane = lax.broadcasted_iota(jnp.int32, (n, block.shape[1]), 1) < HD
    return jnp.where(low_lane, block[:n], block[n:])


def norm_stats(v):
    mean = jnp.mean(v, -1, keepdims=True)
    centred = v - mean
    root = lax.rsqrt(jnp.mean(centred * centred, -1, keepdims=True) + norm_eps)
    return centred * root, root


def norm_back(grad, gain, xhat, root):
    gg = grad * gain
    return (gg - jnp.mean(gg, -1, keepdims=True) - xhat * jnp.mean(gg * xhat, -1, keepdims=True)) * root


def fold_rows(v):
    return jnp.sum(v.reshape(v.shape[0] // 8, 8, v.shape[1]), 0)


def gelu_pair(u):
    u2 = u * u
    s = 0.5 + 0.5 * jnp.tanh(u * (GELU_A + GELU_B * u2))
    a = u * s
    return a, s + a * (1.0 - s) * (2.0 * GELU_A + 6.0 * GELU_B * u2)


def places(groups):
    out = []
    for d in range(groups * SEQ):
        z, y, x, c = d // SEQ, (d // 4) % 2, (d // 2) % 2, d % 2
        out.append((((x * 2 + y) * groups + z, c), ((y * 2 + x) * groups + z, c)))
    return out


class Scatter:
    def __init__(self, src, base, bits, recv0, recv1, recv2, last, send_sem, recv_sem, send_z, recv_z):
        self.src, self.base, self.bits = src, base, bits
        self.recv, self.last = (recv0, recv1, recv2), last
        self.rows, self.lanes = last.shape[1:]
        self.send_sem, self.recv_sem, self.send_z, self.recv_z = send_sem, recv_sem, send_z, recv_z

    def mine(self, n):
        _, s = here()
        return lax.rem(lax.div(s, self.bits[n]), 2)

    def half(self, n, which):
        size = self.recv[n].shape[0]
        if n == 0:
            return self.src, self.base, which * self.lanes
        return self.recv[n - 1], which * size, 0

    def hop(self, n):
        g, s = here()
        mine, bit = self.mine(n), self.bits[n]
        src, row, lane = self.half(n, 1 - mine)
        size = self.recv[n].shape[0]
        return pltpu.make_async_remote_copy(
            src_ref=src.at[span(row, size, self.rows), span(lane, self.lanes, 128)],
            dst_ref=self.recv[n],
            send_sem=self.send_sem.at[n],
            recv_sem=self.recv_sem.at[n],
            device_id=(g, s + bit - 2 * bit * mine),
            device_id_type=MESH_ID,
        )

    def along(self):
        g, s = here()
        groups = self.last.shape[0] + 1
        out = []
        for k in range(1, groups):
            to = lax.rem(g + k, groups)
            out.append(
                pltpu.make_async_remote_copy(
                    src_ref=self.recv[2].at[span(to * self.rows, self.rows)],
                    dst_ref=self.last.at[k - 1],
                    send_sem=self.send_z.at[k - 1],
                    recv_sem=self.recv_z.at[k - 1],
                    device_id=(to, s),
                    device_id_type=MESH_ID,
                )
            )
        return out

    def start(self):
        self.hop(0).start()

    def step(self, n):
        src, row, lane = self.half(n, self.mine(n))
        self.hop(n).wait_recv()
        dst = self.recv[n]
        block = 2 * self.rows

        @pl.loop(0, dst.shape[0] // block)
        def _(i):
            to, at = span(i * block, block), span(row + i * block, block, self.rows)
            dst[to, :] = (dst[to, :].astype(F32) + src[at, span(lane, self.lanes, 128)].astype(F32)).astype(BF)

        if n < 2:
            self.hop(n + 1).start()
        else:
            for c in self.along():
                c.start()

    def total(self, out, row, column):
        for c in self.along():
            c.wait_recv()
        g, _ = here()
        total = self.recv[2][span(g * self.rows, self.rows), :].astype(F32)
        for k in range(self.last.shape[0]):
            total += self.last[k].astype(F32)
        few = self.rows // 2
        out[row : row + few, column : column + self.lanes] = total[:few]
        out[row : row + few, column + self.lanes : column + 2 * self.lanes] = total[few:]

    def close(self):
        for n in range(3):
            self.hop(n).wait_send()
        for c in self.along():
            c.wait_send()


class Place:
    def __init__(self, ref, row):
        self.ref, self.row = ref, row

    def __add__(self, rows):
        return Place(self.ref, self.row + rows)


def window(place, size, step=None):
    row = place.row
    rows = pl.ds(row, size) if isinstance(row, int) else span(row, size, step)
    return place.ref, rows


class Arena:
    def __getitem__(self, key):
        (ref, rows), lanes = key
        return ref[rows, lanes]

    def __setitem__(self, key, value):
        (ref, rows), lanes = key
        ref[rows, lanes] = value


class Vectors:
    def __init__(self, mine, recv, last, send_sem, recv_sem, send_z, recv_z):
        self.mine, self.recv, self.last = mine, recv, last
        self.sems = (send_sem, recv_sem, send_z, recv_z)

    def hop(self, n):
        g, s = here()
        bit = 1 << n
        other = s + bit - 2 * bit * lax.rem(lax.div(s, bit), 2)
        return pltpu.make_async_remote_copy(
            src_ref=self.mine.at[n],
            dst_ref=self.recv.at[n],
            send_sem=self.sems[0].at[n],
            recv_sem=self.sems[1].at[n],
            device_id=(g, other),
            device_id_type=MESH_ID,
        )

    def along(self):
        g, s = here()
        groups = self.last.shape[0] + 1
        return [
            pltpu.make_async_remote_copy(
                src_ref=self.mine.at[3],
                dst_ref=self.last.at[k - 1],
                send_sem=self.sems[2].at[k - 1],
                recv_sem=self.sems[3].at[k - 1],
                device_id=(lax.rem(g + k, groups), s),
                device_id_type=MESH_ID,
            )
            for k in range(1, groups)
        ]

    def start(self):
        self.hop(0).start()

    def step(self, n):
        self.hop(n).wait_recv()
        self.mine[n + 1] = self.mine[n] + self.recv[n]
        if n < 2:
            self.hop(n + 1).start()
        else:
            for c in self.along():
                c.start()

    def total(self):
        for c in self.along():
            c.wait_recv()
        return self.mine[3] + sum(self.last[k] for k in range(self.last.shape[0]))

    def close(self):
        for c in [self.hop(n) for n in range(3)] + self.along():
            c.wait_send()


class ProjGrad:
    def __init__(self, part, got, short, got_short, *sems):
        self.part, self.got, self.short, self.got_short, self.sems = part, got, short, got_short, sems

    def along(self, first, size):
        g, s = here()
        groups = self.part.shape[0]
        send, recv = self.sems[:2] if first == 0 else self.sems[2:4]
        out = []
        for k in range(1, groups):
            to = lax.rem(g + k, groups)
            out.append(
                pltpu.make_async_remote_copy(
                    src_ref=self.part.at[to, :, pl.ds(first, size)],
                    dst_ref=self.got.at[k - 1, :, pl.ds(first, size)],
                    send_sem=send.at[k - 1],
                    recv_sem=recv.at[k - 1],
                    device_id=(to, s),
                    device_id_type=MESH_ID,
                )
            )
        return out

    def across(self, b):
        g, s = here()
        slot = lax.rem(s - b + 2 * SEQ - 1, SEQ)
        return pltpu.make_async_remote_copy(
            src_ref=self.short.at[b],
            dst_ref=self.got_short.at[slot],
            send_sem=self.sems[4].at[b],
            recv_sem=self.sems[5].at[slot],
            device_id=(g, jnp.int32(b)),
            device_id_type=MESH_ID,
        )

    def arrived(self, slot):
        g, s = here()
        return pltpu.make_async_remote_copy(
            src_ref=self.short.at[0],
            dst_ref=self.got_short.at[slot],
            send_sem=self.sems[4].at[0],
            recv_sem=self.sems[5].at[slot],
            device_id=(g, s),
            device_id_type=MESH_ID,
        )

    def start(self, first, size):
        for c in self.along(first, size):
            c.start()

    def summed(self, first, size):
        g, _ = here()
        for c in self.along(first, size):
            c.wait_recv()
        total = self.part[g, :, first : first + size].astype(F32)
        for k in range(self.got.shape[0]):
            total += self.got[k, :, first : first + size].astype(F32)
        return total

    def across_all(self, shard, short_len):
        _, s = here()
        total = self.summed(shard, short_len)
        for b in range(self.short.shape[0]):
            self.short[b] = total[:, b * shard : (b + 1) * shard].astype(BF)

            @pl.when(s != b)
            def _(b=b):
                self.across(b).start()

    def finish(self, out, shard):
        _, s = here()
        count = self.short.shape[0]
        out[...] = self.summed(0, shard)

        @pl.when(s < count)
        def _():
            total = out[...] + self.short[lax.rem(s, count)].astype(F32)
            for slot in range(SEQ - 1):
                self.arrived(slot).wait_recv()
                total += self.got_short[slot].astype(F32)
            out[...] = total

    def close(self):
        _, s = here()
        shard = self.short.shape[2]
        for c in self.along(0, shard) + self.along(shard, self.part.shape[2] - shard):
            c.wait_send()
        for b in range(self.short.shape[0]):

            @pl.when(s != b)
            def _(b=b):
                self.across(b).wait_send()


def layer_kernel(slots, groups, shard, *refs):
    refs = list(refs)

    def take(n):
        out = refs[:n]
        del refs[:n]
        return out

    (long_x, short_x, long_dy, short_dy, live) = take(5)
    (wq_in, wk_in, wv_in, wo_in, up_in, down_in, proj) = take(7)
    (gain1, shift1, gain2, shift2) = (a[...].reshape(1, -1) for a in take(4))
    (long_out, short_out, long_grad, short_grad) = take(4)
    (grad_q, grad_k, grad_v, grad_o, grad_up, grad_down, grad_proj, vec_out) = take(8)
    (q_hbm, y_hbm, mixed_hbm, probs_hbm, sums_hbm) = take(5)
    (a_ref, s_ref, ud_ref, x_ref, m_ref, h_ref, w_ref, p_ref, b_ref, resid, root, vec, pcols, pshort, pacc) = take(15)
    (sem_in, sem_out, sem_back) = take(3)
    exch_bufs = take(4)
    forward_exchange = Exchange(*exch_bufs, *take(2))
    backward_exchange = Exchange(*exch_bufs, *take(2))
    vectors = Vectors(*take(7))
    projected = ProjGrad(*take(10))

    g, s = here()
    short_len = short_x.shape[1]
    width = resid.shape[1]
    wide = 4 * width
    shorts = slots * short_len
    tokens = shorts + shard
    devices = groups * SEQ
    few = width // devices
    lanes = width // 2
    act, slope = Place(a_ref, 0), Place(s_ref, 0)
    up, down = Place(ud_ref, 0), Place(ud_ref, wide)
    xs, ms, hs, xhs = Place(x_ref, 0), Place(m_ref, 0), Place(h_ref, 0), Place(h_ref, tokens)
    wo, pack, weights = Place(w_ref, 0), Place(p_ref, 0), Place(h_ref, 0)
    pack_up = act
    q1, y1 = act, act + tokens
    probs1, sums1 = Place(s_ref, 0), Place(p_ref, 0)
    q2, y2 = slope, slope + tokens
    long_sums2 = y2 + (slots + 1) * KP
    key_grads = long_sums2 + 2 * KP
    probs2, through = Place(ud_ref, 0), Place(ud_ref, 0)
    sums2, gq2 = pack + width, pack_up + 4 * width
    value_grads, ms2, x2s = Place(b_ref, 0), hs, ms

    orders = ((1, 2, 4), (1, 4, 2))

    def unit(base, order):
        return Scatter(base.ref, base.row, orders[order], *take(8))

    downs = [unit(pack + n * width, n % 2) for n in range(4)]
    ups = [unit(pack_up + n * width, n % 2) for n in range(4)]
    unit_o, unit_q, unit_v, unit_k = (unit(pack + n * width, n % 2) for n in range(4))
    assert not refs

    copy = pltpu.make_async_copy
    at = lambda place, size: place.ref.at[pl.ds(place.row, size)]
    arena = Arena()
    counts = {"in": 0, "out": 0, "back": 0}

    def move(kind, a, b):
        sem = {"in": sem_in, "out": sem_out, "back": sem_back}[kind]
        counts[kind] += 1
        return copy(a, b, sem.at[counts[kind] - 1])

    def rows_of(long_a, short_a, base, kind, back=False):
        pairs = [(long_a.at[0], at(base + shorts, shard))]
        pairs += [(short_a.at[i], at(base + i * short_len, short_len)) for i in range(slots)]
        return [move(kind, b, a) if back else move(kind, a, b) for a, b in pairs]

    in_x = rows_of(long_x, short_x, xs, "in")
    in_cols = move("in", proj.at[:, span(s * shard, shard)], pcols)
    in_wk = move("in", wk_in, at(weights + width, width))
    in_wv = move("in", wv_in, at(weights + 2 * width, width))
    in_wq = move("in", wq_in, at(weights, width))
    in_pshort = move("in", proj.at[:, pl.ds(0, short_len)], pshort)
    in_wo = move("in", wo_in, at(wo, width))
    in_up = [move("in", up_in.at[:, pl.ds(j * width, width)], at(up + j * width, width)) for j in range(4)]
    in_down = move("in", down_in, at(down, wide))
    for c in [in_x[0], in_cols] + in_x[1:] + [in_pshort, in_wk, in_wv, in_wq, in_wo] + in_up + [in_down]:
        c.start()
    greet(seq_peers() + grp_peers(groups))

    part, full = forward_exchange.part, forward_exchange.full
    blocks = KP // SEQ
    items = slots * KP
    in_x[0].wait()
    in_cols.wait()
    part[...] = mm(pcols[...], arena[window(xs + shorts, shard), :]).astype(BF).reshape(SEQ, blocks, width)
    forward_exchange.start()
    for c in in_x[1:] + [in_pshort]:
        c.wait()
    for i in range(slots):
        x = arena[window(xs + i * short_len, short_len), :]
        arena[window(y1 + i * KP, KP), :] = mm(pshort[...], x).astype(BF)
    in_wk.wait()

    def summaries(to, y, size):
        for n in range(2):
            w = arena[window(weights + (1 + n) * width, width), :]
            arena[window(to + n * size, size), :] = mm(arena[window(y, size), :], w).astype(BF)

    in_wv.wait()
    summaries(sums1, y1, items)
    forward_exchange.first()
    in_wq.wait()
    arena[window(q1, tokens), :] = (0.125 * mm(arena[window(xs, tokens), :], arena[window(weights, width), :])).astype(BF)
    out_q = move("out", at(q1, tokens), q_hbm)
    out_q.start()
    forward_exchange.second()
    heads = width // HD
    item_rows = heads * short_len // width * KP

    def head(h, size):
        beside = width // size
        return h // beside * KP, slice(h % beside * size, (h % beside + 1) * size)

    def staged(before, between, after):
        now, last = before(0), None
        for pair in range(heads // 2):
            ahead = before(pair + 1) if pair + 1 < heads // 2 else None
            middle = between(pair, *now)
            if last is not None:
                after(pair - 1, last)
            now, last = ahead, middle
        after(heads // 2 - 1, last)

    def lanes_of(pair):
        return slice(pair * 2 * HD, (pair + 1) * 2 * HD)

    def attend(row, size, ks, vs, probs):
        def scores(pair):
            q = arena[window(q1 + row, size, 128), lanes_of(pair)]
            return (mm(halves(arena[window(ks, KP), lanes_of(pair)]), q, 1, 1),)

        def softmax(pair, sc):
            parts = []
            for h in range(2):
                part = sc[h * KP : (h + 1) * KP]
                e = jnp.exp(part - jnp.max(part, 0, keepdims=True))
                parts.append((e * (1.0 / jnp.sum(e, 0, keepdims=True))).astype(BF))
                first, cols = head(2 * pair + h, size)
                arena[window(probs + first, KP, 128), cols] = parts[h]
            return jnp.concatenate(parts, 0)

        def mix(pair, p):
            out = mm(halves(arena[window(vs, KP), lanes_of(pair)]), p, 0, 0)
            arena[window(ms + row, size, 128), lanes_of(pair)] = out.T.astype(BF)

        staged(scores, softmax, mix)

    @pl.loop(0, slots)
    def _(i):
        attend(i * short_len, short_len, sums1 + i * KP, sums1 + (items + i * KP), probs1 + i * item_rows)

        @pl.when(i == 1)
        def _():
            forward_exchange.third()

    long_probs = probs1 + slots * item_rows
    out_probs = [move("out", at(probs1, slots * item_rows), probs_hbm.at[pl.ds(0, slots * item_rows)])]
    out_probs[0].start()
    forward_exchange.finish()
    long_sums = sums1 + 2 * items
    arena[window(y1 + items, KP), :] = full[...].reshape(KP, width)
    summaries(long_sums, y1 + items, KP)
    out_y = move("out", at(y1, items + KP), y_hbm)
    out_y.start()

    def enter(row, size, step):
        r = span(row, size, step)
        x = arena[window(xs + row, size, step), :].astype(F32)
        xh, rs = norm_stats(mm(arena[window(ms + row, size, step), :], arena[window(wo, width), :]) + x)
        arena[window(xhs + row, size, step), :] = xh.astype(BF)
        root[r, :] = jnp.broadcast_to(rs, (size, 128))
        hidden = xh * gain1 + shift1
        resid[r, :] = hidden
        arena[window(hs + row, size, step), :] = hidden.astype(BF)

    in_wo.wait()

    @pl.loop(0, slots // 2)
    def _(i):
        enter(i * 2 * short_len, 2 * short_len, 128)

    attend(shorts, shard, long_sums, long_sums + KP, long_probs)
    long_size = heads * shard // width * KP
    out_probs += [move("out", at(long_probs, long_size), probs_hbm.at[pl.ds(slots * item_rows, long_size)])]
    out_sums = move("out", at(sums1, (2 * slots + 2) * KP), sums_hbm)
    out_mixed = move("out", at(ms, tokens), mixed_hbm)
    for c in out_probs[1:] + [out_sums, out_mixed]:
        c.start()
    enter(shorts, shard, 128)
    block = tokens // 3
    in_dy = rows_of(long_dy, short_dy, xs, "in")
    for c in in_dy:
        c.start()
    for c in [out_y, out_q, out_mixed] + out_probs:
        c.wait()
    for c in in_up + [in_down]:
        c.wait()

    part_rows = tokens // 2

    @pl.loop(0, 8)
    def _(i):
        j, r = lax.div(i, 2), lax.rem(i, 2) * part_rows
        hidden = arena[window(hs + r, part_rows, 64), :]
        a, slope_j = gelu_pair(mm(hidden, arena[window(up + j * width, width, 128), :]))
        a = a.astype(BF)
        arena[window(act + j * tokens + r, part_rows, 64), :] = a
        arena[window(slope + j * tokens + r, part_rows, 64), :] = slope_j.astype(BF)
        resid[span(r, part_rows), :] += mm(a, arena[window(down + j * width, width, 128), :])

    vec[...] = jnp.zeros_like(vec)
    for c in in_dy:
        c.wait()
    rb = 128

    @pl.loop(0, tokens // rb)
    def _(i):
        r = span(i * rb, rb)
        rx = window(xs + i * rb, rb, 128)
        alive = jnp.where(lax.div(i * rb, short_len) < live[0], 1.0, 0.0).astype(F32)
        alive = jnp.where(i * rb >= shorts, 1.0, alive)
        xh, rs = norm_stats(resid[r, :])
        top = alive * arena[rx, :].astype(F32)
        vec[16:24, :] += fold_rows(top * xh)
        vec[24:32, :] += fold_rows(top)
        arena[rx, :] = (alive * (xh * gain2 + shift2)).astype(BF)
        dx = norm_back(top, gain2, xh, rs)
        resid[r, :] = dx
        arena[window(ms + i * rb, rb, 128), :] = dx.astype(BF)

    outs = rows_of(long_out, short_out, xs, "out", back=True)
    for c in outs:
        c.start()
    out_sums.wait()
    place = places(groups)

    def packed(base, order, value, step, first):
        for d in range(value.shape[0] // step):
            row, core = place[d][order]
            rows = slice(d * step + first, d * step + first + few)
            arena[window(base + row * 2 * few, 2 * few), core * lanes : (core + 1) * lanes] = jnp.concatenate(
                [value[rows, :lanes], value[rows, lanes:]], 0
            ).astype(BF)

    @pl.loop(0, groups)
    def _(j):
        value = mm(arena[window(act + j * tokens, tokens, 128), :], arena[window(ms, tokens), :], 0, 0)
        for n in range(4):
            packed(pack + n * width + j * 2 * few, n % 2, value, 4 * few, n * few)

    for piece in downs:
        piece.start()
    low = at(ms, tokens)

    @pl.loop(0, 8)
    def _(i):
        j, r = lax.div(i, 2), lax.rem(i, 2) * part_rows
        rj = window(slope + j * tokens + r, part_rows, 64)
        gb = low[span(r, part_rows), :]
        gu = mm(gb, arena[window(down + j * width, width, 128), :], 1, 1) * arena[rj, :].astype(F32)
        gu = gu.astype(BF)
        arena[rj, :] = gu
        resid[span(r, part_rows), :] += mm(gu, arena[window(up + j * width, width, 128), :], 1, 1)

        @pl.when(i == 0)
        def _():
            for piece in downs[:2]:
                piece.step(0)

        @pl.when(i == 1)
        def _():
            for piece in downs[2:]:
                piece.step(0)

        @pl.when(i == 4)
        def _():
            for piece in downs[:2]:
                piece.step(1)

    back = {}

    def load(name, a, b):
        back[name] = move("back", a, b)
        back[name].start()

    load("probs", probs_hbm, at(probs2, 4 * tokens))

    for piece in downs[2:]:
        piece.step(1)

    @pl.loop(0, 2)
    def _(m):
        for n in range(2):
            j = 2 * m + n
            gu = arena[window(slope + j * tokens, tokens, 128), :]
            packed(pack_up + j * width, n, mm(arena[window(hs, tokens), :], gu, 0, 0), few, 0)

        @pl.when(m == 0)
        def _():
            for piece in ups[:2]:
                piece.start()

        @pl.when(m == 1)
        def _():
            for piece in ups[2:]:
                piece.start()
            for piece in ups[:2]:
                piece.step(0)
            for piece in downs[:2]:
                piece.step(2)

    load("y", y_hbm, at(y2, items + KP))
    load("q", q_hbm, at(q2, tokens))
    load("mixed", mixed_hbm, at(ms2, tokens))
    for piece in downs[1:]:
        piece.hop(0).wait_send()
    load("sums", sums_hbm.at[pl.ds(0, 2 * items)], at(sums2, 2 * items))
    load("long_sums", sums_hbm.at[pl.ds(2 * items, 2 * KP)], at(long_sums2, 2 * KP))

    @pl.loop(0, tokens // rb)
    def _(i):
        r = span(i * rb, rb)
        gh = resid[r, :]
        xh = arena[window(xhs + i * rb, rb, 128), :].astype(F32)
        vec[0:8, :] += fold_rows(gh * xh)
        vec[8:16, :] += fold_rows(gh)
        dx = norm_back(gh, gain1, xh, root[r, 0:1])
        resid[r, :] = dx
        low[r, :] = dx.astype(BF)

    four = jnp.sum(vec[...].reshape(4, 8, width), 1)
    vectors.mine[0] = jnp.concatenate([four, jnp.zeros_like(four)], 0)
    vectors.start()
    for c in outs:
        c.wait()
    arena[window(xs, tokens), :] = mm(low[...], arena[window(wo, width), :], 1, 1).astype(BF)
    for piece in ups[2:]:
        piece.step(0)
    for piece in downs[2:]:
        piece.step(2)
    downs[0].hop(0).wait_send()
    back["mixed"].wait()
    packed(pack, 0, mm(arena[window(ms2, tokens), :], low[...], 0, 0), few, 0)
    unit_o.start()
    load("wq", wq_in, at(weights, width))
    load("wk", wk_in, at(weights + width, width))
    load("wv", wv_in, at(weights + 2 * width, width))
    for n, c in enumerate(rows_of(long_x, short_x, x2s, "back")):
        back["x", n] = c
        c.start()

    def attend_back(row, size, ks, vs, probs, n):
        def front(pair):
            gm = arena[window(xs + row, size, 128), lanes_of(pair)]
            p = []
            for h in range(2):
                first, cols = head(2 * pair + h, size)
                p.append(arena[window(probs + first, KP, 128), cols])
            gp = mm(halves(arena[window(vs, KP), lanes_of(pair)]), gm, 1, 1)
            grad = unhalve(mm(jnp.concatenate(p, 0), gm)).astype(BF)
            arena[window(value_grads + n * KP, KP, 128), lanes_of(pair)] = grad
            return gp, p

        def middle(pair, gp, p):
            parts = []
            for h in range(2):
                ph = p[h].astype(F32)
                t = ph * gp[h * KP : (h + 1) * KP]
                parts.append((t - ph * jnp.sum(t, 0, keepdims=True)).astype(BF))
            return jnp.concatenate(parts, 0)

        def rear(pair, gs):
            q = arena[window(q2 + row, size, 128), lanes_of(pair)]
            arena[window(key_grads + n * KP, KP, 128), lanes_of(pair)] = unhalve(mm(gs, q)).astype(BF)
            gq = mm(halves(arena[window(ks, KP), lanes_of(pair)]), gs, 0, 0).T.astype(BF).astype(F32)
            arena[window(gq2 + row, size, 128), lanes_of(pair)] = (gq * 0.125).astype(BF)

        staged(front, middle, rear)

    def through_projections(first, count):
        rows = count * KP
        key_grad = mm(arena[window(key_grads + first * KP, rows), :], arena[window(weights + width, width), :], 1, 1)
        return key_grad + mm(arena[window(value_grads + first * KP, rows), :], arena[window(weights + 2 * width, width), :], 1, 1)

    for name in ("q", "y", "sums", "long_sums", "probs"):
        back[name].wait()
    forward_exchange.close()
    attend_back(shorts, shard, long_sums2, long_sums2 + KP, probs2 + slots * item_rows, slots)
    unit_o.step(0)
    for name in ("wq", "wk", "wv"):
        back[name].wait()
    part[...] = through_projections(slots, 1).astype(BF).reshape(SEQ, blocks, width)
    backward_exchange.start()

    @pl.loop(0, slots)
    def _(i):
        attend_back(i * short_len, short_len, sums2 + i * KP, sums2 + (items + i * KP), probs2 + i * item_rows, i)

        @pl.when(i == 0)
        def _():
            backward_exchange.first()
            for piece in ups[:2]:
                piece.step(1)

        @pl.when(i == 1)
        def _():
            vectors.step(0)
            for piece in ups[2:]:
                piece.step(1)

        @pl.when(i == slots - 1)
        def _():
            backward_exchange.second()
            for piece in ups[:2]:
                piece.step(2)

    for n in range(1 + slots):
        back["x", n].wait()
    x2, gq = at(x2s, tokens), at(gq2, tokens)

    packed(pack + width, 1, mm(x2[...], gq[...], 0, 0), few, 0)
    unit_q.start()
    unit_o.step(1)
    y = arena[window(y2, items + KP), :]
    packed(pack + 2 * width, 0, mm(y, arena[window(value_grads, items + KP), :], 0, 0), few, 0)
    unit_v.start()
    vectors.step(1)
    unit_q.step(0)
    packed(pack + 3 * width, 1, mm(y, arena[window(key_grads, items + KP), :], 0, 0), few, 0)
    unit_k.start()
    unit_v.step(0)
    backward_exchange.third()
    for piece in ups[2:]:
        piece.step(2)

    arena[window(through, items), :] = through_projections(0, slots).astype(BF)
    unit_k.step(0)
    unit_o.step(2)
    pacc[...] = jnp.zeros_like(pacc)

    def leave(cols, row, size, n):
        grad = arena[window(through + n * KP, KP), :]
        r = span(row, size, 128)
        dx = resid[r, :] + mm(gq[r, :], arena[window(weights, width), :], 1, 1) + mm(cols[...], grad, 0, 0)
        arena[window(xs + row, size, 128), :] = dx.astype(BF)
        return mm(grad, x2[r, :], 1, 1)

    @pl.loop(0, slots)
    def _(i):
        pacc[...] += leave(pshort, i * short_len, short_len, i)

    prow = KP // groups
    projected.part[:, :, shard:] = pacc[...].astype(BF).reshape(groups, prow, short_len)
    projected.start(shard, short_len)
    backward_exchange.finish()
    arena[window(through + items, KP), :] = full[...].reshape(KP, width)
    long_cols = leave(pcols, shorts, shard, slots)
    projected.part[:, :, 0:shard] = long_cols.astype(BF).reshape(groups, prow, shard)
    projected.start(0, shard)
    unit_q.step(1)
    vectors.step(2)
    outs = rows_of(long_grad, short_grad, xs, "out", back=True)
    for c in outs:
        c.start()
    unit_v.step(1)
    projected.across_all(shard, short_len)
    for n, piece in enumerate(downs):
        piece.total(grad_down, n * few, 0)
    for n, piece in enumerate(ups):
        piece.total(grad_up, 0, n * width)
    unit_o.total(grad_o, 0, 0)
    unit_k.step(1)
    unit_q.step(2)
    vec_out[...] = vectors.total()
    unit_v.step(2)
    projected.finish(grad_proj, shard)
    unit_k.step(2)
    unit_q.total(grad_q, 0, 0)
    unit_v.total(grad_v, 0, 0)
    unit_k.total(grad_k, 0, 0)
    for c in outs:
        c.wait()
    for piece in downs:
        for n in range(1, 3):
            piece.hop(n).wait_send()
        for c in piece.along():
            c.wait_send()
    for piece in ups + [unit_o, unit_q, unit_v, unit_k, vectors, projected, backward_exchange]:
        piece.close()


def fast_shards(groups, *args):
    (long_x, short_x, long_dy, short_dy, live, wq, wk, wv, wo, up, down, proj, g1, b1, g2, b2) = args
    slots, short_len, width = short_x.shape
    shard = long_x.shape[1]
    tokens = slots * short_len + shard
    wide = up.shape[1]
    devices = groups * SEQ
    few = width // devices
    sds = jax.ShapeDtypeStruct
    anyspace = pl.BlockSpec(memory_space=pl.ANY)
    vmem = pl.BlockSpec(memory_space=pltpu.VMEM)
    dma = pltpu.SemaphoreType.DMA
    prow = KP // groups
    out_shapes = [sds(a.shape, BF) for a in (long_x, short_x, long_x, short_x)]
    grads = [(few, width)] * 4 + [(few, wide), (4 * few, width), (prow, shard), (8, width)]
    out_shapes += [sds(a, F32) for a in grads]
    row = (tokens, width)
    out_shapes += [
        sds(a, BF)
        for a in [row, ((slots + 1) * KP, width), row, (4 * tokens, width), ((2 * slots + 2) * KP, width)]
    ]
    regions = [4 * tokens, 4 * tokens, 2 * wide, tokens, tokens, 2 * tokens, width, 4 * width, (slots + 1) * KP]
    heads = short_len // shard
    scratch = [
        *[pltpu.VMEM((n, width), BF) for n in regions],
        pltpu.VMEM(row, F32),
        pltpu.VMEM((tokens, 128), F32),
        pltpu.VMEM((32, width), F32),
        pltpu.VMEM((KP, shard), BF),
        pltpu.VMEM((KP, short_len), BF),
        pltpu.VMEM((KP, short_len), F32),
        dma((12 + 2 * (1 + slots),)),
        dma((13 + 2 * (1 + slots),)),
        dma((13 + 1 + slots,)),
    ]
    scratch += exchange_scratch(KP // SEQ, width)
    along = [dma((groups - 1,)), dma((groups - 1,))]
    scratch += [pltpu.VMEM((n, 8, width), F32) for n in (4, 3, groups - 1)] + [dma((3,)), dma((3,))] + along
    scratch += [pltpu.VMEM((n, prow, shard + short_len), BF) for n in (groups, groups - 1)]
    scratch += [pltpu.VMEM((n, prow, shard), BF) for n in (heads, SEQ - 1)]
    scratch += along + along + [dma((heads,)), dma((SEQ - 1,))]
    lanes = width // 2
    unit = [pltpu.VMEM((width // n, lanes), BF) for n in (1, 2, 4)]
    unit += [pltpu.VMEM((groups - 1, 2 * few, lanes), BF), dma((3,)), dma((3,))] + along
    scratch += unit * 12
    outs = pl.pallas_call(
        functools.partial(layer_kernel, slots, groups, shard),
        name="encoder_layer",
        out_shape=out_shapes,
        in_specs=[anyspace] * 4 + [pl.BlockSpec(memory_space=pltpu.SMEM)] + [anyspace] * 7 + [vmem] * 4,
        out_specs=[anyspace] * 4 + [vmem] * 8 + [anyspace] * 5,
        scratch_shapes=scratch,
        compiler_params=pltpu.CompilerParams(
            collective_id=0, has_side_effects=True, vmem_limit_bytes=VMEM_BYTES
        ),
    )(long_x, short_x, long_dy, short_dy, live, wq, wk, wv, wo, up, down, proj, g1, b1, g2, b2)
    return emit_call(outs[:12], few)


def emit_kernel(*refs):
    *ins, vec = refs[:12]
    outs, vectors, stages = refs[12:23], refs[23:27], refs[27:38]
    sem_in, sem_out = refs[38:]
    reads = [pltpu.make_async_copy(a, b, sem_in.at[n]) for n, (a, b) in enumerate(zip(ins, stages))]
    writes = [pltpu.make_async_copy(a, b, sem_out.at[n]) for n, (a, b) in enumerate(zip(stages, outs))]
    for c in reads:
        c.start()
    g, s = here()
    width = vec.shape[1]
    few = vectors[0].shape[0]
    mine = pltpu.roll(vec[...], width - (g * SEQ + s) * few, 1)
    for n in range(4):
        vectors[n][...] = mine[n, 0:few]
    for a, b in zip(reads, writes):
        a.wait()
        b.start()
    for c in writes:
        c.wait()


def emit_call(arrays, few):
    anyspace = pl.BlockSpec(memory_space=pl.ANY)
    vmem = pl.BlockSpec(memory_space=pltpu.VMEM)
    return pl.pallas_call(
        emit_kernel,
        name="emit",
        out_shape=[jax.ShapeDtypeStruct(a.shape, a.dtype) for a in arrays[:11]] + [jax.ShapeDtypeStruct((few,), F32)] * 4,
        in_specs=[anyspace] * 11 + [vmem],
        out_specs=[anyspace] * 11 + [vmem] * 4,
        scratch_shapes=[pltpu.VMEM(a.shape, a.dtype) for a in arrays[:11]] + [pltpu.SemaphoreType.DMA((11,))] * 2,
        compiler_params=pltpu.CompilerParams(vmem_limit_bytes=VMEM_BYTES),
    )(*arrays)


def fits(mesh, args):
    long_x, width, wide = args[0], args[0].shape[2], args[9].shape[1]
    devices = mesh.shape["grp"] * mesh.shape["seq"]
    whole = width % (devices * 8) == 0 and wide == 4 * width
    return mesh.shape["seq"] == SEQ and whole and long_x.shape[0] == 1


def solution(mesh):
    placed = (
        P("grp", "seq", None),
        P(("grp", "seq"), None, None),
        P("grp", "seq", None),
        P(("grp", "seq"), None, None),
        P(("grp", "seq")),
        P(),
        P(),
        P(),
        P(),
        P(),
        P(),
        P(),
        P(),
        P(),
        P(),
        P(),
    )
    groups = mesh.shape["grp"]

    def body(*args):
        if fits(mesh, args):
            return fast_shards(groups, *args)
        return shards(*args)

    return jax.shard_map(
        body,
        mesh=mesh,
        in_specs=placed,
        out_specs=(
            P("grp", "seq", None),
            P(("grp", "seq"), None, None),
            P("grp", "seq", None),
            P(("grp", "seq"), None, None),
            P(("grp", "seq"), None),
            P(("grp", "seq"), None),
            P(("grp", "seq"), None),
            P(("grp", "seq"), None),
            P(("grp", "seq"), None),
            P(("grp", "seq"), None),
            P("grp", "seq"),
            P(("grp", "seq")),
            P(("grp", "seq")),
            P(("grp", "seq")),
            P(("grp", "seq")),
        ),
        check_vma=False,
    )
```

```python
import functools

import jax
import jax.numpy as jnp
from jax import lax
from jax.experimental import pallas as pl
from jax.experimental.pallas import tpu as pltpu
from jax.sharding import PartitionSpec as P

HD = 64
KP = 256


norm_eps = 1e-05


def shortened(shard):
    return jax.tree.map(lambda a: a.astype(jnp.bfloat16) if a.dtype == jnp.float32 else a, shard)


def norm_rows(resid, gain_vec, shift_vec):
    row_mean = jnp.mean(resid, axis=-1, keepdims=True)
    centred = resid - row_mean
    variance = jnp.mean(centred * centred, axis=-1, keepdims=True)
    return centred * lax.rsqrt(variance + norm_eps) * gain_vec + shift_vec


def smooth_gate(upward):
    return jax.nn.gelu(upward, approximate=True)


def same_sums(partials):
    return partials


def layer_pass(sequences, cotangent, live_rows, proj_cols, fold_summaries, fold_grads, params):
    (
        query_w,
        key_w,
        value_w,
        out_w,
        up_w,
        down_w,
        gain_first,
        shift_first,
        gain_second,
        shift_second,
    ) = params
    seq_count, length, model_width = sequences.shape
    head_count = model_width // HD
    wide = jnp.float32
    narrow = jnp.bfloat16
    queries = (
        0.125 * jnp.einsum("nld,de->nle", sequences, query_w, preferred_element_type=wide)
    ).astype(narrow)
    key_vecs = jnp.einsum("nld,de->nle", sequences, key_w, preferred_element_type=wide).astype(
        narrow
    )
    value_vecs = jnp.einsum("nld,de->nle", sequences, value_w, preferred_element_type=wide).astype(
        narrow
    )
    key_part = jnp.einsum("kl,nld->nkd", proj_cols, key_vecs, preferred_element_type=wide)
    value_part = jnp.einsum("kl,nld->nkd", proj_cols, value_vecs, preferred_element_type=wide)
    key_sum, value_sum = fold_summaries((key_part, value_part))
    key_heads = key_sum.astype(narrow).reshape(seq_count, KP, head_count, HD)
    value_heads = value_sum.astype(narrow).reshape(seq_count, KP, head_count, HD)
    query_heads = queries.reshape(seq_count, length, head_count, HD)
    scores = jnp.einsum("nlhe,nkhe->nhlk", query_heads, key_heads, preferred_element_type=wide)
    attn_probs = jax.nn.softmax(scores, axis=-1)
    probs_low = attn_probs.astype(narrow)
    mixed_heads = (
        jnp.einsum("nhlk,nkhe->nlhe", probs_low, value_heads, preferred_element_type=wide)
        .reshape(seq_count, length, model_width)
        .astype(narrow)
    )
    attn_out = jnp.einsum("nld,de->nle", mixed_heads, out_w, preferred_element_type=wide)
    hidden, first_back = jax.vjp(
        norm_rows, sequences.astype(wide) + attn_out, gain_first, shift_first
    )
    hidden_low = hidden.astype(narrow)
    upward = jnp.einsum("nld,df->nlf", hidden_low, up_w, preferred_element_type=wide)
    activated, gate_back = jax.vjp(smooth_gate, upward)
    activated_low = activated.astype(narrow)
    branch = jnp.einsum("nlf,fd->nld", activated_low, down_w, preferred_element_type=wide)
    normed, second_back = jax.vjp(norm_rows, hidden + branch, gain_second, shift_second)
    result = normed * live_rows[:, None, None]
    grad_top = cotangent.astype(wide) * live_rows[:, None, None]
    grad_resid_two, grad_gain_two, grad_shift_two = second_back(grad_top)
    grad_branch = grad_resid_two.astype(narrow)
    grad_down = jnp.einsum("nlf,nld->fd", activated_low, grad_branch, preferred_element_type=wide)
    grad_activated = jnp.einsum("nld,fd->nlf", grad_branch, down_w, preferred_element_type=wide)
    (grad_upward,) = gate_back(grad_activated)
    grad_upward_low = grad_upward.astype(narrow)
    grad_up = jnp.einsum("nld,nlf->df", hidden_low, grad_upward_low, preferred_element_type=wide)
    grad_hidden = grad_resid_two + jnp.einsum(
        "nlf,df->nld", grad_upward_low, up_w, preferred_element_type=wide
    )
    grad_resid_one, grad_gain_one, grad_shift_one = first_back(grad_hidden)
    grad_attn = grad_resid_one.astype(narrow)
    grad_out = jnp.einsum("nld,nle->de", mixed_heads, grad_attn, preferred_element_type=wide)
    grad_mixed = (
        jnp.einsum("nle,de->nld", grad_attn, out_w, preferred_element_type=wide)
        .astype(narrow)
        .reshape(seq_count, length, head_count, HD)
    )
    grad_probs = jnp.einsum("nlhe,nkhe->nhlk", grad_mixed, value_heads, preferred_element_type=wide)
    value_grad_part = jnp.einsum(
        "nhlk,nlhe->nkhe", probs_low, grad_mixed, preferred_element_type=wide
    ).reshape(seq_count, KP, model_width)
    grad_scores = attn_probs * (
        grad_probs - jnp.sum(grad_probs * attn_probs, axis=-1, keepdims=True)
    )
    scores_low = grad_scores.astype(narrow)
    grad_queries = (
        jnp.einsum("nhlk,nkhe->nlhe", scores_low, key_heads, preferred_element_type=wide).astype(
            narrow
        )
        * 0.125
    ).reshape(seq_count, length, model_width)
    key_grad_part = jnp.einsum(
        "nhlk,nlhe->nkhe", scores_low, query_heads, preferred_element_type=wide
    ).reshape(seq_count, KP, model_width)
    key_grad_sum, value_grad_sum = fold_grads((key_grad_part, value_grad_part))
    key_grad_low = key_grad_sum.astype(narrow)
    value_grad_low = value_grad_sum.astype(narrow)
    grad_keys = jnp.einsum(
        "kl,nkd->nld", proj_cols, key_grad_low, preferred_element_type=wide
    ).astype(narrow)
    grad_values = jnp.einsum(
        "kl,nkd->nld", proj_cols, value_grad_low, preferred_element_type=wide
    ).astype(narrow)
    grad_cols = jnp.einsum(
        "nkd,nld->kl", key_grad_low, key_vecs, preferred_element_type=wide
    ) + jnp.einsum("nkd,nld->kl", value_grad_low, value_vecs, preferred_element_type=wide)
    grad_query = jnp.einsum("nld,nle->de", sequences, grad_queries, preferred_element_type=wide)
    grad_key = jnp.einsum("nld,nle->de", sequences, grad_keys, preferred_element_type=wide)
    grad_value = jnp.einsum("nld,nle->de", sequences, grad_values, preferred_element_type=wide)
    grad_sequences = grad_resid_one + jnp.einsum(
        "nle,de->nld", grad_queries, query_w, preferred_element_type=wide
    )
    grad_sequences = grad_sequences + jnp.einsum(
        "nle,de->nld", grad_keys, key_w, preferred_element_type=wide
    )
    grad_sequences = grad_sequences + jnp.einsum(
        "nle,de->nld", grad_values, value_w, preferred_element_type=wide
    )
    weight_grads = (
        grad_query,
        grad_key,
        grad_value,
        grad_out,
        grad_up,
        grad_down,
        grad_gain_one,
        grad_shift_one,
        grad_gain_two,
        grad_shift_two,
    )
    return (result, grad_sequences, weight_grads, grad_cols)


def shards(
    long_x,
    short_x,
    long_dy,
    short_dy,
    short_live,
    query_weight,
    key_weight,
    value_weight,
    out_weight,
    up_weight,
    down_weight,
    length_proj,
    gain_one,
    shift_one,
    gain_two,
    shift_two,
):
    params = (
        query_weight,
        key_weight,
        value_weight,
        out_weight,
        up_weight,
        down_weight,
        gain_one,
        shift_one,
        gain_two,
        shift_two,
    )
    shard_len = long_x.shape[1]
    slot_count = short_x.shape[0]
    short_len = short_x.shape[1]
    shard_start = lax.axis_index("seq") * shard_len
    long_cols = lax.dynamic_slice_in_dim(length_proj, shard_start, shard_len, 1)

    def sum_summaries(partials):
        return jax.tree.map(
            lambda part: part.astype(jnp.float32), lax.psum(shortened(partials), "seq")
        )

    def sum_summary_grads(partials):
        return jax.tree.map(
            lambda part: part.astype(jnp.float32), lax.psum(shortened(partials), "seq")
        )

    long_live = jnp.ones((long_x.shape[0],), jnp.float32)
    long_result, long_back, long_weights, long_proj = layer_pass(
        long_x, long_dy, long_live, long_cols, sum_summaries, sum_summary_grads, params
    )
    short_mask = (jnp.arange(slot_count) < short_live[0]).astype(jnp.float32)
    short_result, short_back, short_weights, short_proj = layer_pass(
        short_x, short_dy, short_mask, length_proj[:, :short_len], same_sums, same_sums, params
    )
    summed = jax.tree.map(jnp.add, long_weights, short_weights)
    (
        grad_query,
        grad_key,
        grad_value,
        grad_out,
        grad_up,
        grad_down,
        grad_gain_one,
        grad_shift_one,
        grad_gain_two,
        grad_shift_two,
    ) = summed
    proj_total = jnp.zeros(length_proj.shape, jnp.float32)
    proj_total = lax.dynamic_update_slice_in_dim(proj_total, long_proj, shard_start, 1)
    proj_total = proj_total.at[:, :short_len].add(short_proj)
    proj_rows = lax.psum_scatter(
        proj_total.astype(jnp.bfloat16), "grp", scatter_dimension=0, tiled=True
    )
    proj_part = lax.psum_scatter(proj_rows, "seq", scatter_dimension=1, tiled=True).astype(
        jnp.float32
    )
    reduced = (
        lax.psum_scatter(grad_query, ("grp", "seq"), scatter_dimension=0, tiled=True),
        lax.psum_scatter(grad_key, ("grp", "seq"), scatter_dimension=0, tiled=True),
        lax.psum_scatter(grad_value, ("grp", "seq"), scatter_dimension=0, tiled=True),
        lax.psum_scatter(grad_out, ("grp", "seq"), scatter_dimension=0, tiled=True),
        lax.psum_scatter(grad_up, ("grp", "seq"), scatter_dimension=0, tiled=True),
        lax.psum_scatter(grad_down, ("grp", "seq"), scatter_dimension=0, tiled=True),
        lax.psum_scatter(grad_gain_one, ("grp", "seq"), scatter_dimension=0, tiled=True),
        lax.psum_scatter(grad_shift_one, ("grp", "seq"), scatter_dimension=0, tiled=True),
        lax.psum_scatter(grad_gain_two, ("grp", "seq"), scatter_dimension=0, tiled=True),
        lax.psum_scatter(grad_shift_two, ("grp", "seq"), scatter_dimension=0, tiled=True),
    )
    reduced = tuple(reduced)
    return (
        (
            long_result.astype(jnp.bfloat16),
            short_result.astype(jnp.bfloat16),
            long_back.astype(jnp.bfloat16),
            short_back.astype(jnp.bfloat16),
        )
        + reduced[:6]
        + (proj_part,)
        + reduced[6:]
    )


MESH_ID = pl.DeviceIdType.MESH
BF = jnp.bfloat16
F32 = jnp.float32
VMEM_BYTES = 65400 * 1024
GELU_A = 0.7978845608028654
GELU_B = 0.044715 * GELU_A
SEQ = 8


def mm(a, b, ca=1, cb=0):
    return lax.dot_general(a, b, (((ca,), (cb,)), ((), ())), preferred_element_type=F32)


def span(start, size, step=None):
    return pl.ds(pl.multiple_of(start, step or size), size)


def here():
    return lax.axis_index("grp"), lax.axis_index("seq")


def greet(peers):
    barrier = pltpu.get_barrier_semaphore()
    for peer in peers:
        pl.semaphore_signal(barrier, inc=1, device_id=peer, device_id_type=MESH_ID)
    pl.semaphore_wait(barrier, len(peers))


def seq_peers():
    g, s = here()
    return [(g, lax.rem(s + k, SEQ)) for k in range(1, SEQ)]


def grp_peers(groups):
    g, s = here()
    return [(lax.rem(g + k, groups), s) for k in range(1, groups)]


class Exchange:
    def __init__(self, part, got_core, got, full, send_sem, recv_sem):
        self.part, self.got_core, self.got, self.full = part, got_core, got, full
        self.send_sem, self.recv_sem = send_sem, recv_sem

    def place(self):
        _, s = here()
        core, chip = lax.rem(s, 2), lax.div(s, 2)
        x, y = 1 - 2 * lax.rem(chip, 2), 2 - 4 * lax.div(chip, 2)
        return core, chip, (chip + x, chip + y, chip + x + y)

    def send(self, n, src, dst, to):
        g, _ = here()
        return pltpu.make_async_remote_copy(
            src_ref=src,
            dst_ref=dst,
            send_sem=self.send_sem.at[n],
            recv_sem=self.recv_sem.at[n],
            device_id=(g, to),
            device_id_type=MESH_ID,
        )

    def halve(self):
        core, chip, _ = self.place()
        return self.send(0, self.part.at[pl.ds(4 * (1 - core), 4)], self.got_core, 2 * chip + 1 - core)

    def across(self):
        core, _, chips = self.place()
        return [
            self.send(1 + k, self.part.at[4 * core + to], self.got.at[k], 2 * to + core) for k, to in enumerate(chips)
        ]

    def spread(self):
        core, chip, chips = self.place()
        own = self.full.at[4 * core + chip]
        return [self.send(4 + k, own, own, 2 * to + core) for k, to in enumerate(chips)]

    def join(self):
        core, chip, _ = self.place()
        own = self.full.at[pl.ds(4 * core, 4)]
        return self.send(7, own, own, 2 * chip + 1 - core)

    def start(self):
        self.halve().start()

    def first(self):
        core, _, _ = self.place()
        self.halve().wait_recv()
        for n in range(4):
            self.part[4 * core + n] = (self.part[4 * core + n].astype(F32) + self.got_core[n].astype(F32)).astype(BF)
        for c in self.across():
            c.start()

    def second(self):
        core, chip, _ = self.place()
        for c in self.across():
            c.wait_recv()
        total = self.part[4 * core + chip].astype(F32)
        for k in range(3):
            total += self.got[k].astype(F32)
        self.full[4 * core + chip] = total.astype(BF)
        for c in self.spread():
            c.start()

    def third(self):
        for c in self.spread():
            c.wait_recv()
        self.join().start()

    def finish(self):
        self.join().wait_recv()

    def close(self):
        for c in [self.halve()] + self.across() + self.spread() + [self.join()]:
            c.wait_send()


def exchange_scratch(rows, width):
    shapes = [(SEQ, rows, width), (4, rows, width), (3, rows, width), (SEQ, rows, width)]
    return [pltpu.VMEM(a, BF) for a in shapes] + [pltpu.SemaphoreType.DMA((8,)) for _ in range(4)]


def halves(block):
    low_lane = lax.broadcasted_iota(jnp.int32, block.shape, 1) < HD
    zero = jnp.zeros_like(block)
    return jnp.concatenate([jnp.where(low_lane, block, zero), jnp.where(low_lane, zero, block)], 0)


def unhalve(block):
    n = block.shape[0] // 2
    low_lane = lax.broadcasted_iota(jnp.int32, (n, block.shape[1]), 1) < HD
    return jnp.where(low_lane, block[:n], block[n:])


def norm_stats(v):
    mean = jnp.mean(v, -1, keepdims=True)
    centred = v - mean
    root = lax.rsqrt(jnp.mean(centred * centred, -1, keepdims=True) + norm_eps)
    return centred * root, root


def norm_back(grad, gain, xhat, root):
    gg = grad * gain
    return (gg - jnp.mean(gg, -1, keepdims=True) - xhat * jnp.mean(gg * xhat, -1, keepdims=True)) * root


def fold_rows(v):
    return jnp.sum(v.reshape(v.shape[0] // 8, 8, v.shape[1]), 0)


def gelu_pair(u):
    u2 = u * u
    s = 0.5 + 0.5 * jnp.tanh(u * (GELU_A + GELU_B * u2))
    a = u * s
    return a, s + a * (1.0 - s) * (2.0 * GELU_A + 6.0 * GELU_B * u2)


def places(groups):
    out = []
    for d in range(groups * SEQ):
        z, y, x, c = d // SEQ, (d // 4) % 2, (d // 2) % 2, d % 2
        out.append((((x * 2 + y) * groups + z, c), ((y * 2 + x) * groups + z, c)))
    return out


class Scatter:
    def __init__(self, src, base, bits, recv0, recv1, recv2, last, send_sem, recv_sem, send_z, recv_z):
        self.src, self.base, self.bits = src, base, bits
        self.recv, self.last = (recv0, recv1, recv2), last
        self.rows, self.lanes = last.shape[1:]
        self.send_sem, self.recv_sem, self.send_z, self.recv_z = send_sem, recv_sem, send_z, recv_z

    def mine(self, n):
        _, s = here()
        return lax.rem(lax.div(s, self.bits[n]), 2)

    def half(self, n, which):
        size = self.recv[n].shape[0]
        if n == 0:
            return self.src, self.base, which * self.lanes
        return self.recv[n - 1], which * size, 0

    def hop(self, n):
        g, s = here()
        mine, bit = self.mine(n), self.bits[n]
        src, row, lane = self.half(n, 1 - mine)
        size = self.recv[n].shape[0]
        return pltpu.make_async_remote_copy(
            src_ref=src.at[span(row, size, self.rows), span(lane, self.lanes, 128)],
            dst_ref=self.recv[n],
            send_sem=self.send_sem.at[n],
            recv_sem=self.recv_sem.at[n],
            device_id=(g, s + bit - 2 * bit * mine),
            device_id_type=MESH_ID,
        )

    def along(self):
        g, s = here()
        groups = self.last.shape[0] + 1
        out = []
        for k in range(1, groups):
            to = lax.rem(g + k, groups)
            out.append(
                pltpu.make_async_remote_copy(
                    src_ref=self.recv[2].at[span(to * self.rows, self.rows)],
                    dst_ref=self.last.at[k - 1],
                    send_sem=self.send_z.at[k - 1],
                    recv_sem=self.recv_z.at[k - 1],
                    device_id=(to, s),
                    device_id_type=MESH_ID,
                )
            )
        return out

    def start(self):
        self.hop(0).start()

    def step(self, n):
        src, row, lane = self.half(n, self.mine(n))
        self.hop(n).wait_recv()
        dst = self.recv[n]
        block = 2 * self.rows

        @pl.loop(0, dst.shape[0] // block)
        def _(i):
            to, at = span(i * block, block), span(row + i * block, block, self.rows)
            dst[to, :] = (dst[to, :].astype(F32) + src[at, span(lane, self.lanes, 128)].astype(F32)).astype(BF)

        if n < 2:
            self.hop(n + 1).start()
        else:
            for c in self.along():
                c.start()

    def total(self, out, row, column):
        for c in self.along():
            c.wait_recv()
        g, _ = here()
        total = self.recv[2][span(g * self.rows, self.rows), :].astype(F32)
        for k in range(self.last.shape[0]):
            total += self.last[k].astype(F32)
        few = self.rows // 2
        out[row : row + few, column : column + self.lanes] = total[:few]
        out[row : row + few, column + self.lanes : column + 2 * self.lanes] = total[few:]

    def close(self):
        for n in range(3):
            self.hop(n).wait_send()
        for c in self.along():
            c.wait_send()


class Place:
    def __init__(self, ref, row):
        self.ref, self.row = ref, row

    def __add__(self, rows):
        return Place(self.ref, self.row + rows)


def window(place, size, step=None):
    row = place.row
    rows = pl.ds(row, size) if isinstance(row, int) else span(row, size, step)
    return place.ref, rows


class Arena:
    def __getitem__(self, key):
        (ref, rows), lanes = key
        return ref[rows, lanes]

    def __setitem__(self, key, value):
        (ref, rows), lanes = key
        ref[rows, lanes] = value


class Vectors:
    def __init__(self, mine, recv, last, send_sem, recv_sem, send_z, recv_z):
        self.mine, self.recv, self.last = mine, recv, last
        self.sems = (send_sem, recv_sem, send_z, recv_z)

    def hop(self, n):
        g, s = here()
        bit = 1 << n
        other = s + bit - 2 * bit * lax.rem(lax.div(s, bit), 2)
        return pltpu.make_async_remote_copy(
            src_ref=self.mine.at[n],
            dst_ref=self.recv.at[n],
            send_sem=self.sems[0].at[n],
            recv_sem=self.sems[1].at[n],
            device_id=(g, other),
            device_id_type=MESH_ID,
        )

    def along(self):
        g, s = here()
        groups = self.last.shape[0] + 1
        return [
            pltpu.make_async_remote_copy(
                src_ref=self.mine.at[3],
                dst_ref=self.last.at[k - 1],
                send_sem=self.sems[2].at[k - 1],
                recv_sem=self.sems[3].at[k - 1],
                device_id=(lax.rem(g + k, groups), s),
                device_id_type=MESH_ID,
            )
            for k in range(1, groups)
        ]

    def start(self):
        self.hop(0).start()

    def step(self, n):
        self.hop(n).wait_recv()
        self.mine[n + 1] = self.mine[n] + self.recv[n]
        if n < 2:
            self.hop(n + 1).start()
        else:
            for c in self.along():
                c.start()

    def total(self):
        for c in self.along():
            c.wait_recv()
        return self.mine[3] + sum(self.last[k] for k in range(self.last.shape[0]))

    def close(self):
        for c in [self.hop(n) for n in range(3)] + self.along():
            c.wait_send()


class ProjGrad:
    def __init__(self, part, got, short, got_short, *sems):
        self.part, self.got, self.short, self.got_short, self.sems = part, got, short, got_short, sems

    def along(self, first, size):
        g, s = here()
        groups = self.part.shape[0]
        send, recv = self.sems[:2] if first == 0 else self.sems[2:4]
        out = []
        for k in range(1, groups):
            to = lax.rem(g + k, groups)
            out.append(
                pltpu.make_async_remote_copy(
                    src_ref=self.part.at[to, :, pl.ds(first, size)],
                    dst_ref=self.got.at[k - 1, :, pl.ds(first, size)],
                    send_sem=send.at[k - 1],
                    recv_sem=recv.at[k - 1],
                    device_id=(to, s),
                    device_id_type=MESH_ID,
                )
            )
        return out

    def across(self, b):
        g, s = here()
        slot = lax.rem(s - b + 2 * SEQ - 1, SEQ)
        return pltpu.make_async_remote_copy(
            src_ref=self.short.at[b],
            dst_ref=self.got_short.at[slot],
            send_sem=self.sems[4].at[b],
            recv_sem=self.sems[5].at[slot],
            device_id=(g, jnp.int32(b)),
            device_id_type=MESH_ID,
        )

    def arrived(self, slot):
        g, s = here()
        return pltpu.make_async_remote_copy(
            src_ref=self.short.at[0],
            dst_ref=self.got_short.at[slot],
            send_sem=self.sems[4].at[0],
            recv_sem=self.sems[5].at[slot],
            device_id=(g, s),
            device_id_type=MESH_ID,
        )

    def start(self, first, size):
        for c in self.along(first, size):
            c.start()

    def summed(self, first, size):
        g, _ = here()
        for c in self.along(first, size):
            c.wait_recv()
        total = self.part[g, :, first : first + size].astype(F32)
        for k in range(self.got.shape[0]):
            total += self.got[k, :, first : first + size].astype(F32)
        return total

    def across_all(self, shard, short_len):
        _, s = here()
        total = self.summed(shard, short_len)
        for b in range(self.short.shape[0]):
            self.short[b] = total[:, b * shard : (b + 1) * shard].astype(BF)

            @pl.when(s != b)
            def _(b=b):
                self.across(b).start()

    def finish(self, out, shard):
        _, s = here()
        count = self.short.shape[0]
        out[...] = self.summed(0, shard)

        @pl.when(s < count)
        def _():
            total = out[...] + self.short[lax.rem(s, count)].astype(F32)
            for slot in range(SEQ - 1):
                self.arrived(slot).wait_recv()
                total += self.got_short[slot].astype(F32)
            out[...] = total

    def close(self):
        _, s = here()
        shard = self.short.shape[2]
        for c in self.along(0, shard) + self.along(shard, self.part.shape[2] - shard):
            c.wait_send()
        for b in range(self.short.shape[0]):

            @pl.when(s != b)
            def _(b=b):
                self.across(b).wait_send()


def layer_kernel(slots, groups, shard, *refs):
    refs = list(refs)

    def take(n):
        out = refs[:n]
        del refs[:n]
        return out

    (long_x, short_x, long_dy, short_dy, live) = take(5)
    (wq_in, wk_in, wv_in, wo_in, up_in, down_in, proj) = take(7)
    (gain1, shift1, gain2, shift2) = (a[...].reshape(1, -1) for a in take(4))
    (long_out, short_out, long_grad, short_grad) = take(4)
    (grad_q, grad_k, grad_v, grad_o, grad_up, grad_down, grad_proj, vec_out) = take(8)
    (q_hbm, y_hbm, mixed_hbm, probs_hbm, sums_hbm) = take(5)
    (a_ref, s_ref, ud_ref, x_ref, m_ref, h_ref, w_ref, p_ref, b_ref, resid, root, vec, pcols, pshort, pacc) = take(15)
    (sem_in, sem_out, sem_back) = take(3)
    exch_bufs = take(4)
    forward_exchange = Exchange(*exch_bufs, *take(2))
    backward_exchange = Exchange(*exch_bufs, *take(2))
    vectors = Vectors(*take(7))
    projected = ProjGrad(*take(10))

    g, s = here()
    short_len = short_x.shape[1]
    width = resid.shape[1]
    wide = 4 * width
    shorts = slots * short_len
    tokens = shorts + shard
    devices = groups * SEQ
    few = width // devices
    lanes = width // 2
    act, slope = Place(a_ref, 0), Place(s_ref, 0)
    up, down = Place(ud_ref, 0), Place(ud_ref, wide)
    xs, ms, hs, xhs = Place(x_ref, 0), Place(m_ref, 0), Place(h_ref, 0), Place(h_ref, tokens)
    wo, pack, weights = Place(w_ref, 0), Place(p_ref, 0), Place(h_ref, 0)
    pack_up = act
    q1, y1 = act, act + tokens
    probs1, sums1 = Place(s_ref, 0), Place(p_ref, 0)
    q2, y2 = slope, slope + tokens
    long_sums2 = y2 + (slots + 1) * KP
    key_grads = long_sums2 + 2 * KP
    probs2, through = Place(ud_ref, 0), Place(ud_ref, 0)
    sums2, gq2 = pack + width, pack_up + 4 * width
    value_grads, ms2, x2s = Place(b_ref, 0), hs, ms

    orders = ((1, 2, 4), (1, 4, 2))

    def unit(base, order):
        return Scatter(base.ref, base.row, orders[order], *take(8))

    downs = [unit(pack + n * width, n % 2) for n in range(4)]
    ups = [unit(pack_up + n * width, n % 2) for n in range(4)]
    unit_o, unit_q, unit_v, unit_k = (unit(pack + n * width, n % 2) for n in range(4))
    assert not refs

    copy = pltpu.make_async_copy
    at = lambda place, size: place.ref.at[pl.ds(place.row, size)]
    arena = Arena()
    counts = {"in": 0, "out": 0, "back": 0}

    def move(kind, a, b):
        sem = {"in": sem_in, "out": sem_out, "back": sem_back}[kind]
        counts[kind] += 1
        return copy(a, b, sem.at[counts[kind] - 1])

    def rows_of(long_a, short_a, base, kind, back=False):
        pairs = [(long_a.at[0], at(base + shorts, shard))]
        pairs += [(short_a.at[i], at(base + i * short_len, short_len)) for i in range(slots)]
        return [move(kind, b, a) if back else move(kind, a, b) for a, b in pairs]

    in_x = rows_of(long_x, short_x, xs, "in")
    in_cols = move("in", proj.at[:, span(s * shard, shard)], pcols)
    in_wk = move("in", wk_in, at(weights + width, width))
    in_wv = move("in", wv_in, at(weights + 2 * width, width))
    in_wq = move("in", wq_in, at(weights, width))
    in_pshort = move("in", proj.at[:, pl.ds(0, short_len)], pshort)
    in_wo = move("in", wo_in, at(wo, width))
    in_up = [move("in", up_in.at[:, pl.ds(j * width, width)], at(up + j * width, width)) for j in range(4)]
    in_down = move("in", down_in, at(down, wide))
    for c in [in_x[0], in_cols] + in_x[1:] + [in_pshort, in_wk, in_wv, in_wq, in_wo] + in_up + [in_down]:
        c.start()
    greet(seq_peers() + grp_peers(groups))

    part, full = forward_exchange.part, forward_exchange.full
    blocks = KP // SEQ
    items = slots * KP
    in_x[0].wait()
    in_cols.wait()
    part[...] = mm(pcols[...], arena[window(xs + shorts, shard), :]).astype(BF).reshape(SEQ, blocks, width)
    forward_exchange.start()
    for c in in_x[1:] + [in_pshort]:
        c.wait()
    for i in range(slots):
        x = arena[window(xs + i * short_len, short_len), :]
        arena[window(y1 + i * KP, KP), :] = mm(pshort[...], x).astype(BF)
    in_wk.wait()

    def summaries(to, y, size):
        for n in range(2):
            w = arena[window(weights + (1 + n) * width, width), :]
            arena[window(to + n * size, size), :] = mm(arena[window(y, size), :], w).astype(BF)

    in_wv.wait()
    summaries(sums1, y1, items)
    forward_exchange.first()
    in_wq.wait()
    arena[window(q1, tokens), :] = (0.125 * mm(arena[window(xs, tokens), :], arena[window(weights, width), :])).astype(BF)
    out_q = move("out", at(q1, tokens), q_hbm)
    out_q.start()
    forward_exchange.second()
    heads = width // HD
    item_rows = heads * short_len // width * KP

    def head(h, size):
        beside = width // size
        return h // beside * KP, slice(h % beside * size, (h % beside + 1) * size)

    def staged(before, between, after):
        now, last = before(0), None
        for pair in range(heads // 2):
            ahead = before(pair + 1) if pair + 1 < heads // 2 else None
            middle = between(pair, *now)
            if last is not None:
                after(pair - 1, last)
            now, last = ahead, middle
        after(heads // 2 - 1, last)

    def lanes_of(pair):
        return slice(pair * 2 * HD, (pair + 1) * 2 * HD)

    def attend(row, size, ks, vs, probs):
        def scores(pair):
            q = arena[window(q1 + row, size, 128), lanes_of(pair)]
            return (mm(halves(arena[window(ks, KP), lanes_of(pair)]), q, 1, 1),)

        def softmax(pair, sc):
            parts = []
            for h in range(2):
                part = sc[h * KP : (h + 1) * KP]
                e = jnp.exp(part - jnp.max(part, 0, keepdims=True))
                parts.append((e * (1.0 / jnp.sum(e, 0, keepdims=True))).astype(BF))
                first, cols = head(2 * pair + h, size)
                arena[window(probs + first, KP, 128), cols] = parts[h]
            return jnp.concatenate(parts, 0)

        def mix(pair, p):
            out = mm(halves(arena[window(vs, KP), lanes_of(pair)]), p, 0, 0)
            arena[window(ms + row, size, 128), lanes_of(pair)] = out.T.astype(BF)

        staged(scores, softmax, mix)

    @pl.loop(0, slots)
    def _(i):
        attend(i * short_len, short_len, sums1 + i * KP, sums1 + (items + i * KP), probs1 + i * item_rows)

        @pl.when(i == 1)
        def _():
            forward_exchange.third()

    long_probs = probs1 + slots * item_rows
    out_probs = [move("out", at(probs1, slots * item_rows), probs_hbm.at[pl.ds(0, slots * item_rows)])]
    out_probs[0].start()
    forward_exchange.finish()
    long_sums = sums1 + 2 * items
    arena[window(y1 + items, KP), :] = full[...].reshape(KP, width)
    summaries(long_sums, y1 + items, KP)
    out_y = move("out", at(y1, items + KP), y_hbm)
    out_y.start()

    def enter(row, size, step):
        r = span(row, size, step)
        x = arena[window(xs + row, size, step), :].astype(F32)
        xh, rs = norm_stats(mm(arena[window(ms + row, size, step), :], arena[window(wo, width), :]) + x)
        arena[window(xhs + row, size, step), :] = xh.astype(BF)
        root[r, :] = jnp.broadcast_to(rs, (size, 128))
        hidden = xh * gain1 + shift1
        resid[r, :] = hidden
        arena[window(hs + row, size, step), :] = hidden.astype(BF)

    in_wo.wait()

    @pl.loop(0, slots // 2)
    def _(i):
        enter(i * 2 * short_len, 2 * short_len, 128)

    attend(shorts, shard, long_sums, long_sums + KP, long_probs)
    long_size = heads * shard // width * KP
    out_probs += [move("out", at(long_probs, long_size), probs_hbm.at[pl.ds(slots * item_rows, long_size)])]
    out_sums = move("out", at(sums1, (2 * slots + 2) * KP), sums_hbm)
    out_mixed = move("out", at(ms, tokens), mixed_hbm)
    for c in out_probs[1:] + [out_sums, out_mixed]:
        c.start()
    enter(shorts, shard, 128)
    block = tokens // 3
    in_dy = rows_of(long_dy, short_dy, xs, "in")
    for c in in_dy:
        c.start()
    for c in [out_y, out_q, out_mixed] + out_probs:
        c.wait()
    for c in in_up + [in_down]:
        c.wait()

    part_rows = tokens // 3

    def rows_in(place, j, r):
        return window(place + (j * tokens + r * part_rows), part_rows, 64)

    @pl.loop(0, 4)
    def _(j):
        def upward(r):
            return mm(arena[rows_in(hs, 0, r), :], arena[window(up + j * width, width, 128), :])

        def activate(r, u):
            a, slope_j = gelu_pair(u)
            a = a.astype(BF)
            arena[rows_in(act, j, r), :] = a
            arena[rows_in(slope, j, r), :] = slope_j.astype(BF)
            return a

        def downward(r, a):
            resid[pl.ds(r * part_rows, part_rows), :] += mm(a, arena[window(down + j * width, width, 128), :])

        u0 = upward(0)
        u1 = upward(1)
        a0 = activate(0, u0)
        u2 = upward(2)
        a1 = activate(1, u1)
        downward(0, a0)
        a2 = activate(2, u2)
        downward(1, a1)
        downward(2, a2)

    vec[...] = jnp.zeros_like(vec)
    for c in in_dy:
        c.wait()
    rb = 128

    @pl.loop(0, tokens // rb)
    def _(i):
        r = span(i * rb, rb)
        rx = window(xs + i * rb, rb, 128)
        alive = jnp.where(lax.div(i * rb, short_len) < live[0], 1.0, 0.0).astype(F32)
        alive = jnp.where(i * rb >= shorts, 1.0, alive)
        xh, rs = norm_stats(resid[r, :])
        top = alive * arena[rx, :].astype(F32)
        vec[16:24, :] += fold_rows(top * xh)
        vec[24:32, :] += fold_rows(top)
        arena[rx, :] = (alive * (xh * gain2 + shift2)).astype(BF)
        dx = norm_back(top, gain2, xh, rs)
        resid[r, :] = dx
        arena[window(ms + i * rb, rb, 128), :] = dx.astype(BF)

    outs = rows_of(long_out, short_out, xs, "out", back=True)
    for c in outs:
        c.start()
    out_sums.wait()
    place = places(groups)

    def packed(base, order, value, step, first):
        for d in range(value.shape[0] // step):
            row, core = place[d][order]
            rows = slice(d * step + first, d * step + first + few)
            arena[window(base + row * 2 * few, 2 * few), core * lanes : (core + 1) * lanes] = jnp.concatenate(
                [value[rows, :lanes], value[rows, lanes:]], 0
            ).astype(BF)

    @pl.loop(0, groups)
    def _(j):
        value = mm(arena[window(act + j * tokens, tokens, 128), :], arena[window(ms, tokens), :], 0, 0)
        for n in range(4):
            packed(pack + n * width + j * 2 * few, n % 2, value, 4 * few, n * few)

    for piece in downs:
        piece.start()
    low = at(ms, tokens)

    @pl.loop(0, 4)
    def _(j):
        def grad_up_of(r):
            gb = low[pl.ds(r * part_rows, part_rows), :]
            gu = mm(gb, arena[window(down + j * width, width, 128), :], 1, 1)
            gu = (gu * arena[rows_in(slope, j, r), :].astype(F32)).astype(BF)
            arena[rows_in(slope, j, r), :] = gu
            return gu

        def into_resid(r, gu):
            resid[pl.ds(r * part_rows, part_rows), :] += mm(gu, arena[window(up + j * width, width, 128), :], 1, 1)

        gu0 = grad_up_of(0)
        gu1 = grad_up_of(1)
        into_resid(0, gu0)
        gu2 = grad_up_of(2)
        into_resid(1, gu1)
        into_resid(2, gu2)

        @pl.when(j == 0)
        def _():
            for piece in downs[:2]:
                piece.step(0)

        @pl.when(j == 1)
        def _():
            for piece in downs[2:]:
                piece.step(0)

    back = {}

    def load(name, a, b):
        back[name] = move("back", a, b)
        back[name].start()

    load("probs", probs_hbm, at(probs2, 4 * tokens))

    for piece in downs:
        piece.step(1)

    @pl.loop(0, 2)
    def _(m):
        for n in range(2):
            j = 2 * m + n
            gu = arena[window(slope + j * tokens, tokens, 128), :]
            packed(pack_up + j * width, n, mm(arena[window(hs, tokens), :], gu, 0, 0), few, 0)

        @pl.when(m == 0)
        def _():
            for piece in ups[:2]:
                piece.start()

        @pl.when(m == 1)
        def _():
            for piece in ups[2:]:
                piece.start()
            for piece in ups[:2]:
                piece.step(0)
            for piece in downs[:2]:
                piece.step(2)

    load("y", y_hbm, at(y2, items + KP))
    load("q", q_hbm, at(q2, tokens))
    load("mixed", mixed_hbm, at(ms2, tokens))
    for piece in downs[1:]:
        piece.hop(0).wait_send()
    load("sums", sums_hbm.at[pl.ds(0, 2 * items)], at(sums2, 2 * items))
    load("long_sums", sums_hbm.at[pl.ds(2 * items, 2 * KP)], at(long_sums2, 2 * KP))

    @pl.loop(0, tokens // rb)
    def _(i):
        r = span(i * rb, rb)
        gh = resid[r, :]
        xh = arena[window(xhs + i * rb, rb, 128), :].astype(F32)
        vec[0:8, :] += fold_rows(gh * xh)
        vec[8:16, :] += fold_rows(gh)
        dx = norm_back(gh, gain1, xh, root[r, 0:1])
        resid[r, :] = dx
        low[r, :] = dx.astype(BF)

    four = jnp.sum(vec[...].reshape(4, 8, width), 1)
    vectors.mine[0] = jnp.concatenate([four, jnp.zeros_like(four)], 0)
    vectors.start()
    for c in outs:
        c.wait()
    arena[window(xs, tokens), :] = mm(low[...], arena[window(wo, width), :], 1, 1).astype(BF)
    for piece in ups[2:]:
        piece.step(0)
    for piece in downs[2:]:
        piece.step(2)
    downs[0].hop(0).wait_send()
    back["mixed"].wait()
    packed(pack, 0, mm(arena[window(ms2, tokens), :], low[...], 0, 0), few, 0)
    unit_o.start()
    load("wq", wq_in, at(weights, width))
    load("wk", wk_in, at(weights + width, width))
    load("wv", wv_in, at(weights + 2 * width, width))
    for n, c in enumerate(rows_of(long_x, short_x, x2s, "back")):
        back["x", n] = c
        c.start()

    def attend_back(row, size, ks, vs, probs, n):
        def front(pair):
            gm = arena[window(xs + row, size, 128), lanes_of(pair)]
            p = []
            for h in range(2):
                first, cols = head(2 * pair + h, size)
                p.append(arena[window(probs + first, KP, 128), cols])
            gp = mm(halves(arena[window(vs, KP), lanes_of(pair)]), gm, 1, 1)
            grad = unhalve(mm(jnp.concatenate(p, 0), gm)).astype(BF)
            arena[window(value_grads + n * KP, KP, 128), lanes_of(pair)] = grad
            return gp, p

        def middle(pair, gp, p):
            parts = []
            for h in range(2):
                ph = p[h].astype(F32)
                t = ph * gp[h * KP : (h + 1) * KP]
                parts.append((t - ph * jnp.sum(t, 0, keepdims=True)).astype(BF))
            return jnp.concatenate(parts, 0)

        def rear(pair, gs):
            q = arena[window(q2 + row, size, 128), lanes_of(pair)]
            arena[window(key_grads + n * KP, KP, 128), lanes_of(pair)] = unhalve(mm(gs, q)).astype(BF)
            gq = mm(halves(arena[window(ks, KP), lanes_of(pair)]), gs, 0, 0).T.astype(BF).astype(F32)
            arena[window(gq2 + row, size, 128), lanes_of(pair)] = (gq * 0.125).astype(BF)

        staged(front, middle, rear)

    def through_projections(first, count):
        rows = count * KP
        key_grad = mm(arena[window(key_grads + first * KP, rows), :], arena[window(weights + width, width), :], 1, 1)
        return key_grad + mm(arena[window(value_grads + first * KP, rows), :], arena[window(weights + 2 * width, width), :], 1, 1)

    for name in ("q", "y", "sums", "long_sums", "probs"):
        back[name].wait()
    forward_exchange.close()
    attend_back(shorts, shard, long_sums2, long_sums2 + KP, probs2 + slots * item_rows, slots)
    unit_o.step(0)
    for name in ("wq", "wk", "wv"):
        back[name].wait()
    part[...] = through_projections(slots, 1).astype(BF).reshape(SEQ, blocks, width)
    backward_exchange.start()

    @pl.loop(0, slots)
    def _(i):
        attend_back(i * short_len, short_len, sums2 + i * KP, sums2 + (items + i * KP), probs2 + i * item_rows, i)

        @pl.when(i == 0)
        def _():
            backward_exchange.first()
            for piece in ups[:2]:
                piece.step(1)

        @pl.when(i == 1)
        def _():
            vectors.step(0)
            for piece in ups[2:]:
                piece.step(1)

        @pl.when(i == slots - 1)
        def _():
            backward_exchange.second()
            for piece in ups[:2]:
                piece.step(2)

    for n in range(1 + slots):
        back["x", n].wait()
    x2, gq = at(x2s, tokens), at(gq2, tokens)

    packed(pack + width, 1, mm(x2[...], gq[...], 0, 0), few, 0)
    unit_q.start()
    unit_o.step(1)
    y = arena[window(y2, items + KP), :]
    packed(pack + 2 * width, 0, mm(y, arena[window(value_grads, items + KP), :], 0, 0), few, 0)
    unit_v.start()
    vectors.step(1)
    unit_q.step(0)
    packed(pack + 3 * width, 1, mm(y, arena[window(key_grads, items + KP), :], 0, 0), few, 0)
    unit_k.start()
    unit_v.step(0)
    backward_exchange.third()
    for piece in ups[2:]:
        piece.step(2)

    arena[window(through, items), :] = through_projections(0, slots).astype(BF)
    unit_k.step(0)
    unit_o.step(2)
    pacc[...] = jnp.zeros_like(pacc)

    def leave(cols, row, size, n):
        grad = arena[window(through + n * KP, KP), :]
        r = span(row, size, 128)
        dx = resid[r, :] + mm(gq[r, :], arena[window(weights, width), :], 1, 1) + mm(cols[...], grad, 0, 0)
        arena[window(xs + row, size, 128), :] = dx.astype(BF)
        return mm(grad, x2[r, :], 1, 1)

    @pl.loop(0, slots)
    def _(i):
        pacc[...] += leave(pshort, i * short_len, short_len, i)

    prow = KP // groups
    projected.part[:, :, shard:] = pacc[...].astype(BF).reshape(groups, prow, short_len)
    projected.start(shard, short_len)
    backward_exchange.finish()
    arena[window(through + items, KP), :] = full[...].reshape(KP, width)
    long_cols = leave(pcols, shorts, shard, slots)
    projected.part[:, :, 0:shard] = long_cols.astype(BF).reshape(groups, prow, shard)
    projected.start(0, shard)
    unit_q.step(1)
    vectors.step(2)
    outs = rows_of(long_grad, short_grad, xs, "out", back=True)
    for c in outs:
        c.start()
    unit_v.step(1)
    projected.across_all(shard, short_len)
    for n, piece in enumerate(downs):
        piece.total(grad_down, n * few, 0)
    for n, piece in enumerate(ups):
        piece.total(grad_up, 0, n * width)
    unit_o.total(grad_o, 0, 0)
    unit_k.step(1)
    unit_q.step(2)
    vec_out[...] = vectors.total()
    unit_v.step(2)
    projected.finish(grad_proj, shard)
    unit_k.step(2)
    unit_q.total(grad_q, 0, 0)
    unit_v.total(grad_v, 0, 0)
    unit_k.total(grad_k, 0, 0)
    for c in outs:
        c.wait()
    for piece in downs:
        for n in range(1, 3):
            piece.hop(n).wait_send()
        for c in piece.along():
            c.wait_send()
    for piece in ups + [unit_o, unit_q, unit_v, unit_k, vectors, projected, backward_exchange]:
        piece.close()


def fast_shards(groups, *args):
    (long_x, short_x, long_dy, short_dy, live, wq, wk, wv, wo, up, down, proj, g1, b1, g2, b2) = args
    slots, short_len, width = short_x.shape
    shard = long_x.shape[1]
    tokens = slots * short_len + shard
    wide = up.shape[1]
    devices = groups * SEQ
    few = width // devices
    sds = jax.ShapeDtypeStruct
    anyspace = pl.BlockSpec(memory_space=pl.ANY)
    vmem = pl.BlockSpec(memory_space=pltpu.VMEM)
    dma = pltpu.SemaphoreType.DMA
    prow = KP // groups
    out_shapes = [sds(a.shape, BF) for a in (long_x, short_x, long_x, short_x)]
    grads = [(few, width)] * 4 + [(few, wide), (4 * few, width), (prow, shard), (8, width)]
    out_shapes += [sds(a, F32) for a in grads]
    row = (tokens, width)
    out_shapes += [
        sds(a, BF)
        for a in [row, ((slots + 1) * KP, width), row, (4 * tokens, width), ((2 * slots + 2) * KP, width)]
    ]
    regions = [4 * tokens, 4 * tokens, 2 * wide, tokens, tokens, 2 * tokens, width, 4 * width, (slots + 1) * KP]
    heads = short_len // shard
    scratch = [
        *[pltpu.VMEM((n, width), BF) for n in regions],
        pltpu.VMEM(row, F32),
        pltpu.VMEM((tokens, 128), F32),
        pltpu.VMEM((32, width), F32),
        pltpu.VMEM((KP, shard), BF),
        pltpu.VMEM((KP, short_len), BF),
        pltpu.VMEM((KP, short_len), F32),
        dma((12 + 2 * (1 + slots),)),
        dma((13 + 2 * (1 + slots),)),
        dma((13 + 1 + slots,)),
    ]
    scratch += exchange_scratch(KP // SEQ, width)
    along = [dma((groups - 1,)), dma((groups - 1,))]
    scratch += [pltpu.VMEM((n, 8, width), F32) for n in (4, 3, groups - 1)] + [dma((3,)), dma((3,))] + along
    scratch += [pltpu.VMEM((n, prow, shard + short_len), BF) for n in (groups, groups - 1)]
    scratch += [pltpu.VMEM((n, prow, shard), BF) for n in (heads, SEQ - 1)]
    scratch += along + along + [dma((heads,)), dma((SEQ - 1,))]
    lanes = width // 2
    unit = [pltpu.VMEM((width // n, lanes), BF) for n in (1, 2, 4)]
    unit += [pltpu.VMEM((groups - 1, 2 * few, lanes), BF), dma((3,)), dma((3,))] + along
    scratch += unit * 12
    outs = pl.pallas_call(
        functools.partial(layer_kernel, slots, groups, shard),
        name="encoder_layer",
        out_shape=out_shapes,
        in_specs=[anyspace] * 4 + [pl.BlockSpec(memory_space=pltpu.SMEM)] + [anyspace] * 7 + [vmem] * 4,
        out_specs=[anyspace] * 4 + [vmem] * 8 + [anyspace] * 5,
        scratch_shapes=scratch,
        compiler_params=pltpu.CompilerParams(
            collective_id=0, has_side_effects=True, vmem_limit_bytes=VMEM_BYTES
        ),
    )(long_x, short_x, long_dy, short_dy, live, wq, wk, wv, wo, up, down, proj, g1, b1, g2, b2)
    return emit_call(outs[:12], few)


def emit_kernel(*refs):
    *ins, vec = refs[:12]
    outs, vectors, stages = refs[12:23], refs[23:27], refs[27:38]
    sem_in, sem_out = refs[38:]
    reads = [pltpu.make_async_copy(a, b, sem_in.at[n]) for n, (a, b) in enumerate(zip(ins, stages))]
    writes = [pltpu.make_async_copy(a, b, sem_out.at[n]) for n, (a, b) in enumerate(zip(stages, outs))]
    for c in reads:
        c.start()
    g, s = here()
    width = vec.shape[1]
    few = vectors[0].shape[0]
    mine = pltpu.roll(vec[...], width - (g * SEQ + s) * few, 1)
    for n in range(4):
        vectors[n][...] = mine[n, 0:few]
    for a, b in zip(reads, writes):
        a.wait()
        b.start()
    for c in writes:
        c.wait()


def emit_call(arrays, few):
    anyspace = pl.BlockSpec(memory_space=pl.ANY)
    vmem = pl.BlockSpec(memory_space=pltpu.VMEM)
    return pl.pallas_call(
        emit_kernel,
        name="emit",
        out_shape=[jax.ShapeDtypeStruct(a.shape, a.dtype) for a in arrays[:11]] + [jax.ShapeDtypeStruct((few,), F32)] * 4,
        in_specs=[anyspace] * 11 + [vmem],
        out_specs=[anyspace] * 11 + [vmem] * 4,
        scratch_shapes=[pltpu.VMEM(a.shape, a.dtype) for a in arrays[:11]] + [pltpu.SemaphoreType.DMA((11,))] * 2,
        compiler_params=pltpu.CompilerParams(vmem_limit_bytes=VMEM_BYTES),
    )(*arrays)


def fits(mesh, args):
    long_x, width, wide = args[0], args[0].shape[2], args[9].shape[1]
    devices = mesh.shape["grp"] * mesh.shape["seq"]
    whole = width % (devices * 8) == 0 and wide == 4 * width
    return mesh.shape["seq"] == SEQ and whole and long_x.shape[0] == 1


def solution(mesh):
    placed = (
        P("grp", "seq", None),
        P(("grp", "seq"), None, None),
        P("grp", "seq", None),
        P(("grp", "seq"), None, None),
        P(("grp", "seq")),
        P(),
        P(),
        P(),
        P(),
        P(),
        P(),
        P(),
        P(),
        P(),
        P(),
        P(),
    )
    groups = mesh.shape["grp"]

    def body(*args):
        if fits(mesh, args):
            return fast_shards(groups, *args)
        return shards(*args)

    return jax.shard_map(
        body,
        mesh=mesh,
        in_specs=placed,
        out_specs=(
            P("grp", "seq", None),
            P(("grp", "seq"), None, None),
            P("grp", "seq", None),
            P(("grp", "seq"), None, None),
            P(("grp", "seq"), None),
            P(("grp", "seq"), None),
            P(("grp", "seq"), None),
            P(("grp", "seq"), None),
            P(("grp", "seq"), None),
            P(("grp", "seq"), None),
            P("grp", "seq"),
            P(("grp", "seq")),
            P(("grp", "seq")),
            P(("grp", "seq")),
            P(("grp", "seq")),
        ),
        check_vma=False,
    )
```

```python
import functools

import jax
import jax.numpy as jnp
from jax import lax
from jax.experimental import pallas as pl
from jax.experimental.pallas import tpu as pltpu
from jax.sharding import PartitionSpec as P

HD = 64
KP = 256


norm_eps = 1e-05


def shortened(shard):
    return jax.tree.map(lambda a: a.astype(jnp.bfloat16) if a.dtype == jnp.float32 else a, shard)


def norm_rows(resid, gain_vec, shift_vec):
    row_mean = jnp.mean(resid, axis=-1, keepdims=True)
    centred = resid - row_mean
    variance = jnp.mean(centred * centred, axis=-1, keepdims=True)
    return centred * lax.rsqrt(variance + norm_eps) * gain_vec + shift_vec


def smooth_gate(upward):
    return jax.nn.gelu(upward, approximate=True)


def same_sums(partials):
    return partials


def layer_pass(sequences, cotangent, live_rows, proj_cols, fold_summaries, fold_grads, params):
    (
        query_w,
        key_w,
        value_w,
        out_w,
        up_w,
        down_w,
        gain_first,
        shift_first,
        gain_second,
        shift_second,
    ) = params
    seq_count, length, model_width = sequences.shape
    head_count = model_width // HD
    wide = jnp.float32
    narrow = jnp.bfloat16
    queries = (
        0.125 * jnp.einsum("nld,de->nle", sequences, query_w, preferred_element_type=wide)
    ).astype(narrow)
    key_vecs = jnp.einsum("nld,de->nle", sequences, key_w, preferred_element_type=wide).astype(
        narrow
    )
    value_vecs = jnp.einsum("nld,de->nle", sequences, value_w, preferred_element_type=wide).astype(
        narrow
    )
    key_part = jnp.einsum("kl,nld->nkd", proj_cols, key_vecs, preferred_element_type=wide)
    value_part = jnp.einsum("kl,nld->nkd", proj_cols, value_vecs, preferred_element_type=wide)
    key_sum, value_sum = fold_summaries((key_part, value_part))
    key_heads = key_sum.astype(narrow).reshape(seq_count, KP, head_count, HD)
    value_heads = value_sum.astype(narrow).reshape(seq_count, KP, head_count, HD)
    query_heads = queries.reshape(seq_count, length, head_count, HD)
    scores = jnp.einsum("nlhe,nkhe->nhlk", query_heads, key_heads, preferred_element_type=wide)
    attn_probs = jax.nn.softmax(scores, axis=-1)
    probs_low = attn_probs.astype(narrow)
    mixed_heads = (
        jnp.einsum("nhlk,nkhe->nlhe", probs_low, value_heads, preferred_element_type=wide)
        .reshape(seq_count, length, model_width)
        .astype(narrow)
    )
    attn_out = jnp.einsum("nld,de->nle", mixed_heads, out_w, preferred_element_type=wide)
    hidden, first_back = jax.vjp(
        norm_rows, sequences.astype(wide) + attn_out, gain_first, shift_first
    )
    hidden_low = hidden.astype(narrow)
    upward = jnp.einsum("nld,df->nlf", hidden_low, up_w, preferred_element_type=wide)
    activated, gate_back = jax.vjp(smooth_gate, upward)
    activated_low = activated.astype(narrow)
    branch = jnp.einsum("nlf,fd->nld", activated_low, down_w, preferred_element_type=wide)
    normed, second_back = jax.vjp(norm_rows, hidden + branch, gain_second, shift_second)
    result = normed * live_rows[:, None, None]
    grad_top = cotangent.astype(wide) * live_rows[:, None, None]
    grad_resid_two, grad_gain_two, grad_shift_two = second_back(grad_top)
    grad_branch = grad_resid_two.astype(narrow)
    grad_down = jnp.einsum("nlf,nld->fd", activated_low, grad_branch, preferred_element_type=wide)
    grad_activated = jnp.einsum("nld,fd->nlf", grad_branch, down_w, preferred_element_type=wide)
    (grad_upward,) = gate_back(grad_activated)
    grad_upward_low = grad_upward.astype(narrow)
    grad_up = jnp.einsum("nld,nlf->df", hidden_low, grad_upward_low, preferred_element_type=wide)
    grad_hidden = grad_resid_two + jnp.einsum(
        "nlf,df->nld", grad_upward_low, up_w, preferred_element_type=wide
    )
    grad_resid_one, grad_gain_one, grad_shift_one = first_back(grad_hidden)
    grad_attn = grad_resid_one.astype(narrow)
    grad_out = jnp.einsum("nld,nle->de", mixed_heads, grad_attn, preferred_element_type=wide)
    grad_mixed = (
        jnp.einsum("nle,de->nld", grad_attn, out_w, preferred_element_type=wide)
        .astype(narrow)
        .reshape(seq_count, length, head_count, HD)
    )
    grad_probs = jnp.einsum("nlhe,nkhe->nhlk", grad_mixed, value_heads, preferred_element_type=wide)
    value_grad_part = jnp.einsum(
        "nhlk,nlhe->nkhe", probs_low, grad_mixed, preferred_element_type=wide
    ).reshape(seq_count, KP, model_width)
    grad_scores = attn_probs * (
        grad_probs - jnp.sum(grad_probs * attn_probs, axis=-1, keepdims=True)
    )
    scores_low = grad_scores.astype(narrow)
    grad_queries = (
        jnp.einsum("nhlk,nkhe->nlhe", scores_low, key_heads, preferred_element_type=wide).astype(
            narrow
        )
        * 0.125
    ).reshape(seq_count, length, model_width)
    key_grad_part = jnp.einsum(
        "nhlk,nlhe->nkhe", scores_low, query_heads, preferred_element_type=wide
    ).reshape(seq_count, KP, model_width)
    key_grad_sum, value_grad_sum = fold_grads((key_grad_part, value_grad_part))
    key_grad_low = key_grad_sum.astype(narrow)
    value_grad_low = value_grad_sum.astype(narrow)
    grad_keys = jnp.einsum(
        "kl,nkd->nld", proj_cols, key_grad_low, preferred_element_type=wide
    ).astype(narrow)
    grad_values = jnp.einsum(
        "kl,nkd->nld", proj_cols, value_grad_low, preferred_element_type=wide
    ).astype(narrow)
    grad_cols = jnp.einsum(
        "nkd,nld->kl", key_grad_low, key_vecs, preferred_element_type=wide
    ) + jnp.einsum("nkd,nld->kl", value_grad_low, value_vecs, preferred_element_type=wide)
    grad_query = jnp.einsum("nld,nle->de", sequences, grad_queries, preferred_element_type=wide)
    grad_key = jnp.einsum("nld,nle->de", sequences, grad_keys, preferred_element_type=wide)
    grad_value = jnp.einsum("nld,nle->de", sequences, grad_values, preferred_element_type=wide)
    grad_sequences = grad_resid_one + jnp.einsum(
        "nle,de->nld", grad_queries, query_w, preferred_element_type=wide
    )
    grad_sequences = grad_sequences + jnp.einsum(
        "nle,de->nld", grad_keys, key_w, preferred_element_type=wide
    )
    grad_sequences = grad_sequences + jnp.einsum(
        "nle,de->nld", grad_values, value_w, preferred_element_type=wide
    )
    weight_grads = (
        grad_query,
        grad_key,
        grad_value,
        grad_out,
        grad_up,
        grad_down,
        grad_gain_one,
        grad_shift_one,
        grad_gain_two,
        grad_shift_two,
    )
    return (result, grad_sequences, weight_grads, grad_cols)


def shards(
    long_x,
    short_x,
    long_dy,
    short_dy,
    short_live,
    query_weight,
    key_weight,
    value_weight,
    out_weight,
    up_weight,
    down_weight,
    length_proj,
    gain_one,
    shift_one,
    gain_two,
    shift_two,
):
    params = (
        query_weight,
        key_weight,
        value_weight,
        out_weight,
        up_weight,
        down_weight,
        gain_one,
        shift_one,
        gain_two,
        shift_two,
    )
    shard_len = long_x.shape[1]
    slot_count = short_x.shape[0]
    short_len = short_x.shape[1]
    shard_start = lax.axis_index("seq") * shard_len
    long_cols = lax.dynamic_slice_in_dim(length_proj, shard_start, shard_len, 1)

    def sum_summaries(partials):
        return jax.tree.map(
            lambda part: part.astype(jnp.float32), lax.psum(shortened(partials), "seq")
        )

    def sum_summary_grads(partials):
        return jax.tree.map(
            lambda part: part.astype(jnp.float32), lax.psum(shortened(partials), "seq")
        )

    long_live = jnp.ones((long_x.shape[0],), jnp.float32)
    long_result, long_back, long_weights, long_proj = layer_pass(
        long_x, long_dy, long_live, long_cols, sum_summaries, sum_summary_grads, params
    )
    short_mask = (jnp.arange(slot_count) < short_live[0]).astype(jnp.float32)
    short_result, short_back, short_weights, short_proj = layer_pass(
        short_x, short_dy, short_mask, length_proj[:, :short_len], same_sums, same_sums, params
    )
    summed = jax.tree.map(jnp.add, long_weights, short_weights)
    (
        grad_query,
        grad_key,
        grad_value,
        grad_out,
        grad_up,
        grad_down,
        grad_gain_one,
        grad_shift_one,
        grad_gain_two,
        grad_shift_two,
    ) = summed
    proj_total = jnp.zeros(length_proj.shape, jnp.float32)
    proj_total = lax.dynamic_update_slice_in_dim(proj_total, long_proj, shard_start, 1)
    proj_total = proj_total.at[:, :short_len].add(short_proj)
    proj_rows = lax.psum_scatter(
        proj_total.astype(jnp.bfloat16), "grp", scatter_dimension=0, tiled=True
    )
    proj_part = lax.psum_scatter(proj_rows, "seq", scatter_dimension=1, tiled=True).astype(
        jnp.float32
    )
    reduced = (
        lax.psum_scatter(grad_query, ("grp", "seq"), scatter_dimension=0, tiled=True),
        lax.psum_scatter(grad_key, ("grp", "seq"), scatter_dimension=0, tiled=True),
        lax.psum_scatter(grad_value, ("grp", "seq"), scatter_dimension=0, tiled=True),
        lax.psum_scatter(grad_out, ("grp", "seq"), scatter_dimension=0, tiled=True),
        lax.psum_scatter(grad_up, ("grp", "seq"), scatter_dimension=0, tiled=True),
        lax.psum_scatter(grad_down, ("grp", "seq"), scatter_dimension=0, tiled=True),
        lax.psum_scatter(grad_gain_one, ("grp", "seq"), scatter_dimension=0, tiled=True),
        lax.psum_scatter(grad_shift_one, ("grp", "seq"), scatter_dimension=0, tiled=True),
        lax.psum_scatter(grad_gain_two, ("grp", "seq"), scatter_dimension=0, tiled=True),
        lax.psum_scatter(grad_shift_two, ("grp", "seq"), scatter_dimension=0, tiled=True),
    )
    reduced = tuple(reduced)
    return (
        (
            long_result.astype(jnp.bfloat16),
            short_result.astype(jnp.bfloat16),
            long_back.astype(jnp.bfloat16),
            short_back.astype(jnp.bfloat16),
        )
        + reduced[:6]
        + (proj_part,)
        + reduced[6:]
    )


MESH_ID = pl.DeviceIdType.MESH
BF = jnp.bfloat16
F32 = jnp.float32
VMEM_BYTES = 65400 * 1024
GELU_A = 0.7978845608028654
GELU_B = 0.044715 * GELU_A
SEQ = 8


def mm(a, b, ca=1, cb=0):
    return lax.dot_general(a, b, (((ca,), (cb,)), ((), ())), preferred_element_type=F32)


def span(start, size, step=None):
    return pl.ds(pl.multiple_of(start, step or size), size)


def here():
    return lax.axis_index("grp"), lax.axis_index("seq")


def greet(peers):
    barrier = pltpu.get_barrier_semaphore()
    for peer in peers:
        pl.semaphore_signal(barrier, inc=1, device_id=peer, device_id_type=MESH_ID)
    pl.semaphore_wait(barrier, len(peers))


def seq_peers():
    g, s = here()
    return [(g, lax.rem(s + k, SEQ)) for k in range(1, SEQ)]


def grp_peers(groups):
    g, s = here()
    return [(lax.rem(g + k, groups), s) for k in range(1, groups)]


class Exchange:
    def __init__(self, part, got_core, got, full, send_sem, recv_sem):
        self.part, self.got_core, self.got, self.full = part, got_core, got, full
        self.send_sem, self.recv_sem = send_sem, recv_sem

    def place(self):
        _, s = here()
        core, chip = lax.rem(s, 2), lax.div(s, 2)
        x, y = 1 - 2 * lax.rem(chip, 2), 2 - 4 * lax.div(chip, 2)
        return core, chip, (chip + x, chip + y, chip + x + y)

    def send(self, n, src, dst, to):
        g, _ = here()
        return pltpu.make_async_remote_copy(
            src_ref=src,
            dst_ref=dst,
            send_sem=self.send_sem.at[n],
            recv_sem=self.recv_sem.at[n],
            device_id=(g, to),
            device_id_type=MESH_ID,
        )

    def halve(self):
        core, chip, _ = self.place()
        return self.send(0, self.part.at[pl.ds(4 * (1 - core), 4)], self.got_core, 2 * chip + 1 - core)

    def across(self):
        core, _, chips = self.place()
        return [
            self.send(1 + k, self.part.at[4 * core + to], self.got.at[k], 2 * to + core) for k, to in enumerate(chips)
        ]

    def spread(self):
        core, chip, chips = self.place()
        own = self.full.at[4 * core + chip]
        return [self.send(4 + k, own, own, 2 * to + core) for k, to in enumerate(chips)]

    def join(self):
        core, chip, _ = self.place()
        own = self.full.at[pl.ds(4 * core, 4)]
        return self.send(7, own, own, 2 * chip + 1 - core)

    def start(self):
        self.halve().start()

    def first(self):
        core, _, _ = self.place()
        self.halve().wait_recv()
        for n in range(4):
            self.part[4 * core + n] = (self.part[4 * core + n].astype(F32) + self.got_core[n].astype(F32)).astype(BF)
        for c in self.across():
            c.start()

    def second(self):
        core, chip, _ = self.place()
        for c in self.across():
            c.wait_recv()
        total = self.part[4 * core + chip].astype(F32)
        for k in range(3):
            total += self.got[k].astype(F32)
        self.full[4 * core + chip] = total.astype(BF)
        for c in self.spread():
            c.start()

    def third(self):
        for c in self.spread():
            c.wait_recv()
        self.join().start()

    def finish(self):
        self.join().wait_recv()

    def close(self):
        for c in [self.halve()] + self.across() + self.spread() + [self.join()]:
            c.wait_send()


def exchange_scratch(rows, width):
    shapes = [(SEQ, rows, width), (4, rows, width), (3, rows, width), (SEQ, rows, width)]
    return [pltpu.VMEM(a, BF) for a in shapes] + [pltpu.SemaphoreType.DMA((8,)) for _ in range(4)]


def halves(block):
    low_lane = lax.broadcasted_iota(jnp.int32, block.shape, 1) < HD
    zero = jnp.zeros_like(block)
    return jnp.concatenate([jnp.where(low_lane, block, zero), jnp.where(low_lane, zero, block)], 0)


def unhalve(block):
    n = block.shape[0] // 2
    low_lane = lax.broadcasted_iota(jnp.int32, (n, block.shape[1]), 1) < HD
    return jnp.where(low_lane, block[:n], block[n:])


def norm_stats(v):
    mean = jnp.mean(v, -1, keepdims=True)
    centred = v - mean
    root = lax.rsqrt(jnp.mean(centred * centred, -1, keepdims=True) + norm_eps)
    return centred * root, root


def norm_back(grad, gain, xhat, root):
    gg = grad * gain
    return (gg - jnp.mean(gg, -1, keepdims=True) - xhat * jnp.mean(gg * xhat, -1, keepdims=True)) * root


def fold_rows(v):
    return jnp.sum(v.reshape(v.shape[0] // 8, 8, v.shape[1]), 0)


def gelu_pair(u):
    u2 = u * u
    s = 0.5 + 0.5 * jnp.tanh(u * (GELU_A + GELU_B * u2))
    a = u * s
    return a, s + a * (1.0 - s) * (2.0 * GELU_A + 6.0 * GELU_B * u2)


def places(groups):
    out = []
    for d in range(groups * SEQ):
        z, y, x, c = d // SEQ, (d // 4) % 2, (d // 2) % 2, d % 2
        out.append((((x * 2 + y) * groups + z, c), ((y * 2 + x) * groups + z, c)))
    return out


class Scatter:
    def __init__(self, src, base, bits, recv0, recv1, recv2, last, send_sem, recv_sem, send_z, recv_z):
        self.src, self.base, self.bits = src, base, bits
        self.recv, self.last = (recv0, recv1, recv2), last
        self.rows, self.lanes = last.shape[1:]
        self.send_sem, self.recv_sem, self.send_z, self.recv_z = send_sem, recv_sem, send_z, recv_z

    def mine(self, n):
        _, s = here()
        return lax.rem(lax.div(s, self.bits[n]), 2)

    def half(self, n, which):
        size = self.recv[n].shape[0]
        if n == 0:
            return self.src, self.base, which * self.lanes
        return self.recv[n - 1], which * size, 0

    def hop(self, n):
        g, s = here()
        mine, bit = self.mine(n), self.bits[n]
        src, row, lane = self.half(n, 1 - mine)
        size = self.recv[n].shape[0]
        return pltpu.make_async_remote_copy(
            src_ref=src.at[span(row, size, self.rows), span(lane, self.lanes, 128)],
            dst_ref=self.recv[n],
            send_sem=self.send_sem.at[n],
            recv_sem=self.recv_sem.at[n],
            device_id=(g, s + bit - 2 * bit * mine),
            device_id_type=MESH_ID,
        )

    def along(self):
        g, s = here()
        groups = self.last.shape[0] + 1
        out = []
        for k in range(1, groups):
            to = lax.rem(g + k, groups)
            out.append(
                pltpu.make_async_remote_copy(
                    src_ref=self.recv[2].at[span(to * self.rows, self.rows)],
                    dst_ref=self.last.at[k - 1],
                    send_sem=self.send_z.at[k - 1],
                    recv_sem=self.recv_z.at[k - 1],
                    device_id=(to, s),
                    device_id_type=MESH_ID,
                )
            )
        return out

    def start(self):
        self.hop(0).start()

    def step(self, n):
        src, row, lane = self.half(n, self.mine(n))
        self.hop(n).wait_recv()
        dst = self.recv[n]
        block = 2 * self.rows

        @pl.loop(0, dst.shape[0] // block)
        def _(i):
            to, at = span(i * block, block), span(row + i * block, block, self.rows)
            dst[to, :] = (dst[to, :].astype(F32) + src[at, span(lane, self.lanes, 128)].astype(F32)).astype(BF)

        if n < 2:
            self.hop(n + 1).start()
        else:
            for c in self.along():
                c.start()

    def total(self, out, row, column):
        for c in self.along():
            c.wait_recv()
        g, _ = here()
        total = self.recv[2][span(g * self.rows, self.rows), :].astype(F32)
        for k in range(self.last.shape[0]):
            total += self.last[k].astype(F32)
        few = self.rows // 2
        out[row : row + few, column : column + self.lanes] = total[:few]
        out[row : row + few, column + self.lanes : column + 2 * self.lanes] = total[few:]

    def close(self):
        for n in range(3):
            self.hop(n).wait_send()
        for c in self.along():
            c.wait_send()


class Place:
    def __init__(self, ref, row):
        self.ref, self.row = ref, row

    def __add__(self, rows):
        return Place(self.ref, self.row + rows)


def window(place, size, step=None):
    row = place.row
    rows = pl.ds(row, size) if isinstance(row, int) else span(row, size, step)
    return place.ref, rows


class Arena:
    def __getitem__(self, key):
        (ref, rows), lanes = key
        return ref[rows, lanes]

    def __setitem__(self, key, value):
        (ref, rows), lanes = key
        ref[rows, lanes] = value


class Vectors:
    def __init__(self, mine, recv, last, send_sem, recv_sem, send_z, recv_z):
        self.mine, self.recv, self.last = mine, recv, last
        self.sems = (send_sem, recv_sem, send_z, recv_z)

    def hop(self, n):
        g, s = here()
        bit = 1 << n
        other = s + bit - 2 * bit * lax.rem(lax.div(s, bit), 2)
        return pltpu.make_async_remote_copy(
            src_ref=self.mine.at[n],
            dst_ref=self.recv.at[n],
            send_sem=self.sems[0].at[n],
            recv_sem=self.sems[1].at[n],
            device_id=(g, other),
            device_id_type=MESH_ID,
        )

    def along(self):
        g, s = here()
        groups = self.last.shape[0] + 1
        return [
            pltpu.make_async_remote_copy(
                src_ref=self.mine.at[3],
                dst_ref=self.last.at[k - 1],
                send_sem=self.sems[2].at[k - 1],
                recv_sem=self.sems[3].at[k - 1],
                device_id=(lax.rem(g + k, groups), s),
                device_id_type=MESH_ID,
            )
            for k in range(1, groups)
        ]

    def start(self):
        self.hop(0).start()

    def step(self, n):
        self.hop(n).wait_recv()
        self.mine[n + 1] = self.mine[n] + self.recv[n]
        if n < 2:
            self.hop(n + 1).start()
        else:
            for c in self.along():
                c.start()

    def total(self):
        for c in self.along():
            c.wait_recv()
        return self.mine[3] + sum(self.last[k] for k in range(self.last.shape[0]))

    def close(self):
        for c in [self.hop(n) for n in range(3)] + self.along():
            c.wait_send()


class ProjGrad:
    def __init__(self, part, got, short, got_short, *sems):
        self.part, self.got, self.short, self.got_short, self.sems = part, got, short, got_short, sems

    def along(self, first, size):
        g, s = here()
        groups = self.part.shape[0]
        send, recv = self.sems[:2] if first == 0 else self.sems[2:4]
        out = []
        for k in range(1, groups):
            to = lax.rem(g + k, groups)
            out.append(
                pltpu.make_async_remote_copy(
                    src_ref=self.part.at[to, :, pl.ds(first, size)],
                    dst_ref=self.got.at[k - 1, :, pl.ds(first, size)],
                    send_sem=send.at[k - 1],
                    recv_sem=recv.at[k - 1],
                    device_id=(to, s),
                    device_id_type=MESH_ID,
                )
            )
        return out

    def across(self, b):
        g, s = here()
        slot = lax.rem(s - b + 2 * SEQ - 1, SEQ)
        return pltpu.make_async_remote_copy(
            src_ref=self.short.at[b],
            dst_ref=self.got_short.at[slot],
            send_sem=self.sems[4].at[b],
            recv_sem=self.sems[5].at[slot],
            device_id=(g, jnp.int32(b)),
            device_id_type=MESH_ID,
        )

    def arrived(self, slot):
        g, s = here()
        return pltpu.make_async_remote_copy(
            src_ref=self.short.at[0],
            dst_ref=self.got_short.at[slot],
            send_sem=self.sems[4].at[0],
            recv_sem=self.sems[5].at[slot],
            device_id=(g, s),
            device_id_type=MESH_ID,
        )

    def start(self, first, size):
        for c in self.along(first, size):
            c.start()

    def summed(self, first, size):
        g, _ = here()
        for c in self.along(first, size):
            c.wait_recv()
        total = self.part[g, :, first : first + size].astype(F32)
        for k in range(self.got.shape[0]):
            total += self.got[k, :, first : first + size].astype(F32)
        return total

    def across_all(self, shard, short_len):
        _, s = here()
        total = self.summed(shard, short_len)
        for b in range(self.short.shape[0]):
            self.short[b] = total[:, b * shard : (b + 1) * shard].astype(BF)

            @pl.when(s != b)
            def _(b=b):
                self.across(b).start()

    def finish(self, out, shard):
        _, s = here()
        count = self.short.shape[0]
        out[...] = self.summed(0, shard)

        @pl.when(s < count)
        def _():
            total = out[...] + self.short[lax.rem(s, count)].astype(F32)
            for slot in range(SEQ - 1):
                self.arrived(slot).wait_recv()
                total += self.got_short[slot].astype(F32)
            out[...] = total

    def close(self):
        _, s = here()
        shard = self.short.shape[2]
        for c in self.along(0, shard) + self.along(shard, self.part.shape[2] - shard):
            c.wait_send()
        for b in range(self.short.shape[0]):

            @pl.when(s != b)
            def _(b=b):
                self.across(b).wait_send()


def layer_kernel(slots, groups, shard, *refs):
    refs = list(refs)

    def take(n):
        out = refs[:n]
        del refs[:n]
        return out

    (long_x, short_x, long_dy, short_dy, live) = take(5)
    (wq_in, wk_in, wv_in, wo_in, up_in, down_in, proj) = take(7)
    (gain1, shift1, gain2, shift2) = (a[...].reshape(1, -1) for a in take(4))
    (long_out, short_out, long_grad, short_grad) = take(4)
    (grad_q, grad_k, grad_v, grad_o, grad_up, grad_down, grad_proj, vec_out) = take(8)
    (q_hbm, y_hbm, mixed_hbm, probs_hbm, sums_hbm) = take(5)
    (a_ref, s_ref, ud_ref, x_ref, m_ref, h_ref, w_ref, p_ref, b_ref, resid, root, vec, pcols, pshort, pacc) = take(15)
    (sem_in, sem_out, sem_back) = take(3)
    exch_bufs = take(4)
    forward_exchange = Exchange(*exch_bufs, *take(2))
    backward_exchange = Exchange(*exch_bufs, *take(2))
    vectors = Vectors(*take(7))
    projected = ProjGrad(*take(10))

    g, s = here()
    short_len = short_x.shape[1]
    width = resid.shape[1]
    wide = 4 * width
    shorts = slots * short_len
    tokens = shorts + shard
    devices = groups * SEQ
    few = width // devices
    lanes = width // 2
    act, slope = Place(a_ref, 0), Place(s_ref, 0)
    up, down = Place(ud_ref, 0), Place(ud_ref, wide)
    xs, ms, hs, xhs = Place(x_ref, 0), Place(m_ref, 0), Place(h_ref, 0), Place(h_ref, tokens)
    wo, pack, weights = Place(w_ref, 0), Place(p_ref, 0), Place(h_ref, 0)
    pack_up = act
    q1, y1 = act, act + tokens
    probs1, sums1 = Place(s_ref, 0), Place(p_ref, 0)
    q2, y2 = slope, slope + tokens
    long_sums2 = y2 + (slots + 1) * KP
    key_grads = long_sums2 + 2 * KP
    probs2, through = Place(ud_ref, 0), Place(ud_ref, 0)
    sums2, gq2 = pack + width, pack_up + 4 * width
    value_grads, ms2, x2s = Place(b_ref, 0), hs, ms

    orders = ((1, 2, 4), (1, 4, 2))

    def unit(base, order):
        return Scatter(base.ref, base.row, orders[order], *take(8))

    downs = [unit(pack + n * width, n % 2) for n in range(4)]
    ups = [unit(pack_up + n * width, n % 2) for n in range(4)]
    unit_o, unit_q, unit_v, unit_k = (unit(pack + n * width, n % 2) for n in range(4))
    assert not refs

    copy = pltpu.make_async_copy
    at = lambda place, size: place.ref.at[pl.ds(place.row, size)]
    arena = Arena()
    counts = {"in": 0, "out": 0, "back": 0}

    def move(kind, a, b):
        sem = {"in": sem_in, "out": sem_out, "back": sem_back}[kind]
        counts[kind] += 1
        return copy(a, b, sem.at[counts[kind] - 1])

    def rows_of(long_a, short_a, base, kind, back=False):
        pairs = [(long_a.at[0], at(base + shorts, shard))]
        pairs += [(short_a.at[i], at(base + i * short_len, short_len)) for i in range(slots)]
        return [move(kind, b, a) if back else move(kind, a, b) for a, b in pairs]

    in_x = rows_of(long_x, short_x, xs, "in")
    in_cols = move("in", proj.at[:, span(s * shard, shard)], pcols)
    in_wk = move("in", wk_in, at(weights + width, width))
    in_wv = move("in", wv_in, at(weights + 2 * width, width))
    in_wq = move("in", wq_in, at(weights, width))
    in_pshort = move("in", proj.at[:, pl.ds(0, short_len)], pshort)
    in_wo = move("in", wo_in, at(wo, width))
    in_up = [move("in", up_in.at[:, pl.ds(j * width, width)], at(up + j * width, width)) for j in range(4)]
    in_down = move("in", down_in, at(down, wide))
    for c in [in_x[0], in_cols] + in_x[1:] + [in_pshort, in_wk, in_wv, in_wq, in_wo] + in_up + [in_down]:
        c.start()
    greet(seq_peers() + grp_peers(groups))

    part, full = forward_exchange.part, forward_exchange.full
    blocks = KP // SEQ
    items = slots * KP
    in_x[0].wait()
    in_cols.wait()
    part[...] = mm(pcols[...], arena[window(xs + shorts, shard), :]).astype(BF).reshape(SEQ, blocks, width)
    forward_exchange.start()
    for c in in_x[1:] + [in_pshort]:
        c.wait()
    for i in range(slots):
        x = arena[window(xs + i * short_len, short_len), :]
        arena[window(y1 + i * KP, KP), :] = mm(pshort[...], x).astype(BF)
    in_wk.wait()

    def summaries(to, y, size):
        for n in range(2):
            w = arena[window(weights + (1 + n) * width, width), :]
            arena[window(to + n * size, size), :] = mm(arena[window(y, size), :], w).astype(BF)

    in_wv.wait()
    summaries(sums1, y1, items)
    forward_exchange.first()
    in_wq.wait()
    arena[window(q1, tokens), :] = (0.125 * mm(arena[window(xs, tokens), :], arena[window(weights, width), :])).astype(BF)
    out_q = move("out", at(q1, tokens), q_hbm)
    out_q.start()
    forward_exchange.second()
    heads = width // HD
    item_rows = heads * short_len // width * KP

    def head(h, size):
        beside = width // size
        return h // beside * KP, slice(h % beside * size, (h % beside + 1) * size)

    def staged(before, between, after):
        now, last = before(0), None
        for pair in range(heads // 2):
            ahead = before(pair + 1) if pair + 1 < heads // 2 else None
            middle = between(pair, *now)
            if last is not None:
                after(pair - 1, last)
            now, last = ahead, middle
        after(heads // 2 - 1, last)

    def lanes_of(pair):
        return slice(pair * 2 * HD, (pair + 1) * 2 * HD)

    def attend(row, size, ks, vs, probs):
        def scores(pair):
            q = arena[window(q1 + row, size, 128), lanes_of(pair)]
            return (mm(halves(arena[window(ks, KP), lanes_of(pair)]), q, 1, 1),)

        def softmax(pair, sc):
            parts = []
            for h in range(2):
                part = sc[h * KP : (h + 1) * KP]
                e = jnp.exp(part - jnp.max(part, 0, keepdims=True))
                parts.append((e * (1.0 / jnp.sum(e, 0, keepdims=True))).astype(BF))
                first, cols = head(2 * pair + h, size)
                arena[window(probs + first, KP, 128), cols] = parts[h]
            return jnp.concatenate(parts, 0)

        def mix(pair, p):
            out = mm(halves(arena[window(vs, KP), lanes_of(pair)]), p, 0, 0)
            arena[window(ms + row, size, 128), lanes_of(pair)] = out.T.astype(BF)

        staged(scores, softmax, mix)

    @pl.loop(0, slots)
    def _(i):
        attend(i * short_len, short_len, sums1 + i * KP, sums1 + (items + i * KP), probs1 + i * item_rows)

        @pl.when(i == 1)
        def _():
            forward_exchange.third()

    long_probs = probs1 + slots * item_rows
    out_probs = [move("out", at(probs1, slots * item_rows), probs_hbm.at[pl.ds(0, slots * item_rows)])]
    out_probs[0].start()
    forward_exchange.finish()
    long_sums = sums1 + 2 * items
    arena[window(y1 + items, KP), :] = full[...].reshape(KP, width)
    summaries(long_sums, y1 + items, KP)
    out_y = move("out", at(y1, items + KP), y_hbm)
    out_y.start()

    def enter(row, size, step):
        r = span(row, size, step)
        x = arena[window(xs + row, size, step), :].astype(F32)
        xh, rs = norm_stats(mm(arena[window(ms + row, size, step), :], arena[window(wo, width), :]) + x)
        arena[window(xhs + row, size, step), :] = xh.astype(BF)
        root[r, :] = jnp.broadcast_to(rs, (size, 128))
        hidden = xh * gain1 + shift1
        resid[r, :] = hidden
        arena[window(hs + row, size, step), :] = hidden.astype(BF)

    in_wo.wait()

    @pl.loop(0, slots // 2)
    def _(i):
        enter(i * 2 * short_len, 2 * short_len, 128)

    attend(shorts, shard, long_sums, long_sums + KP, long_probs)
    long_size = heads * shard // width * KP
    out_probs += [move("out", at(long_probs, long_size), probs_hbm.at[pl.ds(slots * item_rows, long_size)])]
    out_sums = move("out", at(sums1, (2 * slots + 2) * KP), sums_hbm)
    out_mixed = move("out", at(ms, tokens), mixed_hbm)
    for c in out_probs[1:] + [out_sums, out_mixed]:
        c.start()
    enter(shorts, shard, 128)
    block = tokens // 3
    in_dy = rows_of(long_dy, short_dy, xs, "in")
    for c in in_dy:
        c.start()
    for c in [out_y, out_q, out_mixed] + out_probs:
        c.wait()
    for c in in_up + [in_down]:
        c.wait()

    part_rows = tokens // 3

    def rows_in(place, j, r):
        return window(place + (j * tokens + r * part_rows), part_rows, 64)

    @pl.loop(0, 4)
    def _(j):
        def upward(r):
            return mm(arena[rows_in(hs, 0, r), :], arena[window(up + j * width, width, 128), :])

        def activate(r, u):
            a, slope_j = gelu_pair(u)
            a = a.astype(BF)
            arena[rows_in(act, j, r), :] = a
            arena[rows_in(slope, j, r), :] = slope_j.astype(BF)
            return a

        def downward(r, a):
            resid[pl.ds(r * part_rows, part_rows), :] += mm(a, arena[window(down + j * width, width, 128), :])

        u0 = upward(0)
        u1 = upward(1)
        a0 = activate(0, u0)
        u2 = upward(2)
        a1 = activate(1, u1)
        downward(0, a0)
        a2 = activate(2, u2)
        downward(1, a1)
        downward(2, a2)

    vec[...] = jnp.zeros_like(vec)
    for c in in_dy:
        c.wait()
    rb = 128

    @pl.loop(0, tokens // rb)
    def _(i):
        r = span(i * rb, rb)
        rx = window(xs + i * rb, rb, 128)
        alive = jnp.where(lax.div(i * rb, short_len) < live[0], 1.0, 0.0).astype(F32)
        alive = jnp.where(i * rb >= shorts, 1.0, alive)
        xh, rs = norm_stats(resid[r, :])
        top = alive * arena[rx, :].astype(F32)
        vec[16:24, :] += fold_rows(top * xh)
        vec[24:32, :] += fold_rows(top)
        arena[rx, :] = (alive * (xh * gain2 + shift2)).astype(BF)
        dx = norm_back(top, gain2, xh, rs)
        resid[r, :] = dx
        arena[window(ms + i * rb, rb, 128), :] = dx.astype(BF)

    outs = rows_of(long_out, short_out, xs, "out", back=True)
    for c in outs:
        c.start()
    out_sums.wait()
    place = places(groups)

    def packed(base, order, value, step, first):
        for d in range(value.shape[0] // step):
            row, core = place[d][order]
            rows = slice(d * step + first, d * step + first + few)
            arena[window(base + row * 2 * few, 2 * few), core * lanes : (core + 1) * lanes] = jnp.concatenate(
                [value[rows, :lanes], value[rows, lanes:]], 0
            ).astype(BF)

    @pl.loop(0, groups)
    def _(j):
        value = mm(arena[window(act + j * tokens, tokens, 128), :], arena[window(ms, tokens), :], 0, 0)
        for n in range(4):
            packed(pack + n * width + j * 2 * few, n % 2, value, 4 * few, n * few)

    for piece in downs:
        piece.start()
    low = at(ms, tokens)

    @pl.loop(0, 4)
    def _(j):
        def grad_up_of(r):
            gb = low[pl.ds(r * part_rows, part_rows), :]
            gu = mm(gb, arena[window(down + j * width, width, 128), :], 1, 1)
            gu = (gu * arena[rows_in(slope, j, r), :].astype(F32)).astype(BF)
            arena[rows_in(slope, j, r), :] = gu
            return gu

        def into_resid(r, gu):
            resid[pl.ds(r * part_rows, part_rows), :] += mm(gu, arena[window(up + j * width, width, 128), :], 1, 1)

        gu0 = grad_up_of(0)
        gu1 = grad_up_of(1)
        into_resid(0, gu0)
        gu2 = grad_up_of(2)
        into_resid(1, gu1)
        into_resid(2, gu2)

        @pl.when(j == 0)
        def _():
            for piece in downs[:2]:
                piece.step(0)

        @pl.when(j == 1)
        def _():
            for piece in downs[2:]:
                piece.step(0)

    back = {}

    def load(name, a, b):
        back[name] = move("back", a, b)
        back[name].start()

    load("probs", probs_hbm, at(probs2, 4 * tokens))

    for piece in downs[:2]:
        piece.step(1)

    @pl.loop(0, 2)
    def _(m):
        for n in range(2):
            j = 2 * m + n
            gu = arena[window(slope + j * tokens, tokens, 128), :]
            packed(pack_up + j * width, n, mm(arena[window(hs, tokens), :], gu, 0, 0), few, 0)

        @pl.when(m == 0)
        def _():
            for piece in ups[:2]:
                piece.start()
            for piece in downs[2:]:
                piece.step(1)

        @pl.when(m == 1)
        def _():
            for piece in ups[2:]:
                piece.start()
            for piece in ups[:2]:
                piece.step(0)

    load("y", y_hbm, at(y2, items + KP))
    load("q", q_hbm, at(q2, tokens))
    load("mixed", mixed_hbm, at(ms2, tokens))
    for piece in downs[1:]:
        piece.hop(0).wait_send()
    load("sums", sums_hbm.at[pl.ds(0, 2 * items)], at(sums2, 2 * items))
    load("long_sums", sums_hbm.at[pl.ds(2 * items, 2 * KP)], at(long_sums2, 2 * KP))

    @pl.loop(0, tokens // rb)
    def _(i):
        r = span(i * rb, rb)
        gh = resid[r, :]
        xh = arena[window(xhs + i * rb, rb, 128), :].astype(F32)
        vec[0:8, :] += fold_rows(gh * xh)
        vec[8:16, :] += fold_rows(gh)
        dx = norm_back(gh, gain1, xh, root[r, 0:1])
        resid[r, :] = dx
        low[r, :] = dx.astype(BF)

    for piece in downs[:2]:
        piece.step(2)
    four = jnp.sum(vec[...].reshape(4, 8, width), 1)
    vectors.mine[0] = jnp.concatenate([four, jnp.zeros_like(four)], 0)
    vectors.start()
    for c in outs:
        c.wait()
    arena[window(xs, tokens), :] = mm(low[...], arena[window(wo, width), :], 1, 1).astype(BF)
    for piece in ups[2:]:
        piece.step(0)
    for piece in downs[2:]:
        piece.step(2)
    downs[0].hop(0).wait_send()
    back["mixed"].wait()
    packed(pack, 0, mm(arena[window(ms2, tokens), :], low[...], 0, 0), few, 0)
    unit_o.start()
    load("wq", wq_in, at(weights, width))
    load("wk", wk_in, at(weights + width, width))
    load("wv", wv_in, at(weights + 2 * width, width))
    for n, c in enumerate(rows_of(long_x, short_x, x2s, "back")):
        back["x", n] = c
        c.start()

    def attend_back(row, size, ks, vs, probs, n):
        def front(pair):
            gm = arena[window(xs + row, size, 128), lanes_of(pair)]
            p = []
            for h in range(2):
                first, cols = head(2 * pair + h, size)
                p.append(arena[window(probs + first, KP, 128), cols])
            gp = mm(halves(arena[window(vs, KP), lanes_of(pair)]), gm, 1, 1)
            grad = unhalve(mm(jnp.concatenate(p, 0), gm)).astype(BF)
            arena[window(value_grads + n * KP, KP, 128), lanes_of(pair)] = grad
            return gp, p

        def middle(pair, gp, p):
            parts = []
            for h in range(2):
                ph = p[h].astype(F32)
                t = ph * gp[h * KP : (h + 1) * KP]
                parts.append((t - ph * jnp.sum(t, 0, keepdims=True)).astype(BF))
            return jnp.concatenate(parts, 0)

        def rear(pair, gs):
            q = arena[window(q2 + row, size, 128), lanes_of(pair)]
            arena[window(key_grads + n * KP, KP, 128), lanes_of(pair)] = unhalve(mm(gs, q)).astype(BF)
            gq = mm(halves(arena[window(ks, KP), lanes_of(pair)]), gs, 0, 0).T.astype(BF).astype(F32)
            arena[window(gq2 + row, size, 128), lanes_of(pair)] = (gq * 0.125).astype(BF)

        staged(front, middle, rear)

    def through_projections(first, count):
        rows = count * KP
        key_grad = mm(arena[window(key_grads + first * KP, rows), :], arena[window(weights + width, width), :], 1, 1)
        return key_grad + mm(arena[window(value_grads + first * KP, rows), :], arena[window(weights + 2 * width, width), :], 1, 1)

    for name in ("q", "y", "sums", "long_sums", "probs"):
        back[name].wait()
    forward_exchange.close()
    attend_back(shorts, shard, long_sums2, long_sums2 + KP, probs2 + slots * item_rows, slots)
    unit_o.step(0)
    for name in ("wq", "wk", "wv"):
        back[name].wait()
    part[...] = through_projections(slots, 1).astype(BF).reshape(SEQ, blocks, width)
    backward_exchange.start()

    @pl.loop(0, slots)
    def _(i):
        attend_back(i * short_len, short_len, sums2 + i * KP, sums2 + (items + i * KP), probs2 + i * item_rows, i)

        @pl.when(i == 0)
        def _():
            backward_exchange.first()
            for piece in ups[:2]:
                piece.step(1)

        @pl.when(i == 1)
        def _():
            vectors.step(0)
            for piece in ups[2:]:
                piece.step(1)

        @pl.when(i == slots - 1)
        def _():
            backward_exchange.second()
            for piece in ups[:2]:
                piece.step(2)

    for n in range(1 + slots):
        back["x", n].wait()
    x2, gq = at(x2s, tokens), at(gq2, tokens)

    packed(pack + width, 1, mm(x2[...], gq[...], 0, 0), few, 0)
    unit_q.start()
    unit_o.step(1)
    y = arena[window(y2, items + KP), :]
    packed(pack + 2 * width, 0, mm(y, arena[window(value_grads, items + KP), :], 0, 0), few, 0)
    unit_v.start()
    vectors.step(1)
    unit_q.step(0)
    packed(pack + 3 * width, 1, mm(y, arena[window(key_grads, items + KP), :], 0, 0), few, 0)
    unit_k.start()
    unit_v.step(0)
    backward_exchange.third()
    for piece in ups[2:]:
        piece.step(2)

    arena[window(through, items), :] = through_projections(0, slots).astype(BF)
    unit_k.step(0)
    unit_o.step(2)
    pacc[...] = jnp.zeros_like(pacc)

    def leave(cols, row, size, n):
        grad = arena[window(through + n * KP, KP), :]
        r = span(row, size, 128)
        dx = resid[r, :] + mm(gq[r, :], arena[window(weights, width), :], 1, 1) + mm(cols[...], grad, 0, 0)
        arena[window(xs + row, size, 128), :] = dx.astype(BF)
        return mm(grad, x2[r, :], 1, 1)

    @pl.loop(0, slots)
    def _(i):
        pacc[...] += leave(pshort, i * short_len, short_len, i)

    prow = KP // groups
    projected.part[:, :, shard:] = pacc[...].astype(BF).reshape(groups, prow, short_len)
    projected.start(shard, short_len)
    backward_exchange.finish()
    arena[window(through + items, KP), :] = full[...].reshape(KP, width)
    long_cols = leave(pcols, shorts, shard, slots)
    projected.part[:, :, 0:shard] = long_cols.astype(BF).reshape(groups, prow, shard)
    projected.start(0, shard)
    unit_q.step(1)
    vectors.step(2)
    outs = rows_of(long_grad, short_grad, xs, "out", back=True)
    for c in outs:
        c.start()
    unit_v.step(1)
    projected.across_all(shard, short_len)
    for n, piece in enumerate(downs):
        piece.total(grad_down, n * few, 0)
    for n, piece in enumerate(ups):
        piece.total(grad_up, 0, n * width)
    unit_o.total(grad_o, 0, 0)
    unit_k.step(1)
    unit_q.step(2)
    vec_out[...] = vectors.total()
    unit_v.step(2)
    projected.finish(grad_proj, shard)
    unit_k.step(2)
    unit_q.total(grad_q, 0, 0)
    unit_v.total(grad_v, 0, 0)
    unit_k.total(grad_k, 0, 0)
    for c in outs:
        c.wait()
    for piece in downs:
        for n in range(1, 3):
            piece.hop(n).wait_send()
        for c in piece.along():
            c.wait_send()
    for piece in ups + [unit_o, unit_q, unit_v, unit_k, vectors, projected, backward_exchange]:
        piece.close()


def fast_shards(groups, *args):
    (long_x, short_x, long_dy, short_dy, live, wq, wk, wv, wo, up, down, proj, g1, b1, g2, b2) = args
    slots, short_len, width = short_x.shape
    shard = long_x.shape[1]
    tokens = slots * short_len + shard
    wide = up.shape[1]
    devices = groups * SEQ
    few = width // devices
    sds = jax.ShapeDtypeStruct
    anyspace = pl.BlockSpec(memory_space=pl.ANY)
    vmem = pl.BlockSpec(memory_space=pltpu.VMEM)
    dma = pltpu.SemaphoreType.DMA
    prow = KP // groups
    out_shapes = [sds(a.shape, BF) for a in (long_x, short_x, long_x, short_x)]
    grads = [(few, width)] * 4 + [(few, wide), (4 * few, width), (prow, shard), (8, width)]
    out_shapes += [sds(a, F32) for a in grads]
    row = (tokens, width)
    out_shapes += [
        sds(a, BF)
        for a in [row, ((slots + 1) * KP, width), row, (4 * tokens, width), ((2 * slots + 2) * KP, width)]
    ]
    regions = [4 * tokens, 4 * tokens, 2 * wide, tokens, tokens, 2 * tokens, width, 4 * width, (slots + 1) * KP]
    heads = short_len // shard
    scratch = [
        *[pltpu.VMEM((n, width), BF) for n in regions],
        pltpu.VMEM(row, F32),
        pltpu.VMEM((tokens, 128), F32),
        pltpu.VMEM((32, width), F32),
        pltpu.VMEM((KP, shard), BF),
        pltpu.VMEM((KP, short_len), BF),
        pltpu.VMEM((KP, short_len), F32),
        dma((12 + 2 * (1 + slots),)),
        dma((13 + 2 * (1 + slots),)),
        dma((13 + 1 + slots,)),
    ]
    scratch += exchange_scratch(KP // SEQ, width)
    along = [dma((groups - 1,)), dma((groups - 1,))]
    scratch += [pltpu.VMEM((n, 8, width), F32) for n in (4, 3, groups - 1)] + [dma((3,)), dma((3,))] + along
    scratch += [pltpu.VMEM((n, prow, shard + short_len), BF) for n in (groups, groups - 1)]
    scratch += [pltpu.VMEM((n, prow, shard), BF) for n in (heads, SEQ - 1)]
    scratch += along + along + [dma((heads,)), dma((SEQ - 1,))]
    lanes = width // 2
    unit = [pltpu.VMEM((width // n, lanes), BF) for n in (1, 2, 4)]
    unit += [pltpu.VMEM((groups - 1, 2 * few, lanes), BF), dma((3,)), dma((3,))] + along
    scratch += unit * 12
    outs = pl.pallas_call(
        functools.partial(layer_kernel, slots, groups, shard),
        name="encoder_layer",
        out_shape=out_shapes,
        in_specs=[anyspace] * 4 + [pl.BlockSpec(memory_space=pltpu.SMEM)] + [anyspace] * 7 + [vmem] * 4,
        out_specs=[anyspace] * 4 + [vmem] * 8 + [anyspace] * 5,
        scratch_shapes=scratch,
        compiler_params=pltpu.CompilerParams(
            collective_id=0, has_side_effects=True, vmem_limit_bytes=VMEM_BYTES
        ),
    )(long_x, short_x, long_dy, short_dy, live, wq, wk, wv, wo, up, down, proj, g1, b1, g2, b2)
    return emit_call(outs[:12], few)


def emit_kernel(*refs):
    *ins, vec = refs[:12]
    outs, vectors, stages = refs[12:23], refs[23:27], refs[27:38]
    sem_in, sem_out = refs[38:]
    reads = [pltpu.make_async_copy(a, b, sem_in.at[n]) for n, (a, b) in enumerate(zip(ins, stages))]
    writes = [pltpu.make_async_copy(a, b, sem_out.at[n]) for n, (a, b) in enumerate(zip(stages, outs))]
    for c in reads:
        c.start()
    g, s = here()
    width = vec.shape[1]
    few = vectors[0].shape[0]
    mine = pltpu.roll(vec[...], width - (g * SEQ + s) * few, 1)
    for n in range(4):
        vectors[n][...] = mine[n, 0:few]
    for a, b in zip(reads, writes):
        a.wait()
        b.start()
    for c in writes:
        c.wait()


def emit_call(arrays, few):
    anyspace = pl.BlockSpec(memory_space=pl.ANY)
    vmem = pl.BlockSpec(memory_space=pltpu.VMEM)
    return pl.pallas_call(
        emit_kernel,
        name="emit",
        out_shape=[jax.ShapeDtypeStruct(a.shape, a.dtype) for a in arrays[:11]] + [jax.ShapeDtypeStruct((few,), F32)] * 4,
        in_specs=[anyspace] * 11 + [vmem],
        out_specs=[anyspace] * 11 + [vmem] * 4,
        scratch_shapes=[pltpu.VMEM(a.shape, a.dtype) for a in arrays[:11]] + [pltpu.SemaphoreType.DMA((11,))] * 2,
        compiler_params=pltpu.CompilerParams(vmem_limit_bytes=VMEM_BYTES),
    )(*arrays)


def fits(mesh, args):
    long_x, width, wide = args[0], args[0].shape[2], args[9].shape[1]
    devices = mesh.shape["grp"] * mesh.shape["seq"]
    whole = width % (devices * 8) == 0 and wide == 4 * width
    return mesh.shape["seq"] == SEQ and whole and long_x.shape[0] == 1


def solution(mesh):
    placed = (
        P("grp", "seq", None),
        P(("grp", "seq"), None, None),
        P("grp", "seq", None),
        P(("grp", "seq"), None, None),
        P(("grp", "seq")),
        P(),
        P(),
        P(),
        P(),
        P(),
        P(),
        P(),
        P(),
        P(),
        P(),
        P(),
    )
    groups = mesh.shape["grp"]

    def body(*args):
        if fits(mesh, args):
            return fast_shards(groups, *args)
        return shards(*args)

    return jax.shard_map(
        body,
        mesh=mesh,
        in_specs=placed,
        out_specs=(
            P("grp", "seq", None),
            P(("grp", "seq"), None, None),
            P("grp", "seq", None),
            P(("grp", "seq"), None, None),
            P(("grp", "seq"), None),
            P(("grp", "seq"), None),
            P(("grp", "seq"), None),
            P(("grp", "seq"), None),
            P(("grp", "seq"), None),
            P(("grp", "seq"), None),
            P("grp", "seq"),
            P(("grp", "seq")),
            P(("grp", "seq")),
            P(("grp", "seq")),
            P(("grp", "seq")),
        ),
        check_vma=False,
    )
```
